128 devices in a mesh: dp: 8 (over z, core), fsdp: 16 (over y, x).
Axes of the slice: x: 4, y: 4, z: 4, core: 2. Of those that a mesh axis runs over, the one named last changes fastest.
Arguments:
- patches: bfloat16 [65536, 768], P(('dp', 'fsdp')), may hold values from -6 to 6
- lengths: int32 [256, 4], P(('dp', 'fsdp')), may hold values from 1 to 128, 256 in all within a row
- skipped: int32 [65536, 1], P(('dp', 'fsdp')), may hold values 0 or 1
- strip_order: int32 [8, 16], P('dp'), may hold values from 0 to 15, each once within a row
- decoder_grad: bfloat16 [541696, 512], P(('dp', 'fsdp')), may hold values from -6 to 6
- qkv_weight: bfloat16 [768, 2304], P(('dp', 'fsdp')), may hold values from -0.21875 to 0.21875
- out_weight: bfloat16 [768, 768], P(('dp', 'fsdp')), may hold values from -0.625 to 0.625
- up_weight: bfloat16 [768, 3072], P(('dp', 'fsdp')), may hold values from -0.21875 to 0.21875
- down_weight: bfloat16 [3072, 768], P(('dp', 'fsdp')), may hold values from -0.109375 to 0.109375
- embed_weight: bfloat16 [768, 512], P(('dp', 'fsdp')), may hold values from -0.21875 to 0.21875
- gain_one: bfloat16 [768], P(('dp', 'fsdp')), may hold values from 0.5 to 1.5
- shift_one: bfloat16 [768], P(('dp', 'fsdp')), may hold values from -1.5 to 1.5
- gain_two: bfloat16 [768], P(('dp', 'fsdp')), may hold values from 0.5 to 1.5
- shift_two: bfloat16 [768], P(('dp', 'fsdp')), may hold values from -1.5 to 1.5
- bias_query: bfloat16 [768], P(('dp', 'fsdp')), may hold values from -1.5 to 1.5
- bias_value: bfloat16 [768], P(('dp', 'fsdp')), may hold values from -1.5 to 1.5
- bias_out: bfloat16 [768], P(('dp', 'fsdp')), may hold values from -1.5 to 1.5
- bias_up: bfloat16 [3072], P(('dp', 'fsdp')), may hold values from -1.5 to 1.5
- bias_down: bfloat16 [768], P(('dp', 'fsdp')), may hold values from -1.5 to 1.5
- bias_embed: bfloat16 [512], P(('dp', 'fsdp')), may hold values from -1.5 to 1.5
- mask_token: bfloat16 [512], P(('dp', 'fsdp')), may hold values from -4 to 4
Outputs:
- decoder_in: bfloat16 [541696, 512], P(('dp', 'fsdp'))
- patch_grad: float32 [65536, 768], P(('dp', 'fsdp'))
- grad_qkv: float32 [768, 2304], P(('dp', 'fsdp'))
- grad_out: float32 [768, 768], P(('dp', 'fsdp'))
- grad_up: float32 [768, 3072], P(('dp', 'fsdp'))
- grad_down: float32 [3072, 768], P(('dp', 'fsdp'))
- grad_embed: float32 [768, 512], P(('dp', 'fsdp'))
- grad_gain_one: float32 [768], P(('dp', 'fsdp'))
- grad_shift_one: float32 [768], P(('dp', 'fsdp'))
- grad_gain_two: float32 [768], P(('dp', 'fsdp'))
- grad_shift_two: float32 [768], P(('dp', 'fsdp'))
- grad_bias_query: float32 [768], P(('dp', 'fsdp'))
- grad_bias_value: float32 [768], P(('dp', 'fsdp'))
- grad_bias_out: float32 [768], P(('dp', 'fsdp'))
- grad_bias_up: float32 [3072], P(('dp', 'fsdp'))
- grad_bias_down: float32 [768], P(('dp', 'fsdp'))
- grad_bias_embed: float32 [512], P(('dp', 'fsdp'))
- grad_mask_token: float32 [512], P(('dp', 'fsdp'))
The draws below stay inside these ranges and needn't reach their ends.
Inputs may be any that keep to these rules, and one draw needn't show every extreme that they name: `lengths`: each row sums to 256; the longest strip of every row has exactly 128 rows. `strip_order`: each row is a permutation of 0 to 15.
All inputs are finite; a program needn't handle non-finite values. No bound on the sum of `skipped` on one device may be relied on, other than what follows from the above.
Results may differ from the reference program's by a relative error of at most 0.015.
Values may be sent and summed in bfloat16 or wider, within the bound.
A program may use at most 192 MiB of HBM per device.

```python
import math
import jax
import jax.numpy as jnp
import numpy as np
from jax import lax

D = 768
HEADS = 12
HEAD_DIM = 64
FF = 3072
DE = 512
MB = 2
NSEG = 4
STRIP_POS = 529
MB_ROWS = 256
SEG_MOST = 128
STRIPS = 8
TOKENS = 65536
BLOCKS = 256
OUT_ROWS = 541696
N_DP = 8
N_FSDP = 16


def plant(values, rng, least, largest):
    longest = values.shape.index(max(values.shape))
    spots = []
    for shift in (0, 1):
        where = [jax.random.randint(jax.random.fold_in(rng, axis), (), 0, length) for axis, length in enumerate(values.shape)]
        where[longest] = (where[longest] + shift) % values.shape[longest]
        spots.append(tuple(where))
    return values.at[spots[0]].set(least).at[spots[1]].set(largest)


def block_scale(own_key, shape, shards, smallest, high):
    def one(dim, blocks):
        steps = jax.random.uniform(jax.random.fold_in(jax.random.fold_in(own_key, 6), dim), (blocks,), jnp.float32, smallest / len(shards), high / len(shards))
        return jnp.repeat(jnp.exp(steps), shape[dim] // blocks).reshape((-1,) + (1,) * (len(shape) - dim - 1))

    level = one(*shards[0])
    for cut in shards[1:]:
        level = level * one(*cut)
    return level


def profile(amount, total, reach, skew):
    weights = [(1 << 20) // math.isqrt(rank ** skew) + 1 for rank in range(2, amount + 1)]
    surplus, holding = total - reach - (amount - 1), [1] * (amount - 1)
    while surplus > 0:
        movable = [i for i in range(amount - 1) if holding[i] < reach]
        whole, left = sum([weights[i] for i in movable]), surplus
        for i in movable:
            extra = min(reach - holding[i], max(1, left * weights[i] // whole), surplus)
            holding[i] = holding[i] + extra
            surplus = surplus - extra
    return np.array([reach] + holding)


def ragged(own_key, number_of, total, reach, skew):
    if number_of == 2:
        one = jax.random.randint(own_key, (), max(1, total - reach), min(reach, total - 1) + 1)
        return jnp.stack([one, total - one])
    sizes = jnp.asarray(profile(number_of, total, reach, skew), jnp.int32)
    pairs = (number_of - 1) // 2
    donor, sink = sizes[1:1 + 2 * pairs:2], sizes[2:2 + 2 * pairs:2]
    margin = jnp.minimum(donor - 1, reach - sink)
    passed = jax.random.randint(jax.random.fold_in(own_key, 1), (pairs,), 0, 1 << 20) % (margin + 1)
    sizes = sizes.at[1:1 + 2 * pairs:2].set(donor - passed).at[2:2 + 2 * pairs:2].set(sink + passed)
    return sizes[jax.random.permutation(jax.random.fold_in(own_key, 2), number_of)]


def gaussian(stream_key, extent, width, limit, shards=(), kind=jnp.bfloat16):
    values = width * jax.random.normal(stream_key, extent, jnp.float32)
    if shards:
        values = values * block_scale(stream_key, extent, shards, -0.22, 0.18)
    return jnp.clip(values, -limit, limit).astype(kind)


def setup_inputs(seed: int = 0) -> dict:
    key_of = jax.random.split(jax.random.key(seed), 22)
    patches = gaussian(key_of[0], (TOKENS, D), 1.0, 6.0, ((0, 128),))
    lengths = jax.vmap(lambda own: ragged(own, NSEG, MB_ROWS, SEG_MOST, 2))(jax.random.split(key_of[1], BLOCKS)).reshape((BLOCKS, NSEG)).astype(jnp.int32)
    skipped = plant((jax.random.randint(key_of[2], (TOKENS, 1), 0, 3) < 1).astype(jnp.int32), jax.random.fold_in(key_of[2], 1), 0, 1)
    strip_order = jax.vmap(lambda own: jax.random.permutation(own, N_FSDP))(jax.random.split(key_of[3], N_DP)).reshape((N_DP, N_FSDP)).astype(jnp.int32)
    decoder_grad = gaussian(key_of[4], (OUT_ROWS, DE), 1.0, 6.0, ((0, 128),))
    qkv_weight = gaussian(key_of[5], (D, 3 * D), D ** -0.5, 0.21875, ((0, 128),))
    out_weight = gaussian(key_of[6], (D, D), (D // 8) ** -0.5, 0.625, ((0, 128),))
    up_weight = gaussian(key_of[7], (D, FF), D ** -0.5, 0.21875, ((0, 128),))
    down_weight = gaussian(key_of[8], (FF, D), FF ** -0.5, 0.109375, ((0, 128),))
    embed_weight = gaussian(key_of[9], (D, DE), D ** -0.5, 0.21875, ((0, 128),))
    gain_one = jnp.clip(1.0 + 0.1 * jax.random.normal(key_of[10], (D,), jnp.float32), 0.5, 1.5).astype(jnp.bfloat16)
    shift_one = gaussian(key_of[11], (D,), 0.3, 1.5, ((0, 128),))
    gain_two = jnp.clip(1.0 + 0.1 * jax.random.normal(key_of[12], (D,), jnp.float32), 0.5, 1.5).astype(jnp.bfloat16)
    shift_two = gaussian(key_of[13], (D,), 0.3, 1.5, ((0, 128),))
    bias_query = gaussian(key_of[14], (D,), 0.3, 1.5, ((0, 128),))
    bias_value = gaussian(key_of[15], (D,), 0.3, 1.5, ((0, 128),))
    bias_out = gaussian(key_of[16], (D,), 0.3, 1.5, ((0, 128),))
    bias_up = gaussian(key_of[17], (FF,), 0.3, 1.5, ((0, 128),))
    bias_down = gaussian(key_of[18], (D,), 0.3, 1.5, ((0, 128),))
    bias_embed = gaussian(key_of[19], (DE,), 0.3, 1.5, ((0, 128),))
    mask_token = gaussian(key_of[20], (DE,), 1.0, 4.0, ((0, 128),))
    return {"patches": patches, "lengths": lengths, "skipped": skipped, "strip_order": strip_order, "decoder_grad": decoder_grad, "qkv_weight": qkv_weight, "out_weight": out_weight, "up_weight": up_weight, "down_weight": down_weight, "embed_weight": embed_weight, "gain_one": gain_one, "shift_one": shift_one, "gain_two": gain_two, "shift_two": shift_two, "bias_query": bias_query, "bias_value": bias_value, "bias_out": bias_out, "bias_up": bias_up, "bias_down": bias_down, "bias_embed": bias_embed, "mask_token": mask_token}


@jax.custom_vjp
def low(v):
    return lax.optimization_barrier(v.astype(jnp.bfloat16)).astype(jnp.float32)

@jax.custom_vjp
def low_back(v):
    return v

def low_keep(v):
    return (low(v), None)

def low_pass(kept, grad):
    return (grad,)

def back_keep(v):
    return (v, None)

def back_low(kept, grad):
    return (low(grad),)
low.defvjp(low_keep, low_pass)
low_back.defvjp(back_keep, back_low)
epsilon = 1e-06
masked_score = -1000000000.0
highest = lax.Precision.HIGHEST

def layer_norm(values, gain, shift):
    center = values - lax.optimization_barrier(jnp.mean(values, -1, keepdims=True))
    return center * lax.rsqrt(lax.optimization_barrier(jnp.mean(center * center, -1, keepdims=True)) + epsilon) * gain + shift

def matmul(left, right):
    return jnp.dot(left, right, precision=highest, preferred_element_type=jnp.float32)

def attend_block(parts):
    queries, keys_in, values_in, segment = parts
    same_doc = segment[:, None] == segment[None, :]
    scores = jnp.einsum('qhd,khd->hqk', queries, keys_in, precision=highest) * HEAD_DIM ** (-0.5)
    scores = low_back(jnp.where(same_doc[None], scores, masked_score))
    shifted = jnp.exp(scores - lax.optimization_barrier(jnp.max(scores, -1, keepdims=True)))
    weights = shifted / lax.optimization_barrier(jnp.sum(shifted, -1, keepdims=True))
    return jnp.einsum('hqk,khd->qhd', low(weights), values_in, precision=highest)

def reference(patches, lengths, skipped, strip_order, decoder_grad, qkv_weight, out_weight, up_weight, down_weight, embed_weight, gain_one, shift_one, gain_two, shift_two, bias_query, bias_value, bias_out, bias_up, bias_down, bias_embed, mask_token):
    tokens = patches.shape[0]
    bounds = jnp.cumsum(lengths, -1).astype(jnp.int32)
    starts = (bounds - lengths).astype(jnp.int32)
    places = jnp.arange(MB_ROWS, dtype=jnp.int32)
    segments = lax.optimization_barrier(jnp.sum((places[None, :, None] >= bounds[:, None, :]).astype(jnp.int32), -1)).astype(jnp.int32)
    skip_rows = skipped[:, 0].reshape(BLOCKS, MB_ROWS)
    through = jnp.cumsum(skip_rows, 1).astype(jnp.int32)
    before = (through - skip_rows).astype(jnp.int32)
    start_row = jnp.take_along_axis(starts, segments, 1).astype(jnp.int32)
    base = jnp.take_along_axis(before, start_row, 1).astype(jnp.int32)
    position = places[None, :] - start_row + through - base
    block = jnp.arange(BLOCKS, dtype=jnp.int32)
    device = block // MB
    source = device % N_FSDP
    group = device // N_FSDP
    strip = (block % MB)[:, None] * NSEG + segments
    offset = strip_order[group[:, None], strip]
    owner = (source[:, None] + offset) % N_FSDP
    dest = (((group[:, None] * N_FSDP + owner) * STRIPS + strip) * STRIP_POS + position).reshape(-1).astype(jnp.int32)
    filled = jnp.zeros((OUT_ROWS,), jnp.float32).at[dest].set(1.0)[:, None]

    def forward(rows, w_qkv, w_out, w_up, w_down, w_embed, g_one, c_one, g_two, c_two, b_query, b_value, b_out, b_up, b_down, b_embed, token_mask):
        normed_one = low(layer_norm(rows, g_one, c_one))
        bias_qkv = jnp.concatenate([b_query, jnp.zeros_like(b_query), b_value])
        packed = low(low_back(matmul(normed_one, w_qkv) + bias_qkv))
        split = packed.reshape(BLOCKS, MB_ROWS, 3, HEADS, HEAD_DIM)
        context = lax.map(jax.checkpoint(attend_block), (split[:, :, 0], split[:, :, 1], split[:, :, 2], segments))
        context = low(low_back(context.reshape(tokens, D)))
        middle = rows + low_back(matmul(context, w_out)) + b_out
        normed_two = low(layer_norm(middle, g_two, c_two))
        hidden = low_back(matmul(normed_two, w_up) + b_up)
        active = low(jax.nn.gelu(hidden, approximate=False))
        final_rows = middle + low_back(matmul(active, w_down)) + b_down
        embedded = low(matmul(low(final_rows), w_embed) + b_embed)
        placed = jnp.zeros((OUT_ROWS, DE), jnp.float32).at[dest].set(embedded)
        return filled * placed + (1.0 - filled) * token_mask[None, :]
    inputs = tuple((item.astype(jnp.float32) for item in (patches, qkv_weight, out_weight, up_weight, down_weight, embed_weight, gain_one, shift_one, gain_two, shift_two, bias_query, bias_value, bias_out, bias_up, bias_down, bias_embed, mask_token)))
    result, pullback = jax.vjp(forward, *inputs)
    grads = pullback(decoder_grad.astype(jnp.float32))
    return (result.astype(jnp.bfloat16), grads[0], grads[1], grads[2], grads[3], grads[4], grads[5], grads[6], grads[7], grads[8], grads[9], grads[10], grads[11], grads[12], grads[13], grads[14], grads[15], grads[16])
```

```python
import functools

import jax
import jax.numpy as jnp
from jax import lax
from jax.experimental import pallas as pl
from jax.experimental.pallas import tpu as pltpu
from jax.sharding import PartitionSpec as P

MESH = pl.DeviceIdType.MESH
BF, F32, I32 = jnp.bfloat16, jnp.float32, jnp.int32
ROWS, D, FF, DE, HEADS = 512, 768, 3072, 512, 12
PLANE, STRIPS, STRIP_POS, SEG = 16, 8, 529, 128
OUT_ROWS = STRIPS * STRIP_POS
WINDOW = 272
EPS = 1e-06
MASKED = -1e9
H_VEC, H_QKV, H_OUT, H_UP, H_DOWN, H_EMBED = 0, 1, 10, 13, 25, 37
GROUPS = ((0, 2), (2, 3))
ORDERS = ("xyz", "yzx", "zxy")
V_BE, V_MASK = 12, 13


def dot(a, b):
    return jnp.dot(a, b, preferred_element_type=F32)


def dot_t(a, b):
    return lax.dot_general(a, b, (((1,), (1,)), ((), ())), preferred_element_type=F32)


def tdot(a, b):
    return lax.dot_general(a, b, (((0,), (0,)), ((), ())), preferred_element_type=F32)


def iota(shape, dim):
    return lax.broadcasted_iota(I32, shape, dim)


def hot(mask):
    return jnp.where(mask, 1.0, 0.0).astype(BF)


def spread_hot(each, first):
    row, col = iota((D, 256), 0), iota((D, 256), 1) + first
    owner = (col * 10923) >> 16 if each == 6 else col >> 2
    return hot(row == 6 * owner)


class Place:
    def __init__(self):
        self.dp = lax.axis_index("dp")
        self.fs = lax.axis_index("fsdp")
        self.z, self.c = self.dp // 2, self.dp % 2
        self.y, self.x = self.fs // 4, self.fs % 4
        self.own = {"x": self.x, "y": self.y, "z": self.z}

    def near(self, axis, step):
        at = dict(self.own)
        at[axis] = (at[axis] + step) % 4
        return (at["z"] * 2 + self.c, at["y"] * 4 + at["x"])

    def sibling(self):
        return (self.z * 2 + 1 - self.c, self.fs)

    def plane(self, step):
        return (self.dp, (self.fs + step) % PLANE)


def enter(place):
    barrier = pltpu.get_barrier_semaphore()
    others = [place.near("z", s) for s in (1, 2, 3)] + [place.sibling()]
    others += [place.plane(t) for t in range(1, PLANE)]
    for other in others:
        pl.semaphore_signal(barrier, inc=1, device_id=other, device_id_type=MESH)
    pl.semaphore_wait(barrier, len(others))


class Links:
    def __init__(self, send_sem, recv_sem):
        self.send_sem, self.recv_sem = send_sem, recv_sem
        self.used = 0
        self.started = []

    def make(self, src, dst, index, device):
        return pltpu.make_async_remote_copy(
            src_ref=src,
            dst_ref=dst,
            send_sem=self.send_sem.at[index],
            recv_sem=self.recv_sem.at[index],
            device_id=device,
            device_id_type=MESH,
        )

    def send(self, src, dst, device):
        index = self.used
        self.used += 1
        copy = self.make(src, dst, index, device)
        copy.start()
        self.started.append(copy)
        return index

    def arrive(self, dst, index, device):
        self.make(dst, dst, index, device).wait_recv()

    def drain(self):
        for copy in self.started:
            copy.wait_send()
        self.started = []


def region(ks, coords, core, rows):
    ys = slice(None) if coords["y"] is None else coords["y"]
    zs = slice(None) if coords["z"] is None else coords["z"]
    xs = (
        slice(None)
        if coords["x"] is None
        else pl.ds(pl.multiple_of(coords["x"] * 128, 128), 128)
    )
    return (pl.ds(ks[0], ks[1]), ys, zs, core, rows, xs)


def rows_of(part, half=None):
    return pl.ds(32 * part, 32) if half is None else pl.ds(32 * part + 16 * half, 16)


def free(own, order, count):
    return {a: (None if a in order[:count] else own[a]) for a in "xyz"}


class Spread:
    def __init__(self, place, links, g, ks):
        self.p, self.l, self.g, self.ks = place, links, g, ks

    def at(self, coords, part, half=None, core=None):
        core = self.p.c if core is None else core
        return self.g.at[region(self.ks, coords, core, rows_of(part, half))]

    def send(self, coords, part, half, device):
        view = self.at(coords, part, half)
        return self.l.send(view, view, device)

    def direct(self, phase):
        sent = []
        for part, order in enumerate(ORDERS):
            coords = free(self.p.own, order, phase)
            axis = order[phase]
            for step in (1, 3, 2):
                index = self.send(coords, part, None, self.p.near(axis, step))
                sent.append((part, coords, axis, step, index))
        return sent

    def direct_arrive(self, sent):
        for part, coords, axis, step, index in sent:
            source = dict(coords, **{axis: (self.p.own[axis] + 4 - step) % 4})
            self.l.arrive(self.at(source, part), index, self.p.near(axis, 4 - step))

    def one(self):
        self.sent1 = self.direct(0)

    def two(self):
        self.direct_arrive(self.sent1)
        self.sent2 = self.direct(1)

    def three(self):
        self.direct_arrive(self.sent2)
        self.sib = []
        self.sent3 = []
        for part, order in enumerate(ORDERS):
            axis, base = order[2], free(self.p.own, order, 2)
            up = self.send(base, part, None, self.p.near(axis, 1))
            down = self.send(base, part, None, self.p.near(axis, 3))
            self.sent3.append((up, down))
        for part, order in enumerate(ORDERS):
            self.share(free(self.p.own, order, 2), part, None)

    def share(self, coords, part, half):
        index = self.send(coords, part, half, self.p.sibling())
        self.sib.append((coords, part, half, index))

    def four(self):
        self.sent4 = []
        for part, order in enumerate(ORDERS):
            axis, base = order[2], free(self.p.own, order, 2)
            up, down = self.sent3[part]
            own = self.p.own[axis]
            below = dict(base, **{axis: (own + 3) % 4})
            above = dict(base, **{axis: (own + 1) % 4})
            self.l.arrive(self.at(below, part), up, self.p.near(axis, 3))
            go_up = self.send(below, part, 0, self.p.near(axis, 1))
            self.l.arrive(self.at(above, part), down, self.p.near(axis, 1))
            go_down = self.send(above, part, 1, self.p.near(axis, 3))
            self.sent4.append((go_up, go_down))
            self.share(below, part, None)
            self.share(above, part, None)

    def five(self):
        for part, order in enumerate(ORDERS):
            axis, base = order[2], free(self.p.own, order, 2)
            go_up, go_down = self.sent4[part]
            far = dict(base, **{axis: (self.p.own[axis] + 2) % 4})
            self.l.arrive(self.at(far, part, 0), go_up, self.p.near(axis, 3))
            self.share(far, part, 0)
            self.l.arrive(self.at(far, part, 1), go_down, self.p.near(axis, 1))
            self.share(far, part, 1)

    def six(self):
        for coords, part, half, index in self.sib:
            self.l.arrive(
                self.at(coords, part, half, 1 - self.p.c), index, self.p.sibling()
            )


class Gather:
    def __init__(self, place, links, g, ks, bufs):
        self.p, self.l, self.g, self.ks = place, links, g, ks
        self.core_buf, self.half_bufs, self.full_bufs, self.two_bufs, self.one_bufs = bufs

    def at(self, coords, part, half=None):
        return self.g.at[region(self.ks, coords, self.p.c, rows_of(part, half))]

    def k(self):
        return pl.ds(self.ks[0], self.ks[1])

    def add(self, coords, start, count, reads):
        xs = (
            slice(None)
            if coords["x"] is None
            else pl.ds(pl.multiple_of(coords["x"] * 128, 128), 128)
        )

        def body(k, _):
            for y in range(4) if coords["y"] is None else (coords["y"],):
                for z in range(4) if coords["z"] is None else (coords["z"],):
                    place = (k, y, z, self.p.c, pl.ds(start, count), xs)
                    total = self.g[place].astype(F32)
                    for read in reads:
                        total = total + read(k, y, z).astype(F32)
                    self.g[place] = total.astype(BF)
            return 0

        lax.fori_loop(self.ks[0], self.ks[0] + self.ks[1], body, 0)

    @staticmethod
    def reader(buf, coords, slot):
        def read(k, y, z):
            index = (slot, k)
            index += (y,) if coords["y"] is None else ()
            index += (z,) if coords["z"] is None else ()
            return buf[index]

        return read

    def one(self):
        src = self.g.at[self.k(), :, :, 1 - self.p.c]
        self.sent = self.l.send(src, self.core_buf.at[0 : self.ks[1]], self.p.sibling())

    def two(self):
        self.l.arrive(self.core_buf.at[0 : self.ks[1]], self.sent, self.p.sibling())
        whole = {"x": None, "y": None, "z": None}
        self.sent1 = []
        for part, order in enumerate(ORDERS):
            rows = rows_of(part)
            self.add(whole, 32 * part, 32, [lambda k, y, z: self.core_buf[k - self.ks[0], y, z, rows]])
            axis, base = order[2], free(self.p.own, order, 2)
            far = dict(base, **{axis: (self.p.own[axis] + 2) % 4})
            buf = self.half_bufs[part]
            up = self.l.send(self.at(far, part, 0), buf.at[0, self.k()], self.p.near(axis, 1))
            down = self.l.send(self.at(far, part, 1), buf.at[1, self.k()], self.p.near(axis, 3))
            self.sent1.append((up, down))

    def three(self):
        self.sent2 = []
        for part, order in enumerate(ORDERS):
            axis, base = order[2], free(self.p.own, order, 2)
            half, full = self.half_bufs[part], self.full_bufs[part]
            up, down = self.sent1[part]
            above = dict(base, **{axis: (self.p.own[axis] + 1) % 4})
            below = dict(base, **{axis: (self.p.own[axis] + 3) % 4})
            self.l.arrive(half.at[0, self.k()], up, self.p.near(axis, 3))
            self.add(above, 32 * part, 16, [self.reader(half, above, 0)])
            go_up = self.l.send(self.at(above, part), full.at[0, self.k()], self.p.near(axis, 1))
            self.l.arrive(half.at[1, self.k()], down, self.p.near(axis, 1))
            self.add(below, 32 * part + 16, 16, [self.reader(half, below, 1)])
            go_down = self.l.send(
                self.at(below, part), full.at[1, self.k()], self.p.near(axis, 3)
            )
            self.sent2.append((go_up, go_down))

    def direct(self, coords, part, axis, buf):
        sent = []
        for step in (1, 3, 2):
            target = dict(coords, **{axis: (self.p.own[axis] + step) % 4})
            device = self.p.near(axis, step)
            sent.append(
                (step, self.l.send(self.at(target, part), buf.at[step - 1, self.k()], device))
            )
        return sent

    def direct_arrive(self, sent, coords, part, axis, buf):
        for step, index in sent:
            self.l.arrive(buf.at[step - 1, self.k()], index, self.p.near(axis, 4 - step))
        self.add(coords, 32 * part, 32, [self.reader(buf, coords, s) for s in range(3)])

    def four(self):
        self.sent3 = []
        for part, order in enumerate(ORDERS):
            axis, base = order[2], free(self.p.own, order, 2)
            full = self.full_bufs[part]
            up, down = self.sent2[part]
            self.l.arrive(full.at[0, self.k()], up, self.p.near(axis, 3))
            self.l.arrive(full.at[1, self.k()], down, self.p.near(axis, 1))
            self.add(
                base, 32 * part, 32, [self.reader(full, base, 0), self.reader(full, base, 1)]
            )
            coords = free(self.p.own, order, 1)
            self.sent3.append(self.direct(coords, part, order[1], self.two_bufs[part]))

    def five(self):
        self.sent4 = []
        for part, order in enumerate(ORDERS):
            coords = free(self.p.own, order, 1)
            self.direct_arrive(self.sent3[part], coords, part, order[1], self.two_bufs[part])
            self.sent4.append(self.direct(self.p.own, part, order[0], self.one_bufs[part]))

    def six(self):
        for part, order in enumerate(ORDERS):
            self.direct_arrive(
                self.sent4[part], self.p.own, part, order[0], self.one_bufs[part]
            )


def reduce_bufs():
    half = [(2, 5, 4, 16, 512), (2, 5, 4, 4, 16, 128), (2, 5, 4, 16, 512)]
    full = [(2, 5, 4, 32, 512), (2, 5, 4, 4, 32, 128), (2, 5, 4, 32, 512)]
    two = [(3, 5, 32, 512), (3, 5, 4, 32, 128), (3, 5, 4, 32, 128)]
    one = [(3, 5, 32, 128)] * 3
    return [(3, 4, 4, 96, 512)] + half + full + two + one


def mean_rows(v):
    return jnp.mean(v, -1, keepdims=True)


def hat_of(v):
    center = v - mean_rows(v)
    factor = lax.rsqrt(mean_rows(center * center) + EPS)
    return center * factor, factor


def norm_back(dy, gain, hat, factor):
    scaled = dy * gain
    return factor * (scaled - mean_rows(scaled) - hat * mean_rows(scaled * hat))


def col_sum(v):
    return jnp.sum(v, 0, keepdims=True)


SCRATCH = {
    "g": ((5, 4, 4, 2, 96, 512), BF),
    "rb": ((PLANE, 32, 128), BF),
    "fin_send": ((PLANE, 32, 128), BF),
    "fin_recv": ((PLANE, 32, 128), BF),
    "meta_all": ((PLANE, 8, 128), I32),
    "n1": ((ROWS, D), BF),
    "qkv": ((ROWS, 3 * D), BF),
    "prob": ((2 * HEADS, 256, 256), BF),
    "ctx": ((ROWS, D), BF),
    "h1": ((ROWS, D), F32),
    "n2": ((ROWS, D), BF),
    "act": ((ROWS, FF), BF),
    "slope": ((ROWS, FF), BF),
    "hb": ((ROWS, D), BF),
    "low": ((ROWS, D), BF),
    "emb": ((ROWS, DE), BF),
    "wide": ((ROWS, D), F32),
    "acc": ((ROWS, D), F32),
    "vec": ((16, D), F32),
    "vgrad": ((16, D), F32),
    "bqkv": ((8, 3 * D), F32),
    "bup": ((8, FF), F32),
    "dec": ((OUT_ROWS, DE), BF),
    "perm": ((STRIPS, WINDOW, SEG), BF),
    "out_slots": ((PLANE, SEG, DE), BF),
    "in_slots": ((PLANE, SEG, DE), BF),
}
N_SEM = 256


def kernel(shard, meta, x_ref, cot, dec_out, patch_out, fin, *refs):
    s = dict(zip(SCRATCH, refs))
    rest = refs[len(SCRATCH):]
    bufs, (send_sem, recv_sem, local_sem, core_free, slot_free) = rest[:13], rest[13:]
    bufs = (bufs[0], bufs[1:4], bufs[4:7], bufs[7:10], bufs[10:13])
    g = s["g"]
    place = Place()
    links = Links(send_sem, recv_sem)

    def weight(h):
        tile = h // 2
        lanes = pl.ds(pl.multiple_of((h % 2) * 256, 256), 256)
        return g[tile // 4, tile % 4, :, :, :, lanes].reshape(D, 256)

    def put_grad(h, value):
        tile = h // 2
        lanes = pl.ds(pl.multiple_of((h % 2) * 256, 256), 256)
        g[tile // 4, tile % 4, :, :, :, lanes] = value.astype(BF).reshape(4, 2, 96, 256)

    def cols(i, width=256):
        return pl.ds(pl.multiple_of(i * width, width), width)

    cot_load = pltpu.make_async_copy(cot, s["dec"], local_sem.at[0])
    cot_load.start()
    enter(place)
    rb, meta_all = s["rb"], s["meta_all"]
    sent = []
    for t in range(1, PLANE):
        to = place.plane(t)
        sent.append(links.send(shard.at[to[1]], rb.at[place.fs], to))
    meta_sent = []
    for t in range(1, PLANE):
        meta_sent.append(links.send(meta, meta_all.at[place.fs], place.plane(t)))
    rb[place.fs] = shard[place.fs]
    meta_all[place.fs] = meta[...]
    for t in range(1, PLANE):
        source = place.plane(PLANE - t)
        links.arrive(rb.at[source[1]], sent[t - 1], source)
    arrived = rb[...].reshape(PLANE * 32, 128)
    row, col = iota((96, PLANE * 32), 0), iota((96, PLANE * 32), 1)
    sender = (row * 43) >> 8
    target = sender * 32 + (row - sender * 6)
    own_lanes = pl.ds(pl.multiple_of(place.x * 128, 128), 128)
    for k in range(5):
        block = dot(hot(col == target + 6 * k), arrived).astype(BF)
        g[k, place.y, place.z, place.c, :, own_lanes] = block

    spreads = [Spread(place, links, g, ks) for ks in GROUPS]
    first, later = spreads
    first.one()
    later.one()
    first.two()
    later.two()
    first.three()
    later.three()

    for t in range(1, PLANE):
        source = place.plane(PLANE - t)
        links.arrive(meta_all.at[source[1]], meta_sent[t - 1], source)
    cot_load.wait()

    def lens_of(m, blk):
        lens = [m[4:5, blk * 4 + j : blk * 4 + j + 1].astype(F32) for j in range(4)]
        starts = [jnp.zeros_like(lens[0])]
        for j in range(3):
            starts.append(starts[j] + lens[j])
        return lens, starts

    total = jnp.zeros((1, DE), F32)
    orders = [meta[5:6, k : k + 1] for k in range(STRIPS)]
    for k in range(STRIPS):
        m = jnp.zeros((8, 128), I32)
        for source in range(PLANE):
            here = orders[k] == (place.fs + PLANE - source) % PLANE
            m = jnp.where(here, meta_all[source], m)
        blk, j = k // 4, k % 4
        lens, starts = lens_of(m, blk)
        skip = jnp.concatenate([m[2 * blk : 2 * blk + 1], m[2 * blk + 1 : 2 * blk + 2]], 1)
        skip = jnp.broadcast_to(skip.astype(F32), (8, 256)).astype(BF)
        r, t = iota((256, SEG), 0).astype(F32), iota((256, SEG), 1).astype(F32)
        local = dot(skip, hot(r - starts[j] == t))
        tri = hot(iota((SEG, SEG), 0) <= iota((SEG, SEG), 1))
        through = dot(local.astype(BF), tri)[0:1]
        off = (STRIP_POS * k) % 16
        base = STRIP_POS * k - off
        lane = iota((WINDOW, SEG), 1).astype(F32)
        spot = iota((WINDOW, SEG), 0).astype(F32)
        perm = hot((spot == lane + through + float(off)) & (lane < lens[j]))
        s["perm"][k] = perm
        picked = tdot(perm, s["dec"][base : base + WINDOW])
        s["act"][SEG * j : SEG * j + SEG, DE * blk : DE * blk + DE] = picked.astype(BF)
        total = total - col_sum(picked)

    def sum_rows(i, acc):
        part = s["dec"][pl.ds(pl.multiple_of(i * 16, 16), 16), :].astype(F32)
        return acc + part

    summed = lax.fori_loop(0, OUT_ROWS // 16, sum_rows, jnp.zeros((16, DE), F32))
    total = total + col_sum(summed) + col_sum(s["dec"][OUT_ROWS - 8 :, :].astype(F32))
    s["vgrad"][...] = jnp.zeros_like(s["vgrad"])
    s["vgrad"][V_MASK : V_MASK + 1, 0:DE] = total

    def weight_of(k, value):
        return jnp.where(orders[k] == value, 1.0, 0.0).astype(BF)

    def fill_slot(t, _):
        total = jnp.zeros((SEG, DE), BF)
        for k in range(STRIPS):
            blk, j = k // 4, k % 4
            one = s["act"][SEG * j : SEG * j + SEG, DE * blk : DE * blk + DE]
            total = total + one * weight_of(k, (PLANE - t) % PLANE)
        s["out_slots"][t] = total
        return 0

    lax.fori_loop(0, PLANE, fill_slot, 0)

    first.four()
    later.four()
    first.five()
    first.six()
    later.five()
    later.six()
    cot_sent = []
    for t in range(1, PLANE):
        cot_sent.append(
            links.send(s["out_slots"].at[t], s["in_slots"].at[t], place.plane(t))
        )
    s["in_slots"][0] = s["out_slots"][0]

    chunk = g[0, 0, :, :, :, 0:128].reshape(D, 128)
    table = s["acc"]

    def spread_six(i, _):
        table[0:128, cols(i)] = tdot(chunk, spread_hot(6, 256 * i))
        return 0

    def spread_four(i, _):
        table[128:256, cols(i)] = tdot(chunk, spread_hot(4, 256 * i))
        return 0

    lax.fori_loop(0, 3, spread_six, 0)
    lax.fori_loop(0, 2, spread_four, 0)
    lane6 = iota((16, D), 1)
    lane6 = lane6 - 6 * ((lane6 * 10923) >> 16)
    row6 = iota((16, D), 0)
    for v in range(12):
        low = (6 * v) // 8 * 8
        window = table[low : low + 16, :]
        s["vec"][v : v + 1] = col_sum(jnp.where(row6 + (low - 6 * v) == lane6, window, 0.0))
    lane4, row4 = iota((8, DE), 1) & 3, iota((8, DE), 0)
    few = table[128 + 72 : 128 + 80, 0:DE]
    for i, v in enumerate((V_BE, V_MASK)):
        s["vec"][v : v + 1, 0:DE] = col_sum(jnp.where(row4 - 4 * i == lane4, few, 0.0))
    vec = s["vec"]
    s["bqkv"][...] = jnp.zeros_like(s["bqkv"])
    s["bqkv"][0:1, 0:D] = vec[4:5]
    s["bqkv"][0:1, 2 * D :] = vec[5:6]
    for q in range(4):
        s["bup"][0:1, q * D : (q + 1) * D] = vec[8 + q : 9 + q]

    def norm_one(i, _):
        rows = cols(i, 128)
        hat, _f = hat_of(x_ref[rows, :].astype(F32))
        s["n1"][rows, :] = (hat * vec[0:1] + vec[1:2]).astype(BF)
        return 0

    lax.fori_loop(0, 4, norm_one, 0)

    def qkv_tile(t, _):
        for i in range(2):
            rows = cols(i)
            out = dot(s["n1"][rows, :], weight(H_QKV + t)) + s["bqkv"][0:1, cols(t)]
            s["qkv"][rows, cols(t)] = out.astype(BF)
        return 0

    lax.fori_loop(0, 9, qkv_tile, 0)

    lens_own = [lens_of(meta[...], b) for b in range(2)]

    def doc_bias(starts):
        r, c = iota((256, 256), 0).astype(F32), iota((256, 256), 1).astype(F32)
        doc_r, doc_c = jnp.zeros_like(r), jnp.zeros_like(c)
        for j in range(1, 4):
            doc_r = doc_r + jnp.where(r >= starts[j], 1.0, 0.0)
            doc_c = doc_c + jnp.where(c >= starts[j], 1.0, 0.0)
        return doc_r == doc_c

    lane = iota((256, 128), 1)
    for blk in range(2):
        rows = slice(256 * blk, 256 * blk + 256)
        same = doc_bias(lens_own[blk][1])

        def heads(hp, _):
            q2 = s["qkv"][rows, cols(hp, 128)] * jnp.asarray(0.125, BF)
            k2 = s["qkv"][rows, cols(6 + hp, 128)]
            v2 = s["qkv"][rows, cols(12 + hp, 128)]
            outs = []
            for h in range(2):
                mine = (lane >= 64) if h else (lane < 64)
                scores = dot_t(jnp.where(mine, q2, jnp.zeros_like(q2)), k2)
                scores = jnp.where(same, scores, MASKED)
                e = jnp.exp(scores - jnp.max(scores, -1, keepdims=True))
                p = (e * (1.0 / jnp.sum(e, -1, keepdims=True))).astype(BF)
                s["prob"][12 * blk + 2 * hp + h] = p
                outs.append(dot(p, v2))
            s["ctx"][rows, cols(hp, 128)] = jnp.where(lane < 64, outs[0], outs[1]).astype(BF)
            return 0

        lax.fori_loop(0, 6, heads, 0)

    def out_tile(t, _):
        out = dot(s["ctx"][...], weight(H_OUT + t)) + vec[6:7, cols(t)]
        s["h1"][:, cols(t)] = x_ref[:, cols(t)].astype(F32) + out
        return 0

    lax.fori_loop(0, 3, out_tile, 0)

    def norm_two(i, _):
        rows = cols(i, 128)
        hat, _f = hat_of(s["h1"][rows, :])
        s["n2"][rows, :] = (hat * vec[2:3] + vec[3:4]).astype(BF)
        return 0

    lax.fori_loop(0, 4, norm_two, 0)

    def up_tile(t, _):
        for i in range(2):
            rows = cols(i)
            u = dot(s["n2"][rows, :], weight(H_UP + t)) + s["bup"][0:1, cols(t)]
            phi = 0.5 * (1.0 + lax.erf(u * 0.7071067811865476))
            density = jnp.exp(-0.5 * u * u) * 0.3989422804014327
            s["act"][rows, cols(t)] = (u * phi).astype(BF)
            s["slope"][rows, cols(t)] = (phi + u * density).astype(BF)
        return 0

    lax.fori_loop(0, 12, up_tile, 0)
    for t in range(3):
        for i in range(2):
            rows = cols(i)
            out = s["h1"][rows, cols(t)] + vec[7:8, cols(t)]
            for q in range(4):
                out = out + dot(s["act"][rows, cols(q, D)], weight(H_DOWN + 3 * q + t))
            s["hb"][rows, cols(t)] = out.astype(BF)
    for t in range(2):
        out = dot(s["hb"][...], weight(H_EMBED + t)) + vec[V_BE : V_BE + 1, cols(t)]
        s["emb"][:, cols(t)] = out.astype(BF)

    slot = iota((1, PLANE), 1)
    slot_start, slot_len = jnp.zeros((1, PLANE), F32), jnp.zeros((1, PLANE), F32)
    for k in range(STRIPS):
        blk, j = k // 4, k % 4
        lens, starts = lens_own[blk]
        slot_start = jnp.where(orders[k] == slot, starts[j] + 256.0 * blk, slot_start)
        slot_len = jnp.where(orders[k] == slot, lens[j], slot_len)

    def slot_hot(t):
        i, r = iota((SEG, ROWS), 0).astype(F32), iota((SEG, ROWS), 1).astype(F32)
        start, size = slot_start[:, t : t + 1], slot_len[:, t : t + 1]
        return hot((r - start == i) & (i < size))

    for t in range(1, PLANE):
        links.arrive(s["in_slots"].at[t], cot_sent[t - 1], place.plane(PLANE - t))
    de = s["emb"]
    total = jnp.zeros((ROWS, DE), F32)
    links.drain()
    for t in range(PLANE):
        pick = slot_hot(t)
        total = total + tdot(pick, s["in_slots"][(PLANE - t) % PLANE])
        s["out_slots"][t] = dot(pick, s["emb"][...]).astype(BF)
    de[...] = total.astype(BF)
    for t in range(1, PLANE):
        pl.semaphore_signal(slot_free, inc=1, device_id=place.plane(t), device_id_type=MESH)
    pl.semaphore_wait(slot_free, PLANE - 1)
    emb_sent = []
    for t in range(1, PLANE):
        emb_sent.append(
            links.send(s["out_slots"].at[t], s["in_slots"].at[t], place.plane(t))
        )
    s["in_slots"][0] = s["out_slots"][0]

    vg = s["vgrad"]
    vg[V_BE : V_BE + 1, 0:DE] = col_sum(de[...].astype(F32))
    wide = s["wide"]

    def embed_back(i, acc):
        rows = cols(i)
        dh = dot_t(de[rows, 0:256], weight(H_EMBED)) + dot_t(de[rows, 256:], weight(H_EMBED + 1))
        wide[rows, :] = dh
        s["low"][rows, :] = dh.astype(BF)
        return acc + col_sum(dh)

    vg[7:8] = lax.fori_loop(0, 2, embed_back, jnp.zeros((1, D), F32))
    for t in range(2):
        put_grad(H_EMBED + t, tdot(s["hb"][...], de[:, cols(t)]))

    def down_part(q, _):

        def rows_part(i, acc):
            rows = cols(i)
            da = dot_t(s["low"][rows, 0:256], weight(H_DOWN + 3 * q))
            for t in range(1, 3):
                da = da + dot_t(s["low"][rows, cols(t)], weight(H_DOWN + 3 * q + t))
            du = (da * s["slope"][rows, cols(q, D)].astype(F32)).astype(BF)
            s["slope"][rows, cols(q, D)] = du
            return acc + col_sum(du.astype(F32))

        vg[pl.ds(8 + q, 1), :] = lax.fori_loop(0, 2, rows_part, jnp.zeros((1, D), F32))
        a = s["act"][:, cols(q, D)]
        for t in range(3):
            put_grad(H_DOWN + 3 * q + t, tdot(a, s["low"][:, cols(t)]))
        return 0

    lax.fori_loop(0, 4, down_part, 0)
    acc = s["acc"]

    def up_part(q, _):
        def rows_part(i, _):
            rows = cols(i)
            total = dot_t(s["slope"][rows, cols(3 * q)], weight(H_UP + 3 * q))
            for t in range(1, 3):
                total = total + dot_t(s["slope"][rows, cols(3 * q + t)], weight(H_UP + 3 * q + t))
            acc[rows, :] = jnp.where(q == 0, total, acc[rows, :] + total)
            return 0

        lax.fori_loop(0, 2, rows_part, 0)
        for t in range(3):
            put_grad(H_UP + 3 * q + t, tdot(s["n2"][...], s["slope"][:, cols(3 * q + t)]))
        return 0

    lax.fori_loop(0, 4, up_part, 0)

    def norm_two_back(i, sums):
        rows = cols(i, 128)
        hat, factor = hat_of(s["h1"][rows, :])
        dn = acc[rows, :]
        dh = wide[rows, :] + norm_back(dn, vec[2:3], hat, factor)
        wide[rows, :] = dh
        s["low"][rows, :] = dh.astype(BF)
        return (sums[0] + col_sum(dn * hat), sums[1] + col_sum(dn), sums[2] + col_sum(dh))

    zero = jnp.zeros((1, D), F32)
    vg[2:3], vg[3:4], vg[6:7] = lax.fori_loop(0, 4, norm_two_back, (zero, zero, zero))

    gathers = [Gather(place, links, g, ks, bufs) for ks in GROUPS]
    g_first, g_later = gathers

    def out_back(i, _):
        rows = cols(i)
        total = dot_t(s["low"][rows, 0:256], weight(H_OUT))
        for t in range(1, 3):
            total = total + dot_t(s["low"][rows, cols(t)], weight(H_OUT + t))
        s["hb"][rows, :] = total.astype(BF)
        return 0

    lax.fori_loop(0, 2, out_back, 0)
    for t in range(3):
        put_grad(H_OUT + t, tdot(s["ctx"][...], s["low"][:, cols(t)]))

    for blk in range(2):
        rows = slice(256 * blk, 256 * blk + 256)

        def heads_back(hp, _):
            q2 = s["qkv"][rows, cols(hp, 128)]
            k2 = s["qkv"][rows, cols(6 + hp, 128)]
            v2 = s["qkv"][rows, cols(12 + hp, 128)]
            do2 = s["hb"][rows, cols(hp, 128)]
            dq, dk, dv = [], [], []
            for h in range(2):
                mine = (lane >= 64) if h else (lane < 64)
                p = s["prob"][12 * blk + 2 * hp + h]
                dp = dot_t(jnp.where(mine, do2, jnp.zeros_like(do2)), v2)
                pf = p.astype(F32)
                inner = jnp.sum(pf * dp, -1, keepdims=True)
                ds = (pf * (dp - inner)).astype(BF)
                dq.append(dot(ds, k2))
                dk.append(tdot(ds, q2))
                dv.append(tdot(p, do2))
            lo = lane < 64
            s["qkv"][rows, cols(hp, 128)] = (jnp.where(lo, dq[0], dq[1]) * 0.125).astype(BF)
            s["qkv"][rows, cols(6 + hp, 128)] = (jnp.where(lo, dk[0], dk[1]) * 0.125).astype(BF)
            s["qkv"][rows, cols(12 + hp, 128)] = jnp.where(lo, dv[0], dv[1]).astype(BF)
            return 0

        lax.fori_loop(0, 6, heads_back, 0)

    def bias_sums(i, sums):
        rows = cols(i, 64)
        q = s["qkv"][rows, 0:D].astype(F32)
        v = s["qkv"][rows, 2 * D :].astype(F32)
        return (sums[0] + col_sum(q), sums[1] + col_sum(v))

    vg[4:5], vg[5:6] = lax.fori_loop(0, 8, bias_sums, (zero, zero))

    def qkv_part(q, _):
        def rows_part(i, _):
            rows = cols(i)
            total = dot_t(s["qkv"][rows, cols(3 * q)], weight(H_QKV + 3 * q))
            for t in range(1, 3):
                total = total + dot_t(s["qkv"][rows, cols(3 * q + t)], weight(H_QKV + 3 * q + t))
            acc[rows, :] = jnp.where(q == 0, total, acc[rows, :] + total)
            return 0

        lax.fori_loop(0, 2, rows_part, 0)
        for t in range(3):
            put_grad(H_QKV + 3 * q + t, tdot(s["n1"][...], s["qkv"][:, cols(3 * q + t)]))
        return 0

    lax.fori_loop(0, 3, qkv_part, 0)

    def norm_one_back(i, sums):
        rows = cols(i, 128)
        hat, factor = hat_of(x_ref[rows, :].astype(F32))
        dn = acc[rows, :]
        wide[rows, :] = wide[rows, :] + norm_back(dn, vec[0:1], hat, factor)
        return (sums[0] + col_sum(dn * hat), sums[1] + col_sum(dn))

    vg[0:1], vg[1:2] = lax.fori_loop(0, 4, norm_one_back, (zero, zero))
    patch_store = pltpu.make_async_copy(wide, patch_out, local_sem.at[1])
    patch_store.start()

    table[0:256, :] = jnp.zeros((256, D), F32)
    lane6 = iota((8, D), 1)
    lane6 = lane6 - 6 * ((lane6 * 10923) >> 16)
    row6 = iota((8, D), 0)
    for a in range(9):
        rows = jnp.zeros((8, D), F32)
        for v in range(12):
            if 6 * v < 8 * a + 8 and 6 * v + 6 > 8 * a:
                rows = jnp.where(row6 + (8 * a - 6 * v) == lane6, vg[v : v + 1], rows)
        table[8 * a : 8 * a + 8, :] = rows
    rows = jnp.zeros((8, DE), F32)
    for i, v in enumerate((V_BE, V_MASK)):
        rows = jnp.where(row4 - 4 * i == lane4, vg[v : v + 1, 0:DE], rows)
    table[128 + 72 : 128 + 80, 0:DE] = rows

    def fold_six(i, total):
        return total + dot_t(spread_hot(6, 256 * i), table[0:128, cols(i)].astype(BF))

    def fold_four(i, total):
        return total + dot_t(spread_hot(4, 256 * i), table[128:256, cols(i)].astype(BF))

    chunk = lax.fori_loop(0, 3, fold_six, jnp.zeros((D, 128), F32))
    chunk = lax.fori_loop(0, 2, fold_four, chunk)
    g[0, 0, :, :, :, 0:128] = chunk.astype(BF).reshape(4, 2, 96, 128)

    g_later.one()
    g_later.two()
    pl.semaphore_signal(core_free, inc=1, device_id=place.sibling(), device_id_type=MESH)
    pl.semaphore_wait(core_free, 1)
    g_first.one()
    g_first.two()
    for t in range(1, PLANE):
        links.arrive(s["in_slots"].at[t], emb_sent[t - 1], place.plane(PLANE - t))
    mask = vec[V_MASK : V_MASK + 1, 0:DE]
    blank = jnp.broadcast_to(mask.astype(BF), (16, DE))

    def fill(i, _):
        s["dec"][cols(i, 16), :] = blank
        return 0

    lax.fori_loop(0, OUT_ROWS // 16, fill, 0)
    s["dec"][OUT_ROWS - 8 :, :] = blank[0:8]
    for k in range(STRIPS):
        perm = s["perm"][k]
        base = STRIP_POS * k - (STRIP_POS * k) % 16

        def find(t, total):
            return total + s["in_slots"][t] * weight_of(k, t)

        strip = lax.fori_loop(0, PLANE, find, jnp.zeros((SEG, DE), BF))
        placed = dot(perm, strip)
        filled = jnp.sum(perm.astype(F32), -1, keepdims=True)
        s["dec"][base : base + WINDOW] = jnp.where(filled > 0.5, placed, mask).astype(BF)
    dec_store = pltpu.make_async_copy(s["dec"], dec_out, local_sem.at[0])
    dec_store.start()
    g_later.three()
    g_first.three()
    g_later.four()
    g_first.four()
    g_later.five()
    g_first.five()
    g_later.six()
    g_first.six()
    row, col = iota((PLANE * 32, 96), 0), iota((PLANE * 32, 96), 1)
    inner_row = row & 31
    base_row = 6 * (row >> 5)
    slots = jnp.zeros((PLANE * 32, 128), F32)
    for k in range(5):
        j = inner_row - 6 * k
        pick = hot((col == base_row + j) & (j >= 0) & (j < 6))
        slots = slots + dot(pick, g[k, place.y, place.z, place.c, :, own_lanes])
    s["fin_send"][...] = slots.astype(BF).reshape(PLANE, 32, 128)
    fin_sent = []
    for t in range(1, PLANE):
        to = place.plane(t)
        fin_sent.append(links.send(s["fin_send"].at[to[1]], s["fin_recv"].at[place.fs], to))
    s["fin_recv"][place.fs] = s["fin_send"][place.fs]
    for t in range(1, PLANE):
        source = place.plane(PLANE - t)
        links.arrive(s["fin_recv"].at[source[1]], fin_sent[t - 1], source)
    fin[...] = s["fin_recv"][...]
    links.drain()
    dec_store.wait()
    patch_store.wait()


def mega(shard, meta, x, cot):
    dma = pltpu.SemaphoreType.DMA
    vmem = pl.BlockSpec(memory_space=pltpu.VMEM)
    hbm = pl.BlockSpec(memory_space=pl.ANY)
    return pl.pallas_call(
        kernel,
        out_shape=(
            jax.ShapeDtypeStruct((OUT_ROWS, DE), BF),
            jax.ShapeDtypeStruct((ROWS, D), F32),
            jax.ShapeDtypeStruct((PLANE, 32, 128), BF),
        ),
        in_specs=[vmem, vmem, vmem, hbm],
        out_specs=(hbm, hbm, vmem),
        scratch_shapes=[pltpu.VMEM(shape, kind) for shape, kind in SCRATCH.values()]
        + [pltpu.VMEM(shape, BF) for shape in reduce_bufs()]
        + [dma((N_SEM,)), dma((N_SEM,)), dma((2,)), pltpu.SemaphoreType.REGULAR, pltpu.SemaphoreType.REGULAR],
        compiler_params=pltpu.CompilerParams(
            collective_id=1, has_side_effects=True, vmem_limit_bytes=64 * 1024 * 1024
        ),
        name="layer",
    )(shard, meta, x, cot)


def on_device(patches, lengths, skipped, strip_order, decoder_grad, qkv_weight, out_weight,
              up_weight, down_weight, embed_weight, gain_one, shift_one, gain_two, shift_two,
              bias_query, bias_value, bias_out, bias_up, bias_down, bias_embed, mask_token):
    vectors = jnp.concatenate(
        [gain_one, shift_one, gain_two, shift_two, bias_query, bias_value, bias_out, bias_down,
         bias_up, bias_embed, mask_token]
    )
    up = up_weight.reshape(6, 128, 4, 6).transpose(0, 2, 1, 3).reshape(6, FF)
    down = down_weight.reshape(4, 6, D).transpose(1, 0, 2).reshape(6, FF)
    first = jnp.zeros((6, 256), BF).at[0, 0:80].set(vectors)
    last = jnp.zeros((6, 256), BF)
    lanes = jnp.concatenate([first, qkv_weight, out_weight, up, down, embed_weight, last], 1)
    shard = lanes.reshape(6, 5, PLANE, 128).transpose(2, 1, 0, 3).reshape(PLANE, 30, 128)
    shard = jnp.pad(shard, ((0, 0), (0, 2), (0, 0)))
    meta = jnp.concatenate(
        [
            skipped.reshape(4, 128),
            jnp.pad(lengths.reshape(1, 8), ((0, 0), (0, 120))),
            jnp.pad(strip_order, ((0, 2), (0, 112))),
        ],
        0,
    )
    dec, patch_grad, fin = mega(shard, meta, patches, decoder_grad)
    fin = fin[:, 0:30].reshape(PLANE, 5, 6, 128).transpose(2, 1, 0, 3).reshape(6, 10240)
    fin = fin.astype(F32)
    parts = []
    at = 256
    for width in (3 * D, D, FF, FF, DE):
        parts.append(fin[:, at : at + width])
        at += width
    g_qkv, g_out, g_up, g_down, g_embed = parts
    g_up = g_up.reshape(6, 4, 128, 6).transpose(0, 2, 1, 3).reshape(6, FF)
    g_down = g_down.reshape(6, 4, D).transpose(1, 0, 2).reshape(24, D)
    v = fin[0, 0:80]
    return (dec, patch_grad, g_qkv, g_out, g_up, g_down, g_embed, v[0:6], v[6:12], v[12:18],
            v[18:24], v[24:30], v[30:36], v[36:42], v[48:72], v[42:48], v[72:76], v[76:80])


def solution(mesh):
    both = ("dp", "fsdp")
    rows, vector = P(both, None), P(both)
    return jax.shard_map(
        on_device,
        mesh=mesh,
        in_specs=(rows, rows, rows, P("dp", None), rows) + (rows,) * 5 + (vector,) * 11,
        out_specs=(rows,) * 7 + (vector,) * 11,
        check_vma=False,
    )
```

```python
import functools

import jax
import jax.numpy as jnp
from jax import lax
from jax.experimental import pallas as pl
from jax.experimental.pallas import tpu as pltpu
from jax.sharding import PartitionSpec as P

MESH = pl.DeviceIdType.MESH
BF, F32, I32 = jnp.bfloat16, jnp.float32, jnp.int32
ROWS, D, FF, DE, HEADS = 512, 768, 3072, 512, 12
PLANE, STRIPS, STRIP_POS, SEG = 16, 8, 529, 128
OUT_ROWS = STRIPS * STRIP_POS
WINDOW = 272
EPS = 1e-06
MASKED = -1e9
H_VEC, H_QKV, H_OUT, H_UP, H_DOWN, H_EMBED = 0, 1, 10, 13, 25, 37
GROUPS = ((0, 2), (2, 3))
SUM_GROUPS = ((0, 1), (1, 1), (2, 3))
ORDERS = ("xyz", "yzx", "zxy")
V_BE, V_MASK = 12, 13
L_QKV, L_OUT, L_UP, L_DOWN, L_EMBED = 256, 2560, 3328, 6400, 9472


def dot(a, b):
    return jnp.dot(a, b, preferred_element_type=F32)


def dot_t(a, b):
    return lax.dot_general(a, b, (((1,), (1,)), ((), ())), preferred_element_type=F32)


def tdot(a, b):
    return lax.dot_general(a, b, (((0,), (0,)), ((), ())), preferred_element_type=F32)


def iota(shape, dim):
    return lax.broadcasted_iota(I32, shape, dim)


def hot(mask):
    return jnp.where(mask, 1.0, 0.0).astype(BF)


def spread_hot(each, first):
    row, col = iota((D, 256), 0), iota((D, 256), 1) + first
    owner = (col * 10923) >> 16 if each == 6 else col >> 2
    return hot(row == 6 * owner)


class Place:
    def __init__(self):
        self.dp = lax.axis_index("dp")
        self.fs = lax.axis_index("fsdp")
        self.z, self.c = self.dp // 2, self.dp % 2
        self.y, self.x = self.fs // 4, self.fs % 4
        self.own = {"x": self.x, "y": self.y, "z": self.z}

    def near(self, axis, step):
        at = dict(self.own)
        at[axis] = (at[axis] + step) % 4
        return (at["z"] * 2 + self.c, at["y"] * 4 + at["x"])

    def sibling(self):
        return (self.z * 2 + 1 - self.c, self.fs)

    def plane(self, step):
        return (self.dp, (self.fs + step) % PLANE)


def announce(place):
    barrier = pltpu.get_barrier_semaphore()
    others = [place.near("z", s) for s in (1, 2, 3)] + [place.sibling()]
    others += [place.plane(t) for t in range(1, PLANE)]
    for other in others:
        pl.semaphore_signal(barrier, inc=1, device_id=other, device_id_type=MESH)
    return len(others)


class Links:
    def __init__(self, send_sem, recv_sem):
        self.send_sem, self.recv_sem = send_sem, recv_sem
        self.used = 0
        self.started = []

    def make(self, src, dst, index, device):
        return pltpu.make_async_remote_copy(
            src_ref=src,
            dst_ref=dst,
            send_sem=self.send_sem.at[index],
            recv_sem=self.recv_sem.at[index],
            device_id=device,
            device_id_type=MESH,
        )

    def send(self, src, dst, device):
        index = self.used
        self.used += 1
        copy = self.make(src, dst, index, device)
        copy.start()
        self.started.append(copy)
        return index

    def arrive(self, dst, index, device):
        self.make(dst, dst, index, device).wait_recv()

    def drain(self, count=None):
        count = len(self.started) if count is None else count
        for copy in self.started[:count]:
            copy.wait_send()
        self.started = self.started[count:]


def region(ks, coords, core, rows):
    ys = slice(None) if coords["y"] is None else coords["y"]
    zs = slice(None) if coords["z"] is None else coords["z"]
    xs = (
        slice(None)
        if coords["x"] is None
        else pl.ds(pl.multiple_of(coords["x"] * 128, 128), 128)
    )
    return (pl.ds(ks[0], ks[1]), ys, zs, core, rows, xs)


def rows_of(part, half=None):
    return pl.ds(32 * part, 32) if half is None else pl.ds(32 * part + 16 * half, 16)


def free(own, order, count):
    return {a: (None if a in order[:count] else own[a]) for a in "xyz"}


class Spread:
    def __init__(self, place, links, g, ks):
        self.p, self.l, self.g, self.ks = place, links, g, ks

    def at(self, coords, part, half=None, core=None):
        core = self.p.c if core is None else core
        return self.g.at[region(self.ks, coords, core, rows_of(part, half))]

    def send(self, coords, part, half, device):
        view = self.at(coords, part, half)
        return self.l.send(view, view, device)

    def direct(self, phase):
        sent = []
        for part, order in enumerate(ORDERS):
            coords = free(self.p.own, order, phase)
            axis = order[phase]
            for step in (1, 3, 2):
                index = self.send(coords, part, None, self.p.near(axis, step))
                sent.append((part, coords, axis, step, index))
        return sent

    def direct_arrive(self, sent):
        for part, coords, axis, step, index in sent:
            source = dict(coords, **{axis: (self.p.own[axis] + 4 - step) % 4})
            self.l.arrive(self.at(source, part), index, self.p.near(axis, 4 - step))

    def one(self):
        self.sent1 = self.direct(0)

    def two(self):
        self.direct_arrive(self.sent1)
        self.sent2 = self.direct(1)

    def three(self):
        self.direct_arrive(self.sent2)
        self.sib = []
        self.sent3 = []
        for part, order in enumerate(ORDERS):
            axis, base = order[2], free(self.p.own, order, 2)
            up = self.send(base, part, None, self.p.near(axis, 1))
            down = self.send(base, part, None, self.p.near(axis, 3))
            self.sent3.append((up, down))
        for part, order in enumerate(ORDERS):
            self.share(free(self.p.own, order, 2), part, None)

    def share(self, coords, part, half):
        index = self.send(coords, part, half, self.p.sibling())
        self.sib.append((coords, part, half, index))

    def four(self):
        self.sent4 = []
        for part, order in enumerate(ORDERS):
            axis, base = order[2], free(self.p.own, order, 2)
            up, down = self.sent3[part]
            own = self.p.own[axis]
            below = dict(base, **{axis: (own + 3) % 4})
            above = dict(base, **{axis: (own + 1) % 4})
            self.l.arrive(self.at(below, part), up, self.p.near(axis, 3))
            go_up = self.send(below, part, 0, self.p.near(axis, 1))
            self.l.arrive(self.at(above, part), down, self.p.near(axis, 1))
            go_down = self.send(above, part, 1, self.p.near(axis, 3))
            self.sent4.append((go_up, go_down))
            self.share(below, part, None)
            self.share(above, part, None)

    def five(self):
        for part, order in enumerate(ORDERS):
            axis, base = order[2], free(self.p.own, order, 2)
            go_up, go_down = self.sent4[part]
            far = dict(base, **{axis: (self.p.own[axis] + 2) % 4})
            self.l.arrive(self.at(far, part, 0), go_up, self.p.near(axis, 3))
            self.share(far, part, 0)
            self.l.arrive(self.at(far, part, 1), go_down, self.p.near(axis, 1))
            self.share(far, part, 1)

    def six(self):
        for coords, part, half, index in self.sib:
            self.l.arrive(
                self.at(coords, part, half, 1 - self.p.c), index, self.p.sibling()
            )


class Gather:
    def __init__(self, place, links, g, ks, bufs):
        self.p, self.l, self.g, self.ks = place, links, g, ks
        self.core_first = 0
        self.core_buf, self.half_bufs, self.full_bufs, self.two_bufs, self.one_bufs = bufs

    def at(self, coords, part, half=None):
        return self.g.at[region(self.ks, coords, self.p.c, rows_of(part, half))]

    def k(self):
        return pl.ds(self.ks[0], self.ks[1])

    def core_at(self):
        return self.core_buf.at[pl.ds(self.core_first, self.ks[1])]

    def add(self, coords, start, count, reads):
        xs = (
            slice(None)
            if coords["x"] is None
            else pl.ds(pl.multiple_of(coords["x"] * 128, 128), 128)
        )

        def body(k, _):
            for y in range(4) if coords["y"] is None else (coords["y"],):
                for z in range(4) if coords["z"] is None else (coords["z"],):
                    place = (k, y, z, self.p.c, pl.ds(start, count), xs)
                    total = self.g[place].astype(F32)
                    for read in reads:
                        total = total + read(k, y, z).astype(F32)
                    self.g[place] = total.astype(BF)
            return 0

        lax.fori_loop(self.ks[0], self.ks[0] + self.ks[1], body, 0)

    @staticmethod
    def reader(buf, coords, slot):
        def read(k, y, z):
            index = (slot, k)
            index += (y,) if coords["y"] is None else ()
            index += (z,) if coords["z"] is None else ()
            return buf[index]

        return read

    def core_reader(self, rows):
        shift = self.core_first - self.ks[0]
        return lambda k, y, z: self.core_buf[k + shift, y, z, rows]

    def one(self):
        src = self.g.at[self.k(), :, :, 1 - self.p.c]
        self.sent = self.l.send(src, self.core_at(), self.p.sibling())

    def two(self):
        self.l.arrive(self.core_at(), self.sent, self.p.sibling())
        whole = {"x": None, "y": None, "z": None}
        self.sent1 = []
        for part, order in enumerate(ORDERS):
            rows = rows_of(part)
            self.add(whole, 32 * part, 32, [self.core_reader(rows)])
            axis, base = order[2], free(self.p.own, order, 2)
            far = dict(base, **{axis: (self.p.own[axis] + 2) % 4})
            buf = self.half_bufs[part]
            up = self.l.send(self.at(far, part, 0), buf.at[0, self.k()], self.p.near(axis, 1))
            down = self.l.send(self.at(far, part, 1), buf.at[1, self.k()], self.p.near(axis, 3))
            self.sent1.append((up, down))

    def three(self):
        self.sent2 = []
        for part, order in enumerate(ORDERS):
            axis, base = order[2], free(self.p.own, order, 2)
            half, full = self.half_bufs[part], self.full_bufs[part]
            up, down = self.sent1[part]
            above = dict(base, **{axis: (self.p.own[axis] + 1) % 4})
            below = dict(base, **{axis: (self.p.own[axis] + 3) % 4})
            self.l.arrive(half.at[0, self.k()], up, self.p.near(axis, 3))
            self.add(above, 32 * part, 16, [self.reader(half, above, 0)])
            go_up = self.l.send(self.at(above, part), full.at[0, self.k()], self.p.near(axis, 1))
            self.l.arrive(half.at[1, self.k()], down, self.p.near(axis, 1))
            self.add(below, 32 * part + 16, 16, [self.reader(half, below, 1)])
            go_down = self.l.send(
                self.at(below, part), full.at[1, self.k()], self.p.near(axis, 3)
            )
            self.sent2.append((go_up, go_down))

    def direct(self, coords, part, axis, buf):
        sent = []
        for step in (1, 3, 2):
            target = dict(coords, **{axis: (self.p.own[axis] + step) % 4})
            device = self.p.near(axis, step)
            sent.append(
                (step, self.l.send(self.at(target, part), buf.at[step - 1, self.k()], device))
            )
        return sent

    def direct_arrive(self, sent, coords, part, axis, buf):
        for step, index in sent:
            self.l.arrive(buf.at[step - 1, self.k()], index, self.p.near(axis, 4 - step))
        self.add(coords, 32 * part, 32, [self.reader(buf, coords, s) for s in range(3)])

    def four(self):
        self.sent3 = []
        for part, order in enumerate(ORDERS):
            axis, base = order[2], free(self.p.own, order, 2)
            full = self.full_bufs[part]
            up, down = self.sent2[part]
            self.l.arrive(full.at[0, self.k()], up, self.p.near(axis, 3))
            self.l.arrive(full.at[1, self.k()], down, self.p.near(axis, 1))
            self.add(
                base, 32 * part, 32, [self.reader(full, base, 0), self.reader(full, base, 1)]
            )
            coords = free(self.p.own, order, 1)
            self.sent3.append(self.direct(coords, part, order[1], self.two_bufs[part]))

    def five(self):
        self.sent4 = []
        for part, order in enumerate(ORDERS):
            coords = free(self.p.own, order, 1)
            self.direct_arrive(self.sent3[part], coords, part, order[1], self.two_bufs[part])
            self.sent4.append(self.direct(self.p.own, part, order[0], self.one_bufs[part]))

    def six(self):
        for part, order in enumerate(ORDERS):
            self.direct_arrive(
                self.sent4[part], self.p.own, part, order[0], self.one_bufs[part]
            )


def reduce_bufs():
    half = [(2, 5, 4, 16, 512), (2, 5, 4, 4, 16, 128), (2, 5, 4, 16, 512)]
    full = [(2, 5, 4, 32, 512), (2, 5, 4, 4, 32, 128), (2, 5, 4, 32, 512)]
    two = [(3, 5, 32, 512), (3, 5, 4, 32, 128), (3, 5, 4, 32, 128)]
    one = [(3, 5, 32, 128)] * 3
    return [(3, 4, 4, 96, 512)] + half + full + two + one


def mean_rows(v):
    return jnp.mean(v, -1, keepdims=True)


def hat_of(v):
    center = v - mean_rows(v)
    factor = lax.rsqrt(mean_rows(center * center) + EPS)
    return center * factor, factor


def norm_back(dy, gain, hat, factor):
    scaled = dy * gain
    return factor * (scaled - mean_rows(scaled) - hat * mean_rows(scaled * hat))


def col_sum(v):
    return jnp.sum(v, 0, keepdims=True)


SCRATCH = {
    "g": ((5, 4, 4, 2, 96, 512), BF),
    "rb": ((PLANE, 32, 128), BF),
    "fin_send": ((PLANE, 32, 128), BF),
    "fin_recv": ((32, 2048), BF),
    "lanes": ((16, 10240), BF),
    "shard": ((32, 2048), BF),
    "up16": ((16, FF), BF),
    "meta": ((8, 128), I32),
    "strip": ((STRIPS + 1, SEG, DE), BF),
    "meta_all": ((PLANE, 8, 128), I32),
    "n1": ((ROWS, D), BF),
    "qkv": ((ROWS, 3 * D), BF),
    "prob": ((2 * HEADS, 256, 256), BF),
    "ctx": ((ROWS, D), BF),
    "h1": ((ROWS, D), F32),
    "n2": ((ROWS, D), BF),
    "act": ((ROWS, FF), BF),
    "slope": ((ROWS, FF), BF),
    "hb": ((ROWS, D), BF),
    "low": ((ROWS, D), BF),
    "emb": ((ROWS, DE), BF),
    "wide": ((ROWS, D), F32),
    "acc": ((ROWS, D), F32),
    "vec": ((16, D), F32),
    "vgrad": ((16, D), F32),
    "bqkv": ((8, 3 * D), F32),
    "bup": ((8, FF), F32),
    "dec": ((OUT_ROWS, DE), BF),
    "slots": ((PLANE, SEG, DE), BF),
}
N_SEM = 260


def kernel(
    w_qkv, w_out, w_up, w_down, w_embed, vectors, skipped, lengths, route, x_ref, cot,
    patch_out, fin, perms, vec_out, cot_from, cot_to, emb_from, emb_to, *refs
):
    s = dict(zip(SCRATCH, refs))
    rest = refs[len(SCRATCH):]
    bufs, (send_sem, recv_sem, local_sem, core_free) = rest[:13], rest[13:]
    bufs = (bufs[0], bufs[1:4], bufs[4:7], bufs[7:10], bufs[10:13])
    g = s["g"]
    place = Place()
    links = Links(send_sem, recv_sem)

    def weight(h):
        tile = h // 2
        lanes = pl.ds(pl.multiple_of((h % 2) * 256, 256), 256)
        return g[tile // 4, tile % 4, :, :, :, lanes].reshape(D, 256)

    def put_grad(h, value):
        tile = h // 2
        lanes = pl.ds(pl.multiple_of((h % 2) * 256, 256), 256)
        g[tile // 4, tile % 4, :, :, :, lanes] = value.astype(BF).reshape(4, 2, 96, 256)

    def cols(i, width=256):
        return pl.ds(pl.multiple_of(i * width, width), width)

    cot_load = pltpu.make_async_copy(cot, s["dec"], local_sem.at[0])
    cot_load.start()
    callers = announce(place)
    meta = s["meta"]
    meta[...] = jnp.zeros_like(meta)
    meta[0:4, :] = skipped[...]
    for b in range(2):
        meta[4:5, 4 * b : 4 * b + 4] = lengths[b : b + 1, :]
    lanes = s["lanes"]
    lanes[...] = jnp.zeros_like(lanes)
    lanes[0:1, 0:128] = vectors[...]
    lanes[0:6, L_QKV:L_OUT] = w_qkv[...]
    lanes[0:6, L_OUT:L_UP] = w_out[...]
    for q in range(4):
        lanes[0:6, L_DOWN + D * q : L_DOWN + D * q + D] = w_down[6 * q : 6 * q + 6, :]
    lanes[0:6, L_EMBED : L_EMBED + DE] = w_embed[...]
    s["up16"][...] = jnp.zeros_like(s["up16"])
    s["up16"][0:6, :] = w_up[...]
    lane = iota((D, 128), 1)
    row = iota((D, 128), 0)
    for n in range(6):
        col = lane + 128 * n
        device = (col * 10923) >> 16
        start = min(24 * (128 * n // 6) // 128 * 128, FF - D)
        target = 24 * device + (col - 6 * device) - start
        for q in range(4):
            part = dot(s["up16"][:, start : start + D], hot(row == target + 6 * q))
            at = L_UP + D * q + 128 * n
            lanes[:, at : at + 128] = part.astype(BF)
    row, col = iota((32, 16), 0), iota((32, 16), 1)
    for i in range(4):
        packed = jnp.zeros((32, 512), F32)
        for k in range(5):
            first = 2048 * k + 512 * i
            pick = hot((row == col + 6 * k) & (col < 6))
            packed = packed + dot(pick, lanes[:, first : first + 512])
        s["shard"][:, 512 * i : 512 * i + 512] = packed.astype(BF)
    shard = s["shard"]
    rb, meta_all = s["rb"], s["meta_all"]
    pl.semaphore_wait(pltpu.get_barrier_semaphore(), callers)
    meta_sent = []
    for t in range(1, PLANE):
        meta_sent.append(links.send(meta, meta_all.at[t], place.plane(t)))
    sent = []
    for t in range(1, PLANE):
        to = place.plane(t)
        sent.append(links.send(shard.at[:, cols(to[1], 128)], rb.at[place.fs], to))
    rb[place.fs] = shard[:, cols(place.fs, 128)]
    meta_all[0] = meta[...]
    for t in range(1, PLANE):
        source = place.plane(PLANE - t)
        links.arrive(rb.at[source[1]], sent[t - 1], source)
    arrived = rb[...].reshape(PLANE * 32, 128)
    row, col = iota((96, PLANE * 32), 0), iota((96, PLANE * 32), 1)
    sender = (row * 43) >> 8
    target = sender * 32 + (row - sender * 6)
    own_lanes = pl.ds(pl.multiple_of(place.x * 128, 128), 128)
    for k in range(5):
        block = dot(hot(col == target + 6 * k), arrived).astype(BF)
        g[k, place.y, place.z, place.c, :, own_lanes] = block

    spreads = [Spread(place, links, g, ks) for ks in GROUPS]
    first, later = spreads
    first.one()
    later.one()
    first.two()
    later.two()
    first.three()
    later.three()

    for t in range(1, PLANE):
        links.arrive(meta_all.at[t], meta_sent[t - 1], place.plane(PLANE - t))
    cot_load.wait()

    def lens_of(m, blk):
        lens = [m[4:5, blk * 4 + j : blk * 4 + j + 1].astype(F32) for j in range(4)]
        starts = [jnp.zeros_like(lens[0])]
        for j in range(3):
            starts.append(starts[j] + lens[j])
        return lens, starts

    total = jnp.zeros((1, DE), F32)
    for k in range(STRIPS):
        m = meta_all[route[0, k]]
        blk, j = k // 4, k % 4
        lens, starts = lens_of(m, blk)
        skip = jnp.concatenate([m[2 * blk : 2 * blk + 1], m[2 * blk + 1 : 2 * blk + 2]], 1)
        skip = jnp.broadcast_to(skip.astype(F32), (8, 256)).astype(BF)
        r, t = iota((256, SEG), 0).astype(F32), iota((256, SEG), 1).astype(F32)
        local = dot(skip, hot(r - starts[j] == t))
        tri = hot(iota((SEG, SEG), 0) <= iota((SEG, SEG), 1))
        through = dot(local.astype(BF), tri)[0:1]
        off = (STRIP_POS * k) % 16
        base = STRIP_POS * k - off
        lane = iota((WINDOW, SEG), 1).astype(F32)
        spot = iota((WINDOW, SEG), 0).astype(F32)
        perm = hot((spot == lane + through + float(off)) & (lane < lens[j]))
        perms[k] = perm
        picked = tdot(perm, s["dec"][base : base + WINDOW])
        s["strip"][k] = picked.astype(BF)
        total = total - col_sum(picked)

    def sum_rows(i, acc):
        part = s["dec"][pl.ds(pl.multiple_of(i * 16, 16), 16), :].astype(F32)
        return acc + part

    summed = lax.fori_loop(0, OUT_ROWS // 16, sum_rows, jnp.zeros((16, DE), F32))
    total = total + col_sum(summed) + col_sum(s["dec"][OUT_ROWS - 8 :, :].astype(F32))
    s["vgrad"][...] = jnp.zeros_like(s["vgrad"])
    s["vgrad"][V_MASK : V_MASK + 1, 0:DE] = total

    s["strip"][STRIPS] = jnp.zeros((SEG, DE), BF)
    for t in range(PLANE):
        s["slots"][t] = s["strip"][route[1, (PLANE - t) % PLANE]]
    slot_store = pltpu.make_async_copy(s["slots"], cot_from, local_sem.at[0])
    slot_store.start()
    own_store = pltpu.make_async_copy(s["slots"].at[0], cot_to.at[0], local_sem.at[1])
    own_store.start()

    slot_store.wait()
    own_store.wait()
    cot_sent, cot_copies = [], []

    def send_cot(begin, end):
        for t in range(begin, end):
            slot = cot_to.at[PLANE - t]
            cot_sent.append(links.send(cot_from.at[t], slot, place.plane(t)))
            cot_copies.append(links.started.pop())

    first.four()
    first.five()
    first.six()

    chunk = g[0, 0, :, :, :, 0:128].reshape(D, 128)
    table = s["acc"]

    def spread_six(i, _):
        table[0:128, cols(i)] = tdot(chunk, spread_hot(6, 256 * i))
        return 0

    def spread_four(i, _):
        table[128:256, cols(i)] = tdot(chunk, spread_hot(4, 256 * i))
        return 0

    lax.fori_loop(0, 3, spread_six, 0)
    lax.fori_loop(0, 2, spread_four, 0)
    lane6 = iota((16, D), 1)
    lane6 = lane6 - 6 * ((lane6 * 10923) >> 16)
    row6 = iota((16, D), 0)
    for v in range(12):
        low = (6 * v) // 8 * 8
        window = table[low : low + 16, :]
        s["vec"][v : v + 1] = col_sum(jnp.where(row6 + (low - 6 * v) == lane6, window, 0.0))
    lane4, row4 = iota((8, DE), 1) & 3, iota((8, DE), 0)
    few = table[128 + 72 : 128 + 80, 0:DE]
    for i, v in enumerate((V_BE, V_MASK)):
        s["vec"][v : v + 1, 0:DE] = col_sum(jnp.where(row4 - 4 * i == lane4, few, 0.0))
    vec = s["vec"]
    s["bqkv"][...] = jnp.zeros_like(s["bqkv"])
    s["bqkv"][0:1, 0:D] = vec[4:5]
    s["bqkv"][0:1, 2 * D :] = vec[5:6]
    for q in range(4):
        s["bup"][0:1, q * D : (q + 1) * D] = vec[8 + q : 9 + q]

    def norm_one(i, _):
        rows = cols(i, 128)
        hat, _f = hat_of(x_ref[rows, :].astype(F32))
        s["n1"][rows, :] = (hat * vec[0:1] + vec[1:2]).astype(BF)
        return 0

    lax.fori_loop(0, 4, norm_one, 0)

    def qkv_tile(t, _):
        for i in range(2):
            rows = cols(i)
            out = dot(s["n1"][rows, :], weight(H_QKV + t)) + s["bqkv"][0:1, cols(t)]
            s["qkv"][rows, cols(t)] = out.astype(BF)
        return 0

    later.four()
    lax.fori_loop(0, 4, qkv_tile, 0)
    later.five()
    send_cot(1, PLANE)
    lax.fori_loop(4, 9, qkv_tile, 0)

    lens_own = [lens_of(meta[...], b) for b in range(2)]

    def doc_bias(starts):
        r, c = iota((256, 256), 0).astype(F32), iota((256, 256), 1).astype(F32)
        doc_r, doc_c = jnp.zeros_like(r), jnp.zeros_like(c)
        for j in range(1, 4):
            doc_r = doc_r + jnp.where(r >= starts[j], 1.0, 0.0)
            doc_c = doc_c + jnp.where(c >= starts[j], 1.0, 0.0)
        return doc_r == doc_c

    lane = iota((256, 128), 1)
    for blk in range(2):
        rows = slice(256 * blk, 256 * blk + 256)
        same = doc_bias(lens_own[blk][1])

        def heads(hp, _):
            q2 = s["qkv"][rows, cols(hp, 128)] * jnp.asarray(0.125, BF)
            k2 = s["qkv"][rows, cols(6 + hp, 128)]
            v2 = s["qkv"][rows, cols(12 + hp, 128)]
            outs = []
            for h in range(2):
                mine = (lane >= 64) if h else (lane < 64)
                scores = dot_t(jnp.where(mine, q2, jnp.zeros_like(q2)), k2)
                scores = jnp.where(same, scores, MASKED)
                e = jnp.exp(scores - jnp.max(scores, -1, keepdims=True))
                p = (e * (1.0 / jnp.sum(e, -1, keepdims=True))).astype(BF)
                s["prob"][12 * blk + 2 * hp + h] = p
                outs.append(dot(p, v2))
            s["ctx"][rows, cols(hp, 128)] = jnp.where(lane < 64, outs[0], outs[1]).astype(BF)
            return 0

        lax.fori_loop(0, 6, heads, 0)
    later.six()
    links.drain()
    links.started = cot_copies

    def out_tile(t, _):
        out = dot(s["ctx"][...], weight(H_OUT + t)) + vec[6:7, cols(t)]
        s["h1"][:, cols(t)] = x_ref[:, cols(t)].astype(F32) + out
        return 0

    lax.fori_loop(0, 3, out_tile, 0)

    def norm_two(i, _):
        rows = cols(i, 128)
        hat, _f = hat_of(s["h1"][rows, :])
        s["n2"][rows, :] = (hat * vec[2:3] + vec[3:4]).astype(BF)
        return 0

    lax.fori_loop(0, 4, norm_two, 0)

    def up_tile(t, _):
        for i in range(2):
            rows = cols(i)
            u = dot(s["n2"][rows, :], weight(H_UP + t)) + s["bup"][0:1, cols(t)]
            phi = 0.5 * (1.0 + lax.erf(u * 0.7071067811865476))
            density = jnp.exp(-0.5 * u * u) * 0.3989422804014327
            s["act"][rows, cols(t)] = (u * phi).astype(BF)
            s["slope"][rows, cols(t)] = (phi + u * density).astype(BF)
        return 0

    lax.fori_loop(0, 12, up_tile, 0)
    for t in range(3):
        for i in range(2):
            rows = cols(i)
            out = s["h1"][rows, cols(t)] + vec[7:8, cols(t)]
            for q in range(4):
                out = out + dot(s["act"][rows, cols(q, D)], weight(H_DOWN + 3 * q + t))
            s["hb"][rows, cols(t)] = out.astype(BF)
    for t in range(2):
        out = dot(s["hb"][...], weight(H_EMBED + t)) + vec[V_BE : V_BE + 1, cols(t)]
        s["emb"][:, cols(t)] = out.astype(BF)

    def strip_hot(blk):
        lens, starts = lens_own[blk]
        picks = []
        for j in range(4):
            r, t = iota((256, SEG), 0).astype(F32), iota((256, SEG), 1).astype(F32)
            picks.append(hot((r - starts[j] == t) & (t < lens[j])))
        return jnp.concatenate(picks, 1)

    for blk in range(2):
        moved = tdot(strip_hot(blk), s["emb"][256 * blk : 256 * blk + 256])
        for j in range(4):
            s["strip"][4 * blk + j] = moved[SEG * j : SEG * j + SEG].astype(BF)
    for t in range(PLANE):
        s["slots"][t] = s["strip"][route[1, t]]
    slot_store = pltpu.make_async_copy(s["slots"], emb_from, local_sem.at[0])
    slot_store.start()
    own_store = pltpu.make_async_copy(s["slots"].at[0], emb_to.at[0], local_sem.at[1])
    own_store.start()
    slot_store.wait()
    own_store.wait()
    emb_sent = []

    def send_emb(first, last):
        for t in range(first, last):
            emb_sent.append(links.send(emb_from.at[t], emb_to.at[t], place.plane(t)))

    send_emb(1, PLANE)

    for t in range(1, PLANE):
        links.arrive(cot_to.at[PLANE - t], cot_sent[t - 1], place.plane(PLANE - t))
    de = s["emb"]
    cot_back = pltpu.make_async_copy(cot_to, s["slots"], local_sem.at[0])
    cot_back.start()
    cot_back.wait()
    for blk in range(2):
        got = [s["slots"][route[0, 4 * blk + j]] for j in range(4)]
        moved = dot(strip_hot(blk), jnp.concatenate(got, 0))
        de[256 * blk : 256 * blk + 256] = moved.astype(BF)
    vg = s["vgrad"]
    vg[V_BE : V_BE + 1, 0:DE] = col_sum(de[...].astype(F32))
    wide = s["wide"]

    def embed_back(i, acc):
        rows = cols(i)
        dh = dot_t(de[rows, 0:256], weight(H_EMBED)) + dot_t(de[rows, 256:], weight(H_EMBED + 1))
        wide[rows, :] = dh
        s["low"][rows, :] = dh.astype(BF)
        return acc + col_sum(dh)

    vg[7:8] = lax.fori_loop(0, 2, embed_back, jnp.zeros((1, D), F32))
    for t in range(2):
        put_grad(H_EMBED + t, tdot(s["hb"][...], de[:, cols(t)]))

    def down_part(q, _):

        def rows_part(i, acc):
            rows = cols(i)
            da = dot_t(s["low"][rows, 0:256], weight(H_DOWN + 3 * q))
            for t in range(1, 3):
                da = da + dot_t(s["low"][rows, cols(t)], weight(H_DOWN + 3 * q + t))
            du = (da * s["slope"][rows, cols(q, D)].astype(F32)).astype(BF)
            s["slope"][rows, cols(q, D)] = du
            return acc + col_sum(du.astype(F32))

        vg[pl.ds(8 + q, 1), :] = lax.fori_loop(0, 2, rows_part, jnp.zeros((1, D), F32))
        a = s["act"][:, cols(q, D)]
        for t in range(3):
            put_grad(H_DOWN + 3 * q + t, tdot(a, s["low"][:, cols(t)]))
        return 0

    lax.fori_loop(0, 4, down_part, 0)
    acc = s["acc"]

    def up_part(q, _):
        def rows_part(i, _):
            rows = cols(i)
            total = dot_t(s["slope"][rows, cols(3 * q)], weight(H_UP + 3 * q))
            for t in range(1, 3):
                total = total + dot_t(s["slope"][rows, cols(3 * q + t)], weight(H_UP + 3 * q + t))
            acc[rows, :] = jnp.where(q == 0, total, acc[rows, :] + total)
            return 0

        lax.fori_loop(0, 2, rows_part, 0)
        for t in range(3):
            put_grad(H_UP + 3 * q + t, tdot(s["n2"][...], s["slope"][:, cols(3 * q + t)]))
        return 0

    lax.fori_loop(0, 4, up_part, 0)

    def norm_two_back(i, sums):
        rows = cols(i, 128)
        hat, factor = hat_of(s["h1"][rows, :])
        dn = acc[rows, :]
        dh = wide[rows, :] + norm_back(dn, vec[2:3], hat, factor)
        wide[rows, :] = dh
        s["low"][rows, :] = dh.astype(BF)
        return (sums[0] + col_sum(dn * hat), sums[1] + col_sum(dn), sums[2] + col_sum(dh))

    zero = jnp.zeros((1, D), F32)
    vg[2:3], vg[3:4], vg[6:7] = lax.fori_loop(0, 4, norm_two_back, (zero, zero, zero))

    g_first, g_mid, g_later = [Gather(place, links, g, ks, bufs) for ks in SUM_GROUPS]
    g_mid.core_first = 1
    g_later.one()

    def out_back(i, _):
        rows = cols(i)
        total = dot_t(s["low"][rows, 0:256], weight(H_OUT))
        for t in range(1, 3):
            total = total + dot_t(s["low"][rows, cols(t)], weight(H_OUT + t))
        s["hb"][rows, :] = total.astype(BF)
        return 0

    lax.fori_loop(0, 2, out_back, 0)
    for t in range(3):
        put_grad(H_OUT + t, tdot(s["ctx"][...], s["low"][:, cols(t)]))

    for blk in range(2):
        rows = slice(256 * blk, 256 * blk + 256)

        def heads_back(hp, _):
            q2 = s["qkv"][rows, cols(hp, 128)]
            k2 = s["qkv"][rows, cols(6 + hp, 128)]
            v2 = s["qkv"][rows, cols(12 + hp, 128)]
            do2 = s["hb"][rows, cols(hp, 128)]
            dq, dk, dv = [], [], []
            for h in range(2):
                mine = (lane >= 64) if h else (lane < 64)
                p = s["prob"][12 * blk + 2 * hp + h]
                dp = dot_t(jnp.where(mine, do2, jnp.zeros_like(do2)), v2)
                pf = p.astype(F32)
                inner = jnp.sum(pf * dp, -1, keepdims=True)
                ds = (pf * (dp - inner)).astype(BF)
                dq.append(dot(ds, k2))
                dk.append(tdot(ds, q2))
                dv.append(tdot(p, do2))
            lo = lane < 64
            s["qkv"][rows, cols(hp, 128)] = (jnp.where(lo, dq[0], dq[1]) * 0.125).astype(BF)
            s["qkv"][rows, cols(6 + hp, 128)] = (jnp.where(lo, dk[0], dk[1]) * 0.125).astype(BF)
            s["qkv"][rows, cols(12 + hp, 128)] = jnp.where(lo, dv[0], dv[1]).astype(BF)
            return 0

        lax.fori_loop(0, 6, heads_back, 0, unroll=2)
        if blk == 0:
            g_later.two()
            sibling = place.sibling()
            pl.semaphore_signal(core_free, inc=1, device_id=sibling, device_id_type=MESH)
        else:
            g_later.three()

    def bias_sums(i, sums):
        rows = cols(i, 64)
        q = s["qkv"][rows, 0:D].astype(F32)
        v = s["qkv"][rows, 2 * D :].astype(F32)
        return (sums[0] + col_sum(q), sums[1] + col_sum(v))

    vg[4:5], vg[5:6] = lax.fori_loop(0, 8, bias_sums, (zero, zero))

    def qkv_part(q, _):
        def rows_part(i, _):
            rows = cols(i)
            total = dot_t(s["qkv"][rows, cols(3 * q)], weight(H_QKV + 3 * q))
            for t in range(1, 3):
                total = total + dot_t(s["qkv"][rows, cols(3 * q + t)], weight(H_QKV + 3 * q + t))
            acc[rows, :] = jnp.where(q == 2, total, acc[rows, :] + total)
            return 0

        lax.fori_loop(0, 2, rows_part, 0)
        for t in range(3):
            put_grad(H_QKV + 3 * q + t, tdot(s["n1"][...], s["qkv"][:, cols(3 * q + t)]))
        return 0

    qkv_part(2, 0)
    pl.semaphore_wait(core_free, 1)
    g_mid.one()
    g_later.four()
    lax.fori_loop(0, 2, qkv_part, 0)
    g_mid.two()

    def norm_one_back(i, sums):
        rows = cols(i, 128)
        hat, factor = hat_of(x_ref[rows, :].astype(F32))
        dn = acc[rows, :]
        wide[rows, :] = wide[rows, :] + norm_back(dn, vec[0:1], hat, factor)
        return (sums[0] + col_sum(dn * hat), sums[1] + col_sum(dn))

    vg[0:1], vg[1:2] = lax.fori_loop(0, 4, norm_one_back, (zero, zero))
    patch_store = pltpu.make_async_copy(wide, patch_out, local_sem.at[1])
    patch_store.start()

    table[0:256, :] = jnp.zeros((256, D), F32)
    lane6 = iota((8, D), 1)
    lane6 = lane6 - 6 * ((lane6 * 10923) >> 16)
    row6 = iota((8, D), 0)
    for a in range(9):
        rows = jnp.zeros((8, D), F32)
        for v in range(12):
            if 6 * v < 8 * a + 8 and 6 * v + 6 > 8 * a:
                rows = jnp.where(row6 + (8 * a - 6 * v) == lane6, vg[v : v + 1], rows)
        table[8 * a : 8 * a + 8, :] = rows
    rows = jnp.zeros((8, DE), F32)
    for i, v in enumerate((V_BE, V_MASK)):
        rows = jnp.where(row4 - 4 * i == lane4, vg[v : v + 1, 0:DE], rows)
    table[128 + 72 : 128 + 80, 0:DE] = rows

    def fold_six(i, total):
        return total + dot_t(spread_hot(6, 256 * i), table[0:128, cols(i)].astype(BF))

    def fold_four(i, total):
        return total + dot_t(spread_hot(4, 256 * i), table[128:256, cols(i)].astype(BF))

    chunk = lax.fori_loop(0, 3, fold_six, jnp.zeros((D, 128), F32))
    chunk = lax.fori_loop(0, 2, fold_four, chunk)
    g[0, 0, :, :, :, 0:128] = chunk.astype(BF).reshape(4, 2, 96, 128)

    g_first.one()
    vec_out[...] = vec[V_MASK : V_MASK + 1, :]
    g_later.five()
    g_mid.three()
    g_first.two()
    g_later.six()
    g_mid.four()
    g_first.three()
    g_mid.five()
    g_first.four()
    g_mid.six()
    g_first.five()
    g_first.six()
    row, col = iota((PLANE * 32, 96), 0), iota((PLANE * 32, 96), 1)
    inner_row = row & 31
    base_row = 6 * (row >> 5)
    slots = jnp.zeros((PLANE * 32, 128), F32)
    for k in range(5):
        j = inner_row - 6 * k
        pick = hot((col == base_row + j) & (j >= 0) & (j < 6))
        slots = slots + dot(pick, g[k, place.y, place.z, place.c, :, own_lanes])
    s["fin_send"][...] = slots.astype(BF).reshape(PLANE, 32, 128)
    fin_sent = []
    for t in range(1, PLANE):
        to = place.plane(t)
        slot = s["fin_recv"].at[:, cols(place.fs, 128)]
        fin_sent.append(links.send(s["fin_send"].at[to[1]], slot, to))
    s["fin_recv"][:, cols(place.fs, 128)] = s["fin_send"][place.fs]
    for t in range(1, PLANE):
        source = place.plane(PLANE - t)
        links.arrive(s["fin_recv"].at[:, cols(source[1], 128)], fin_sent[t - 1], source)
    fin[...] = s["fin_recv"][...]
    for t in range(1, PLANE):
        links.arrive(emb_to.at[t], emb_sent[t - 1], place.plane(PLANE - t))
    links.drain()
    patch_store.wait()


def mega(w_qkv, w_out, w_up, w_down, w_embed, vectors, skipped, lengths, route, x, cot):
    dma = pltpu.SemaphoreType.DMA
    vmem = pl.BlockSpec(memory_space=pltpu.VMEM)
    smem = pl.BlockSpec(memory_space=pltpu.SMEM)
    hbm = pl.BlockSpec(memory_space=pl.ANY)
    return pl.pallas_call(
        kernel,
        out_shape=(
            jax.ShapeDtypeStruct((ROWS, D), F32),
            jax.ShapeDtypeStruct((32, 2048), BF),
            jax.ShapeDtypeStruct((STRIPS, WINDOW, SEG), BF),
            jax.ShapeDtypeStruct((1, D), F32),
        )
        + (jax.ShapeDtypeStruct((PLANE, SEG, DE), BF),) * 4,
        in_specs=[vmem] * 8 + [smem, vmem, hbm],
        out_specs=(hbm, vmem, vmem, vmem) + (hbm,) * 4,
        scratch_shapes=[pltpu.VMEM(shape, kind) for shape, kind in SCRATCH.values()]
        + [pltpu.VMEM(shape, BF) for shape in reduce_bufs()]
        + [dma((N_SEM,)), dma((N_SEM,)), dma((2,))]
        + [pltpu.SemaphoreType.REGULAR],
        compiler_params=pltpu.CompilerParams(
            collective_id=1, has_side_effects=True, vmem_limit_bytes=64 * 1024 * 1024
        ),
        name="layer",
    )(w_qkv, w_out, w_up, w_down, w_embed, vectors, skipped, lengths, route, x, cot)


VECTOR_AT = (0, 6, 12, 18, 24, 30, 36, 48, 42, 72, 76)
VECTOR_SIZE = (6, 6, 6, 6, 6, 6, 6, 24, 6, 4, 4)


def finish_kernel(route, patch, fin, perms, mask, emb, dec_out, patch_out, g_qkv, g_out, g_up,
                  g_down, g_embed, *rest):
    vectors, (dec, wide, strips, rows, sems) = rest[:11], rest[11:]
    loads = []
    for k in range(STRIPS):
        source = emb.at[route[0, k]]
        loads.append(pltpu.make_async_copy(source, strips.at[k], sems.at[2 + k]))
        loads[-1].start()
    patch_load = pltpu.make_async_copy(patch, rows, sems.at[0])
    patch_load.start()
    token = mask[0:1, 0:DE]
    blank = jnp.broadcast_to(token.astype(BF), (64, DE))

    def fill(i, _):
        dec[pl.ds(pl.multiple_of(i * 64, 64), 64), :] = blank
        return 0

    lax.fori_loop(0, OUT_ROWS // 64, fill, 0)
    dec[OUT_ROWS - 8 :, :] = blank[0:8]
    for k in range(STRIPS):
        perm = perms[k]
        base = STRIP_POS * k - (STRIP_POS * k) % 16
        filled = dot(perm, jnp.ones((SEG, 128), BF))[:, 0:1]
        loads[k].wait()
        placed = dot(perm, strips[k])
        dec[base : base + WINDOW] = jnp.where(filled > 0.5, placed, token).astype(BF)
    dec_store = pltpu.make_async_copy(dec, dec_out, sems.at[1])
    dec_store.start()
    patch_load.wait()
    patch_store = pltpu.make_async_copy(rows, patch_out, sems.at[0])
    patch_store.start()
    row, col = iota((8, 32), 0), iota((8, 32), 1)
    for k in range(5):
        pick = hot((col == row + 6 * k) & (row < 6))
        wide[:, 2048 * k : 2048 * k + 2048] = dot(pick, fin[...])
    g_qkv[...] = wide[0:6, L_QKV:L_OUT]
    g_out[...] = wide[0:6, L_OUT:L_UP]
    for q in range(4):
        g_down[6 * q : 6 * q + 6, :] = wide[0:6, L_DOWN + D * q : L_DOWN + D * q + D]
    g_embed[...] = wide[0:6, L_EMBED : L_EMBED + DE]
    col = iota((256, 384), 1)
    device = (col * 2731) >> 16
    inner = col - 24 * device
    part = (inner * 43) >> 8
    source = 6 * device + (inner - 6 * part)
    row = iota((256, 384), 0)
    for shift in range(4):
        pick = [hot((part == q) & (row == source + (96 * shift) % 128)) for q in range(4)]
        for m in (shift, shift + 4):
            start = L_UP + (96 * m) // 128 * 128
            total = jnp.zeros((8, 384), F32)
            for q in range(4):
                window = wide[:, start + D * q : start + D * q + 256].astype(BF)
                total = total + dot(window, pick[q])
            g_up[:, 384 * m : 384 * m + 384] = total[0:6]
    for ref, at, size in zip(vectors, VECTOR_AT, VECTOR_SIZE):
        ref[...] = wide[0, at : at + size]
    patch_store.wait()
    dec_store.wait()


def finish(route, patch, fin, perms, mask, emb):
    vmem = pl.BlockSpec(memory_space=pltpu.VMEM)
    hbm = pl.BlockSpec(memory_space=pl.ANY)
    shape = jax.ShapeDtypeStruct
    return pl.pallas_call(
        finish_kernel,
        out_shape=(shape((OUT_ROWS, DE), BF), shape((ROWS, D), F32))
        + tuple(shape(s, F32) for s in ((6, 3 * D), (6, D), (6, FF), (24, D), (6, DE)))
        + tuple(shape((n,), F32) for n in VECTOR_SIZE),
        in_specs=[pl.BlockSpec(memory_space=pltpu.SMEM), hbm, vmem, vmem, vmem, hbm],
        out_specs=(hbm, hbm) + (vmem,) * 16,
        scratch_shapes=[
            pltpu.VMEM((OUT_ROWS, DE), BF),
            pltpu.VMEM((8, 10240), F32),
            pltpu.VMEM((STRIPS, SEG, DE), BF),
            pltpu.VMEM((ROWS, D), F32),
            pltpu.SemaphoreType.DMA((2 + STRIPS,)),
        ],
        compiler_params=pltpu.CompilerParams(vmem_limit_bytes=64 * 1024 * 1024),
        name="finish",
    )(route, patch, fin, perms, mask, emb)


def on_device(patches, lengths, skipped, strip_order, decoder_grad, qkv_weight, out_weight,
              up_weight, down_weight, embed_weight, gain_one, shift_one, gain_two, shift_two,
              bias_query, bias_value, bias_out, bias_up, bias_down, bias_embed, mask_token):
    pieces = (gain_one, shift_one, gain_two, shift_two, bias_query, bias_value, bias_out,
              bias_down, bias_up, bias_embed, mask_token)
    vectors, at = None, 0
    for piece in pieces:
        size = piece.shape[0]
        padded = jnp.pad(piece, (at, 128 - at - size))
        vectors = padded if vectors is None else vectors + padded
        at += size
    strip = lax.broadcasted_iota(I32, (PLANE, STRIPS), 1)
    place = lax.broadcasted_iota(I32, (PLANE, STRIPS), 0)
    match = (strip_order[0, None, 0:STRIPS] == place).astype(I32)
    inverse = STRIPS + jnp.sum(match * (strip - STRIPS), 1)
    route = jnp.stack([strip_order[0], inverse])
    patch_grad, fin, perms, mask, _, _, _, emb = mega(
        qkv_weight, out_weight, up_weight, down_weight, embed_weight, vectors[None],
        skipped.reshape(4, 128), lengths, route, patches, decoder_grad,
    )
    return tuple(finish(route, patch_grad, fin, perms, mask, emb))


def solution(mesh):
    both = ("dp", "fsdp")
    rows, vector = P(both, None), P(both)
    return jax.shard_map(
        on_device,
        mesh=mesh,
        in_specs=(rows, rows, rows, P("dp", None), rows) + (rows,) * 5 + (vector,) * 11,
        out_specs=(rows,) * 7 + (vector,) * 11,
        check_vma=False,
    )
```

```python
import functools

import jax
import jax.numpy as jnp
from jax import lax
from jax.experimental import pallas as pl
from jax.experimental.pallas import tpu as pltpu
from jax.sharding import PartitionSpec as P

MESH = pl.DeviceIdType.MESH
BF, F32, I32 = jnp.bfloat16, jnp.float32, jnp.int32
ROWS, D, FF, DE, HEADS = 512, 768, 3072, 512, 12
PLANE, STRIPS, STRIP_POS, SEG = 16, 8, 529, 128
OUT_ROWS = STRIPS * STRIP_POS
WINDOW = 272
EPS = 1e-06
MASKED = -1e9
H_VEC, H_QKV, H_OUT, H_UP, H_DOWN, H_EMBED = 0, 1, 10, 13, 25, 37
GROUPS = ((0, 2), (2, 3))
SUM_GROUPS = ((0, 1), (1, 1), (2, 3))
ORDERS = ("xyz", "yzx", "zxy")
V_BE, V_MASK = 12, 13
L_QKV, L_OUT, L_UP, L_DOWN, L_EMBED = 256, 2560, 3328, 6400, 9472


def dot(a, b):
    return jnp.dot(a, b, preferred_element_type=F32)


def dot_t(a, b):
    return lax.dot_general(a, b, (((1,), (1,)), ((), ())), preferred_element_type=F32)


def tdot(a, b):
    return lax.dot_general(a, b, (((0,), (0,)), ((), ())), preferred_element_type=F32)


def iota(shape, dim):
    return lax.broadcasted_iota(I32, shape, dim)


def hot(mask):
    return jnp.where(mask, 1.0, 0.0).astype(BF)


def spread_hot(each, first):
    row, col = iota((D, 256), 0), iota((D, 256), 1) + first
    owner = (col * 10923) >> 16 if each == 6 else col >> 2
    return hot(row == 6 * owner)


class Place:
    def __init__(self):
        self.dp = lax.axis_index("dp")
        self.fs = lax.axis_index("fsdp")
        self.z, self.c = self.dp // 2, self.dp % 2
        self.y, self.x = self.fs // 4, self.fs % 4
        self.own = {"x": self.x, "y": self.y, "z": self.z}

    def near(self, axis, step):
        at = dict(self.own)
        at[axis] = (at[axis] + step) % 4
        return (at["z"] * 2 + self.c, at["y"] * 4 + at["x"])

    def sibling(self):
        return (self.z * 2 + 1 - self.c, self.fs)

    def plane(self, step):
        return (self.dp, (self.fs + step) % PLANE)


def announce(place):
    barrier = pltpu.get_barrier_semaphore()
    others = [place.near("z", s) for s in (1, 2, 3)] + [place.sibling()]
    others += [place.plane(t) for t in range(1, PLANE)]
    for other in others:
        pl.semaphore_signal(barrier, inc=1, device_id=other, device_id_type=MESH)
    return len(others)


class Links:
    def __init__(self, send_sem, recv_sem):
        self.send_sem, self.recv_sem = send_sem, recv_sem
        self.used = 0
        self.started = []

    def make(self, src, dst, index, device):
        return pltpu.make_async_remote_copy(
            src_ref=src,
            dst_ref=dst,
            send_sem=self.send_sem.at[index],
            recv_sem=self.recv_sem.at[index],
            device_id=device,
            device_id_type=MESH,
        )

    def send(self, src, dst, device):
        index = self.used
        self.used += 1
        copy = self.make(src, dst, index, device)
        copy.start()
        self.started.append(copy)
        return index

    def arrive(self, dst, index, device):
        self.make(dst, dst, index, device).wait_recv()

    def drain(self, count=None):
        count = len(self.started) if count is None else count
        for copy in self.started[:count]:
            copy.wait_send()
        self.started = self.started[count:]


def region(ks, coords, core, rows):
    ys = slice(None) if coords["y"] is None else coords["y"]
    zs = slice(None) if coords["z"] is None else coords["z"]
    xs = (
        slice(None)
        if coords["x"] is None
        else pl.ds(pl.multiple_of(coords["x"] * 128, 128), 128)
    )
    return (pl.ds(ks[0], ks[1]), ys, zs, core, rows, xs)


def rows_of(part, half=None):
    return pl.ds(32 * part, 32) if half is None else pl.ds(32 * part + 16 * half, 16)


def free(own, order, count):
    return {a: (None if a in order[:count] else own[a]) for a in "xyz"}


class Spread:
    def __init__(self, place, links, g, ks):
        self.p, self.l, self.g, self.ks = place, links, g, ks

    def at(self, coords, part, half=None, core=None):
        core = self.p.c if core is None else core
        return self.g.at[region(self.ks, coords, core, rows_of(part, half))]

    def send(self, coords, part, half, device):
        view = self.at(coords, part, half)
        return self.l.send(view, view, device)

    def direct(self, phase):
        sent = []
        for part, order in enumerate(ORDERS):
            coords = free(self.p.own, order, phase)
            axis = order[phase]
            for step in (1, 3, 2):
                index = self.send(coords, part, None, self.p.near(axis, step))
                sent.append((part, coords, axis, step, index))
        return sent

    def direct_arrive(self, sent):
        for part, coords, axis, step, index in sent:
            source = dict(coords, **{axis: (self.p.own[axis] + 4 - step) % 4})
            self.l.arrive(self.at(source, part), index, self.p.near(axis, 4 - step))

    def one(self):
        self.sent1 = self.direct(0)

    def two(self):
        self.direct_arrive(self.sent1)
        self.sent2 = self.direct(1)

    def three(self):
        self.direct_arrive(self.sent2)
        self.sib = []
        self.sent3 = []
        for part, order in enumerate(ORDERS):
            axis, base = order[2], free(self.p.own, order, 2)
            up = self.send(base, part, None, self.p.near(axis, 1))
            down = self.send(base, part, None, self.p.near(axis, 3))
            self.sent3.append((up, down))
        for part, order in enumerate(ORDERS):
            self.share(free(self.p.own, order, 2), part, None)

    def share(self, coords, part, half):
        index = self.send(coords, part, half, self.p.sibling())
        self.sib.append((coords, part, half, index))

    def four(self):
        self.sent4 = []
        for part, order in enumerate(ORDERS):
            axis, base = order[2], free(self.p.own, order, 2)
            up, down = self.sent3[part]
            own = self.p.own[axis]
            below = dict(base, **{axis: (own + 3) % 4})
            above = dict(base, **{axis: (own + 1) % 4})
            self.l.arrive(self.at(below, part), up, self.p.near(axis, 3))
            go_up = self.send(below, part, 0, self.p.near(axis, 1))
            self.l.arrive(self.at(above, part), down, self.p.near(axis, 1))
            go_down = self.send(above, part, 1, self.p.near(axis, 3))
            self.sent4.append((go_up, go_down))
            self.share(below, part, None)
            self.share(above, part, None)

    def five(self):
        for part, order in enumerate(ORDERS):
            axis, base = order[2], free(self.p.own, order, 2)
            go_up, go_down = self.sent4[part]
            far = dict(base, **{axis: (self.p.own[axis] + 2) % 4})
            self.l.arrive(self.at(far, part, 0), go_up, self.p.near(axis, 3))
            self.share(far, part, 0)
            self.l.arrive(self.at(far, part, 1), go_down, self.p.near(axis, 1))
            self.share(far, part, 1)

    def six(self):
        for coords, part, half, index in self.sib:
            self.l.arrive(
                self.at(coords, part, half, 1 - self.p.c), index, self.p.sibling()
            )


class Gather:
    def __init__(self, place, links, g, ks, bufs):
        self.p, self.l, self.g, self.ks = place, links, g, ks
        self.core_first = 0
        self.core_buf, self.half_bufs, self.full_bufs, self.two_bufs, self.one_bufs = bufs

    def at(self, coords, part, half=None):
        return self.g.at[region(self.ks, coords, self.p.c, rows_of(part, half))]

    def k(self):
        return pl.ds(self.ks[0], self.ks[1])

    def core_at(self):
        return self.core_buf.at[pl.ds(self.core_first, self.ks[1])]

    def add(self, coords, start, count, reads):
        xs = (
            slice(None)
            if coords["x"] is None
            else pl.ds(pl.multiple_of(coords["x"] * 128, 128), 128)
        )

        def body(k, _):
            for y in range(4) if coords["y"] is None else (coords["y"],):
                for z in range(4) if coords["z"] is None else (coords["z"],):
                    place = (k, y, z, self.p.c, pl.ds(start, count), xs)
                    if len(reads) == 1:
                        self.g[place] = self.g[place] + reads[0](k, y, z)
                        continue
                    total = self.g[place].astype(F32)
                    for read in reads:
                        total = total + read(k, y, z).astype(F32)
                    self.g[place] = total.astype(BF)
            return 0

        lax.fori_loop(self.ks[0], self.ks[0] + self.ks[1], body, 0)

    @staticmethod
    def reader(buf, coords, slot):
        def read(k, y, z):
            index = (slot, k)
            index += (y,) if coords["y"] is None else ()
            index += (z,) if coords["z"] is None else ()
            return buf[index]

        return read

    def core_reader(self, rows):
        shift = self.core_first - self.ks[0]
        return lambda k, y, z: self.core_buf[k + shift, y, z, rows]

    def one(self):
        src = self.g.at[self.k(), :, :, 1 - self.p.c]
        self.sent = self.l.send(src, self.core_at(), self.p.sibling())

    def two(self):
        self.l.arrive(self.core_at(), self.sent, self.p.sibling())
        whole = {"x": None, "y": None, "z": None}
        self.sent1 = []
        for part, order in enumerate(ORDERS):
            rows = rows_of(part)
            self.add(whole, 32 * part, 32, [self.core_reader(rows)])
            axis, base = order[2], free(self.p.own, order, 2)
            far = dict(base, **{axis: (self.p.own[axis] + 2) % 4})
            buf = self.half_bufs[part]
            up = self.l.send(self.at(far, part, 0), buf.at[0, self.k()], self.p.near(axis, 1))
            down = self.l.send(self.at(far, part, 1), buf.at[1, self.k()], self.p.near(axis, 3))
            self.sent1.append((up, down))

    def three(self):
        self.sent2 = []
        for part, order in enumerate(ORDERS):
            axis, base = order[2], free(self.p.own, order, 2)
            half, full = self.half_bufs[part], self.full_bufs[part]
            up, down = self.sent1[part]
            above = dict(base, **{axis: (self.p.own[axis] + 1) % 4})
            below = dict(base, **{axis: (self.p.own[axis] + 3) % 4})
            self.l.arrive(half.at[0, self.k()], up, self.p.near(axis, 3))
            self.add(above, 32 * part, 16, [self.reader(half, above, 0)])
            go_up = self.l.send(self.at(above, part), full.at[0, self.k()], self.p.near(axis, 1))
            self.l.arrive(half.at[1, self.k()], down, self.p.near(axis, 1))
            self.add(below, 32 * part + 16, 16, [self.reader(half, below, 1)])
            go_down = self.l.send(
                self.at(below, part), full.at[1, self.k()], self.p.near(axis, 3)
            )
            self.sent2.append((go_up, go_down))

    def direct(self, coords, part, axis, buf):
        sent = []
        for step in (1, 3, 2):
            target = dict(coords, **{axis: (self.p.own[axis] + step) % 4})
            device = self.p.near(axis, step)
            sent.append(
                (step, self.l.send(self.at(target, part), buf.at[step - 1, self.k()], device))
            )
        return sent

    def direct_arrive(self, sent, coords, part, axis, buf):
        for step, index in sent:
            self.l.arrive(buf.at[step - 1, self.k()], index, self.p.near(axis, 4 - step))
        self.add(coords, 32 * part, 32, [self.reader(buf, coords, s) for s in range(3)])

    def four(self):
        self.sent3 = []
        for part, order in enumerate(ORDERS):
            axis, base = order[2], free(self.p.own, order, 2)
            full = self.full_bufs[part]
            up, down = self.sent2[part]
            self.l.arrive(full.at[0, self.k()], up, self.p.near(axis, 3))
            self.l.arrive(full.at[1, self.k()], down, self.p.near(axis, 1))
            self.add(
                base, 32 * part, 32, [self.reader(full, base, 0), self.reader(full, base, 1)]
            )
            coords = free(self.p.own, order, 1)
            self.sent3.append(self.direct(coords, part, order[1], self.two_bufs[part]))

    def five(self):
        self.sent4 = []
        for part, order in enumerate(ORDERS):
            coords = free(self.p.own, order, 1)
            self.direct_arrive(self.sent3[part], coords, part, order[1], self.two_bufs[part])
            self.sent4.append(self.direct(self.p.own, part, order[0], self.one_bufs[part]))

    def six(self):
        for part, order in enumerate(ORDERS):
            self.direct_arrive(
                self.sent4[part], self.p.own, part, order[0], self.one_bufs[part]
            )


def reduce_bufs():
    half = [(2, 5, 4, 16, 512), (2, 5, 4, 4, 16, 128), (2, 5, 4, 16, 512)]
    full = [(2, 5, 4, 32, 512), (2, 5, 4, 4, 32, 128), (2, 5, 4, 32, 512)]
    two = [(3, 5, 32, 512), (3, 5, 4, 32, 128), (3, 5, 4, 32, 128)]
    one = [(3, 5, 32, 128)] * 3
    return [(3, 4, 4, 96, 512)] + half + full + two + one


def mean_rows(v):
    return jnp.mean(v, -1, keepdims=True)


def hat_of(v):
    center = v - mean_rows(v)
    factor = lax.rsqrt(mean_rows(center * center) + EPS)
    return center * factor, factor


def norm_back(dy, gain, hat, factor):
    scaled = dy * gain
    return factor * (scaled - mean_rows(scaled) - hat * mean_rows(scaled * hat))


def col_sum(v):
    return jnp.sum(v, 0, keepdims=True)


SCRATCH = {
    "g": ((5, 4, 4, 2, 96, 512), BF),
    "rb": ((PLANE, 32, 128), BF),
    "fin_send": ((PLANE, 32, 128), BF),
    "fin_recv": ((32, 2048), BF),
    "lanes": ((16, 10240), BF),
    "shard": ((32, 2048), BF),
    "up16": ((16, FF), BF),
    "meta": ((8, 128), I32),
    "strip": ((STRIPS + 1, SEG, DE), BF),
    "meta_all": ((PLANE, 8, 128), I32),
    "n1": ((ROWS, D), BF),
    "qkv": ((ROWS, 3 * D), BF),
    "prob": ((2 * HEADS, 256, 256), BF),
    "ctx": ((ROWS, D), BF),
    "h1": ((ROWS, D), F32),
    "n2": ((ROWS, D), BF),
    "act": ((ROWS, FF), BF),
    "slope": ((ROWS, FF), BF),
    "hb": ((ROWS, D), BF),
    "low": ((ROWS, D), BF),
    "emb": ((ROWS, DE), BF),
    "wide": ((ROWS, D), F32),
    "acc": ((ROWS, D), F32),
    "vec": ((16, D), F32),
    "vgrad": ((16, D), F32),
    "bqkv": ((8, 3 * D), F32),
    "bup": ((8, FF), F32),
    "dec": ((OUT_ROWS, DE), BF),
    "slots": ((PLANE, SEG, DE), BF),
}
FLIPPED = {"hb": 0, "ctx": D, "act": 2 * D, "n1": 2560, "n2": 2560 + D}
N_SEM = 260


def kernel(
    w_qkv, w_out, w_up, w_down, w_embed, vectors, skipped, lengths, route, x_ref, cot,
    patch_out, fin, perms, vec_out, cot_from, cot_to, emb_from, emb_to, *refs
):
    s = dict(zip(SCRATCH, refs))
    rest = refs[len(SCRATCH):]
    bufs, (send_sem, recv_sem, local_sem, core_free) = rest[:13], rest[13:]
    bufs = (bufs[0], bufs[1:4], bufs[4:7], bufs[7:10], bufs[10:13])
    g = s["g"]
    place = Place()
    links = Links(send_sem, recv_sem)

    def weight(h):
        tile = h // 2
        lanes = pl.ds(pl.multiple_of((h % 2) * 256, 256), 256)
        return g[tile // 4, tile % 4, :, :, :, lanes].reshape(D, 256)

    def put_grad(h, value):
        tile = h // 2
        lanes = pl.ds(pl.multiple_of((h % 2) * 256, 256), 256)
        g[tile // 4, tile % 4, :, :, :, lanes] = value.astype(BF).reshape(4, 2, 96, 256)

    def cols(i, width=256):
        return pl.ds(pl.multiple_of(i * width, width), width)

    cot_load = pltpu.make_async_copy(cot, s["dec"], local_sem.at[0])
    cot_load.start()
    callers = announce(place)
    meta = s["meta"]
    meta[...] = jnp.zeros_like(meta)
    meta[0:4, :] = skipped[...]
    for b in range(2):
        meta[4:5, 4 * b : 4 * b + 4] = lengths[b : b + 1, :]
    lanes = s["lanes"]
    lanes[...] = jnp.zeros_like(lanes)
    lanes[0:1, 0:128] = vectors[...]
    lanes[0:6, L_QKV:L_OUT] = w_qkv[...]
    lanes[0:6, L_OUT:L_UP] = w_out[...]
    for q in range(4):
        lanes[0:6, L_DOWN + D * q : L_DOWN + D * q + D] = w_down[6 * q : 6 * q + 6, :]
    lanes[0:6, L_EMBED : L_EMBED + DE] = w_embed[...]
    s["up16"][...] = jnp.zeros_like(s["up16"])
    s["up16"][0:6, :] = w_up[...]
    lane = iota((D, 128), 1)
    row = iota((D, 128), 0)
    for n in range(6):
        col = lane + 128 * n
        device = (col * 10923) >> 16
        start = min(24 * (128 * n // 6) // 128 * 128, FF - D)
        target = 24 * device + (col - 6 * device) - start
        for q in range(4):
            part = dot(s["up16"][:, start : start + D], hot(row == target + 6 * q))
            at = L_UP + D * q + 128 * n
            lanes[:, at : at + 128] = part.astype(BF)
    row, col = iota((32, 16), 0), iota((32, 16), 1)
    for i in range(4):
        packed = jnp.zeros((32, 512), F32)
        for k in range(5):
            first = 2048 * k + 512 * i
            pick = hot((row == col + 6 * k) & (col < 6))
            packed = packed + dot(pick, lanes[:, first : first + 512])
        s["shard"][:, 512 * i : 512 * i + 512] = packed.astype(BF)
    shard = s["shard"]
    rb, meta_all = s["rb"], s["meta_all"]
    pl.semaphore_wait(pltpu.get_barrier_semaphore(), callers)
    meta_sent = []
    for t in range(1, PLANE):
        meta_sent.append(links.send(meta, meta_all.at[t], place.plane(t)))
    sent = []
    for t in range(1, PLANE):
        to = place.plane(t)
        sent.append(links.send(shard.at[:, cols(to[1], 128)], rb.at[place.fs], to))
    rb[place.fs] = shard[:, cols(place.fs, 128)]
    meta_all[0] = meta[...]
    for t in range(1, PLANE):
        source = place.plane(PLANE - t)
        links.arrive(rb.at[source[1]], sent[t - 1], source)
    arrived = rb[...].reshape(PLANE * 32, 128)
    row, col = iota((96, PLANE * 32), 0), iota((96, PLANE * 32), 1)
    sender = (row * 43) >> 8
    target = sender * 32 + (row - sender * 6)
    own_lanes = pl.ds(pl.multiple_of(place.x * 128, 128), 128)
    for k in range(5):
        block = dot(hot(col == target + 6 * k), arrived).astype(BF)
        g[k, place.y, place.z, place.c, :, own_lanes] = block

    spreads = [Spread(place, links, g, ks) for ks in GROUPS]
    first, later = spreads
    first.one()
    later.one()
    first.two()
    later.two()
    first.three()
    later.three()

    for t in range(1, PLANE):
        links.arrive(meta_all.at[t], meta_sent[t - 1], place.plane(PLANE - t))
    cot_load.wait()

    def lens_of(m, blk):
        lens = [m[4:5, blk * 4 + j : blk * 4 + j + 1].astype(F32) for j in range(4)]
        starts = [jnp.zeros_like(lens[0])]
        for j in range(3):
            starts.append(starts[j] + lens[j])
        return lens, starts

    total = jnp.zeros((1, DE), F32)
    for k in range(STRIPS):
        m = meta_all[route[0, k]]
        blk, j = k // 4, k % 4
        lens, starts = lens_of(m, blk)
        skip = jnp.concatenate([m[2 * blk : 2 * blk + 1], m[2 * blk + 1 : 2 * blk + 2]], 1)
        skip = jnp.broadcast_to(skip.astype(F32), (8, 256)).astype(BF)
        r, t = iota((256, SEG), 0).astype(F32), iota((256, SEG), 1).astype(F32)
        local = dot(skip, hot(r - starts[j] == t))
        tri = hot(iota((SEG, SEG), 0) <= iota((SEG, SEG), 1))
        through = dot(local.astype(BF), tri)[0:1]
        off = (STRIP_POS * k) % 16
        base = STRIP_POS * k - off
        lane = iota((WINDOW, SEG), 1).astype(F32)
        spot = iota((WINDOW, SEG), 0).astype(F32)
        perm = hot((spot == lane + through + float(off)) & (lane < lens[j]))
        perms[k] = perm
        picked = tdot(perm, s["dec"][base : base + WINDOW])
        s["strip"][k] = picked.astype(BF)
        total = total - col_sum(picked)

    def sum_rows(i, acc):
        part = s["dec"][pl.ds(pl.multiple_of(i * 16, 16), 16), :].astype(F32)
        return acc + part

    summed = lax.fori_loop(0, OUT_ROWS // 16, sum_rows, jnp.zeros((16, DE), F32))
    total = total + col_sum(summed) + col_sum(s["dec"][OUT_ROWS - 8 :, :].astype(F32))
    s["vgrad"][...] = jnp.zeros_like(s["vgrad"])
    s["vgrad"][V_MASK : V_MASK + 1, 0:DE] = total

    s["strip"][STRIPS] = jnp.zeros((SEG, DE), BF)
    for t in range(PLANE):
        s["slots"][t] = s["strip"][route[1, (PLANE - t) % PLANE]]
    slot_store = pltpu.make_async_copy(s["slots"], cot_from, local_sem.at[0])
    slot_store.start()
    own_store = pltpu.make_async_copy(s["slots"].at[0], cot_to.at[0], local_sem.at[1])
    own_store.start()

    slot_store.wait()
    own_store.wait()
    cot_sent, cot_copies = [], []

    def send_cot(begin, end):
        for t in range(begin, end):
            slot = cot_to.at[PLANE - t]
            cot_sent.append(links.send(cot_from.at[t], slot, place.plane(t)))
            cot_copies.append(links.started.pop())

    first.four()
    later.four()
    first.five()
    later.five()
    first.six()
    later.six()
    links.drain()
    send_cot(1, PLANE)
    links.started = cot_copies

    chunk = g[0, 0, :, :, :, 0:128].reshape(D, 128)
    table = s["acc"]

    def spread_six(i, _):
        table[0:128, cols(i)] = tdot(chunk, spread_hot(6, 256 * i))
        return 0

    def spread_four(i, _):
        table[128:256, cols(i)] = tdot(chunk, spread_hot(4, 256 * i))
        return 0

    lax.fori_loop(0, 3, spread_six, 0)
    lax.fori_loop(0, 2, spread_four, 0)
    lane6 = iota((16, D), 1)
    lane6 = lane6 - 6 * ((lane6 * 10923) >> 16)
    row6 = iota((16, D), 0)
    for v in range(12):
        low = (6 * v) // 8 * 8
        window = table[low : low + 16, :]
        s["vec"][v : v + 1] = col_sum(jnp.where(row6 + (low - 6 * v) == lane6, window, 0.0))
    lane4, row4 = iota((8, DE), 1) & 3, iota((8, DE), 0)
    few = table[128 + 72 : 128 + 80, 0:DE]
    for i, v in enumerate((V_BE, V_MASK)):
        s["vec"][v : v + 1, 0:DE] = col_sum(jnp.where(row4 - 4 * i == lane4, few, 0.0))
    vec = s["vec"]
    s["bqkv"][...] = jnp.zeros_like(s["bqkv"])
    s["bqkv"][0:1, 0:D] = vec[4:5]
    s["bqkv"][0:1, 2 * D :] = vec[5:6]
    for q in range(4):
        s["bup"][0:1, q * D : (q + 1) * D] = vec[8 + q : 9 + q]

    def norm_one(i, _):
        rows = cols(i, 128)
        hat, _f = hat_of(x_ref[rows, :].astype(F32))
        s["n1"][rows, :] = (hat * vec[0:1] + vec[1:2]).astype(BF)
        return 0

    lax.fori_loop(0, 4, norm_one, 0, unroll=2)

    def qkv_tile(t, _):
        for i in range(2):
            rows = cols(i)
            out = dot(s["n1"][rows, :], weight(H_QKV + t)) + s["bqkv"][0:1, cols(t)]
            s["qkv"][rows, cols(t)] = out.astype(BF)
        return 0

    lax.fori_loop(0, 9, qkv_tile, 0, unroll=3)

    lens_own = [lens_of(meta[...], b) for b in range(2)]

    def doc_bias(starts):
        r, c = iota((256, 256), 0).astype(F32), iota((256, 256), 1).astype(F32)
        doc_r, doc_c = jnp.zeros_like(r), jnp.zeros_like(c)
        for j in range(1, 4):
            doc_r = doc_r + jnp.where(r >= starts[j], 1.0, 0.0)
            doc_c = doc_c + jnp.where(c >= starts[j], 1.0, 0.0)
        return doc_r == doc_c

    lane = iota((256, 128), 1)
    for blk in range(2):
        rows = slice(256 * blk, 256 * blk + 256)
        same = doc_bias(lens_own[blk][1])

        def heads(hp, _):
            q2 = s["qkv"][rows, cols(hp, 128)] * jnp.asarray(0.125, BF)
            k2 = s["qkv"][rows, cols(6 + hp, 128)]
            v2 = s["qkv"][rows, cols(12 + hp, 128)]
            outs = []
            for h in range(2):
                mine = (lane >= 64) if h else (lane < 64)
                scores = dot_t(jnp.where(mine, q2, jnp.zeros_like(q2)), k2)
                scores = jnp.where(same, scores, MASKED)
                e = jnp.exp(scores - jnp.max(scores, -1, keepdims=True))
                p = (e * (1.0 / jnp.sum(e, -1, keepdims=True))).astype(BF)
                s["prob"][12 * blk + 2 * hp + h] = p
                outs.append(dot(p, v2))
            s["ctx"][rows, cols(hp, 128)] = jnp.where(lane < 64, outs[0], outs[1]).astype(BF)
            return 0

        lax.fori_loop(0, 6, heads, 0, unroll=2)

    def out_tile(t, _):
        out = dot(s["ctx"][...], weight(H_OUT + t)) + vec[6:7, cols(t)]
        s["h1"][:, cols(t)] = x_ref[:, cols(t)].astype(F32) + out
        return 0

    lax.fori_loop(0, 3, out_tile, 0, unroll=3)

    def norm_two(i, _):
        rows = cols(i, 128)
        hat, _f = hat_of(s["h1"][rows, :])
        s["n2"][rows, :] = (hat * vec[2:3] + vec[3:4]).astype(BF)
        return 0

    lax.fori_loop(0, 4, norm_two, 0, unroll=2)

    def up_tile(t, _):
        for i in range(2):
            rows = cols(i)
            u = dot(s["n2"][rows, :], weight(H_UP + t)) + s["bup"][0:1, cols(t)]
            phi = 0.5 * (1.0 + lax.erf(u * 0.7071067811865476))
            density = jnp.exp(-0.5 * u * u) * 0.3989422804014327
            s["act"][rows, cols(t)] = (u * phi).astype(BF)
            s["slope"][rows, cols(t)] = (phi + u * density).astype(BF)
        return 0

    lax.fori_loop(0, 12, up_tile, 0, unroll=2)
    for t in range(3):
        for i in range(2):
            rows = cols(i)
            out = s["h1"][rows, cols(t)] + vec[7:8, cols(t)]
            for q in range(4):
                out = out + dot(s["act"][rows, cols(q, D)], weight(H_DOWN + 3 * q + t))
            s["hb"][rows, cols(t)] = out.astype(BF)
    for t in range(2):
        out = dot(s["hb"][...], weight(H_EMBED + t)) + vec[V_BE : V_BE + 1, cols(t)]
        s["emb"][:, cols(t)] = out.astype(BF)

    def strip_hot(blk):
        lens, starts = lens_own[blk]
        picks = []
        for j in range(4):
            r, t = iota((256, SEG), 0).astype(F32), iota((256, SEG), 1).astype(F32)
            picks.append(hot((r - starts[j] == t) & (t < lens[j])))
        return jnp.concatenate(picks, 1)

    for blk in range(2):
        moved = tdot(strip_hot(blk), s["emb"][256 * blk : 256 * blk + 256])
        for j in range(4):
            s["strip"][4 * blk + j] = moved[SEG * j : SEG * j + SEG].astype(BF)
    for t in range(PLANE):
        s["slots"][t] = s["strip"][route[1, t]]
    slot_store = pltpu.make_async_copy(s["slots"], emb_from, local_sem.at[0])
    slot_store.start()
    own_store = pltpu.make_async_copy(s["slots"].at[0], emb_to.at[0], local_sem.at[1])
    own_store.start()
    slot_store.wait()
    own_store.wait()
    emb_sent = []

    def send_emb(first, last):
        for t in range(first, last):
            emb_sent.append(links.send(emb_from.at[t], emb_to.at[t], place.plane(t)))

    send_emb(1, PLANE)

    def flipped(name):
        return s["dec"][FLIPPED[name] : FLIPPED[name] + D, :]

    for name in ("n1", "n2", "ctx", "hb"):

        def flip(i, _, name=name):
            at = pl.ds(pl.multiple_of(FLIPPED[name] + 128 * i, 128), 128)
            s["dec"][at, :] = s[name][:, cols(i, 128)].T
            return 0

        lax.fori_loop(0, 6, flip, 0)

    for t in range(1, PLANE):
        links.arrive(cot_to.at[PLANE - t], cot_sent[t - 1], place.plane(PLANE - t))
    de = s["emb"]
    cot_back = pltpu.make_async_copy(cot_to, s["slots"], local_sem.at[0])
    cot_back.start()
    cot_back.wait()
    for blk in range(2):
        got = [s["slots"][route[0, 4 * blk + j]] for j in range(4)]
        moved = dot(strip_hot(blk), jnp.concatenate(got, 0))
        de[256 * blk : 256 * blk + 256] = moved.astype(BF)
    vg = s["vgrad"]
    vg[V_BE : V_BE + 1, 0:DE] = col_sum(de[...].astype(F32))
    wide = s["wide"]

    def embed_back(i, acc):
        rows = cols(i)
        dh = dot_t(de[rows, 0:256], weight(H_EMBED)) + dot_t(de[rows, 256:], weight(H_EMBED + 1))
        wide[rows, :] = dh
        s["low"][rows, :] = dh.astype(BF)
        return acc + col_sum(dh)

    vg[7:8] = lax.fori_loop(0, 2, embed_back, jnp.zeros((1, D), F32), unroll=2)
    for t in range(2):
        put_grad(H_EMBED + t, dot(flipped("hb"), de[:, cols(t)]))

    def down_part(q, _):

        def rows_part(i, acc):
            rows = cols(i)
            da = dot_t(s["low"][rows, 0:256], weight(H_DOWN + 3 * q))
            for t in range(1, 3):
                da = da + dot_t(s["low"][rows, cols(t)], weight(H_DOWN + 3 * q + t))
            du = (da * s["slope"][rows, cols(q, D)].astype(F32)).astype(BF)
            s["slope"][rows, cols(q, D)] = du
            return acc + col_sum(du.astype(F32))

        vg[pl.ds(8 + q, 1), :] = lax.fori_loop(0, 2, rows_part, jnp.zeros((1, D), F32), unroll=2)
        for i in range(6):
            at = FLIPPED["act"] + 128 * i
            s["dec"][at : at + 128, :] = s["act"][:, cols(6 * q + i, 128)].T
        for t in range(3):
            put_grad(H_DOWN + 3 * q + t, dot(flipped("act"), s["low"][:, cols(t)]))
        return 0

    lax.fori_loop(0, 4, down_part, 0)
    acc = s["acc"]

    def up_part(q, _):
        def rows_part(i, _):
            rows = cols(i)
            total = dot_t(s["slope"][rows, cols(3 * q)], weight(H_UP + 3 * q))
            for t in range(1, 3):
                total = total + dot_t(s["slope"][rows, cols(3 * q + t)], weight(H_UP + 3 * q + t))
            acc[rows, :] = jnp.where(q == 0, total, acc[rows, :] + total)
            return 0

        lax.fori_loop(0, 2, rows_part, 0, unroll=2)
        for t in range(3):
            put_grad(H_UP + 3 * q + t, dot(flipped("n2"), s["slope"][:, cols(3 * q + t)]))
        return 0

    lax.fori_loop(0, 4, up_part, 0)

    def norm_two_back(i, sums):
        rows = cols(i, 128)
        hat, factor = hat_of(s["h1"][rows, :])
        dn = acc[rows, :]
        dh = wide[rows, :] + norm_back(dn, vec[2:3], hat, factor)
        wide[rows, :] = dh
        s["low"][rows, :] = dh.astype(BF)
        return (sums[0] + col_sum(dn * hat), sums[1] + col_sum(dn), sums[2] + col_sum(dh))

    zero = jnp.zeros((1, D), F32)
    vg[2:3], vg[3:4], vg[6:7] = lax.fori_loop(0, 4, norm_two_back, (zero, zero, zero), unroll=2)

    g_first, g_mid, g_later = [Gather(place, links, g, ks, bufs) for ks in SUM_GROUPS]
    g_mid.core_first = 1
    g_later.one()

    def out_back(i, _):
        rows = cols(i)
        total = dot_t(s["low"][rows, 0:256], weight(H_OUT))
        for t in range(1, 3):
            total = total + dot_t(s["low"][rows, cols(t)], weight(H_OUT + t))
        s["hb"][rows, :] = total.astype(BF)
        return 0

    lax.fori_loop(0, 2, out_back, 0, unroll=2)
    for t in range(3):
        put_grad(H_OUT + t, dot(flipped("ctx"), s["low"][:, cols(t)]))

    for blk in range(2):
        rows = slice(256 * blk, 256 * blk + 256)

        def put(chunk, value, blk=blk):
            at = pl.ds(pl.multiple_of(512 * (chunk // 4) + 256 * blk, 256), 256)
            s["dec"][at, cols(chunk % 4, 128)] = value.astype(BF)

        def heads_back(hp, _):
            q2 = s["qkv"][rows, cols(hp, 128)]
            k2 = s["qkv"][rows, cols(6 + hp, 128)]
            v2 = s["qkv"][rows, cols(12 + hp, 128)]
            do2 = s["hb"][rows, cols(hp, 128)]
            dq, dk, dv = [], [], []
            for h in range(2):
                mine = (lane >= 64) if h else (lane < 64)
                p = s["prob"][12 * blk + 2 * hp + h]
                dp = dot_t(jnp.where(mine, do2, jnp.zeros_like(do2)), v2)
                pf = p.astype(F32)
                inner = jnp.sum(pf * dp, -1, keepdims=True)
                ds = (pf * (dp - inner)).astype(BF)
                dq.append(dot(ds, k2))
                dk.append(tdot(ds, q2))
                dv.append(tdot(p, do2))
            lo = lane < 64
            put(hp, jnp.where(lo, dq[0], dq[1]) * 0.125)
            put(6 + hp, jnp.where(lo, dk[0], dk[1]) * 0.125)
            put(12 + hp, jnp.where(lo, dv[0], dv[1]))
            return 0

        lax.fori_loop(0, 6, heads_back, 0, unroll=2)
        if blk == 0:
            g_later.two()
            sibling = place.sibling()
            pl.semaphore_signal(core_free, inc=1, device_id=sibling, device_id_type=MESH)
        else:
            g_later.three()

    def dqkv(t, start=0, size=ROWS):
        rows = pl.ds(pl.multiple_of(512 * (t // 2) + start, 64), size)
        return s["dec"][rows, cols(t % 2)]

    def bias_sums(i, sums):
        q = [dqkv(t, 64 * i, 64).astype(F32) for t in (0, 1, 2)]
        v = [dqkv(t, 64 * i, 64).astype(F32) for t in (6, 7, 8)]
        q, v = [jnp.concatenate(part, 1) for part in (q, v)]
        return (sums[0] + col_sum(q), sums[1] + col_sum(v))

    vg[4:5], vg[5:6] = lax.fori_loop(0, 8, bias_sums, (zero, zero), unroll=2)

    def qkv_part(q, _):
        def rows_part(i, _):
            rows = cols(i)
            total = dot_t(dqkv(3 * q, 256 * i, 256), weight(H_QKV + 3 * q))
            for t in range(1, 3):
                total = total + dot_t(dqkv(3 * q + t, 256 * i, 256), weight(H_QKV + 3 * q + t))
            acc[rows, :] = jnp.where(q == 2, total, acc[rows, :] + total)
            return 0

        lax.fori_loop(0, 2, rows_part, 0, unroll=2)
        for t in range(3):
            put_grad(H_QKV + 3 * q + t, dot(flipped("n1"), dqkv(3 * q + t)))
        return 0

    qkv_part(2, 0)
    pl.semaphore_wait(core_free, 1)
    g_mid.one()
    lax.fori_loop(0, 2, qkv_part, 0)
    g_mid.two()

    def norm_one_back(i, sums):
        rows = cols(i, 128)
        hat, factor = hat_of(x_ref[rows, :].astype(F32))
        dn = acc[rows, :]
        wide[rows, :] = wide[rows, :] + norm_back(dn, vec[0:1], hat, factor)
        return (sums[0] + col_sum(dn * hat), sums[1] + col_sum(dn))

    vg[0:1], vg[1:2] = lax.fori_loop(0, 4, norm_one_back, (zero, zero), unroll=2)
    patch_store = pltpu.make_async_copy(wide, patch_out, local_sem.at[1])
    patch_store.start()

    table[0:256, :] = jnp.zeros((256, D), F32)
    lane6 = iota((8, D), 1)
    lane6 = lane6 - 6 * ((lane6 * 10923) >> 16)
    row6 = iota((8, D), 0)
    for a in range(9):
        rows = jnp.zeros((8, D), F32)
        for v in range(12):
            if 6 * v < 8 * a + 8 and 6 * v + 6 > 8 * a:
                rows = jnp.where(row6 + (8 * a - 6 * v) == lane6, vg[v : v + 1], rows)
        table[8 * a : 8 * a + 8, :] = rows
    rows = jnp.zeros((8, DE), F32)
    for i, v in enumerate((V_BE, V_MASK)):
        rows = jnp.where(row4 - 4 * i == lane4, vg[v : v + 1, 0:DE], rows)
    table[128 + 72 : 128 + 80, 0:DE] = rows

    def fold_six(i, total):
        return total + dot_t(spread_hot(6, 256 * i), table[0:128, cols(i)].astype(BF))

    def fold_four(i, total):
        return total + dot_t(spread_hot(4, 256 * i), table[128:256, cols(i)].astype(BF))

    chunk = lax.fori_loop(0, 3, fold_six, jnp.zeros((D, 128), F32))
    chunk = lax.fori_loop(0, 2, fold_four, chunk)
    g[0, 0, :, :, :, 0:128] = chunk.astype(BF).reshape(4, 2, 96, 128)

    g_first.one()
    vec_out[...] = vec[V_MASK : V_MASK + 1, :]
    g_later.four()
    g_first.two()
    g_mid.three()
    g_later.five()
    g_first.three()
    g_mid.four()
    g_later.six()
    g_first.four()
    g_mid.five()
    g_first.five()
    g_mid.six()
    g_first.six()
    row, col = iota((PLANE * 32, 96), 0), iota((PLANE * 32, 96), 1)
    inner_row = row & 31
    base_row = 6 * (row >> 5)
    slots = jnp.zeros((PLANE * 32, 128), F32)
    for k in range(5):
        j = inner_row - 6 * k
        pick = hot((col == base_row + j) & (j >= 0) & (j < 6))
        slots = slots + dot(pick, g[k, place.y, place.z, place.c, :, own_lanes])
    s["fin_send"][...] = slots.astype(BF).reshape(PLANE, 32, 128)
    fin_sent = []
    for t in range(1, PLANE):
        to = place.plane(t)
        slot = s["fin_recv"].at[:, cols(place.fs, 128)]
        fin_sent.append(links.send(s["fin_send"].at[to[1]], slot, to))
    s["fin_recv"][:, cols(place.fs, 128)] = s["fin_send"][place.fs]
    for t in range(1, PLANE):
        source = place.plane(PLANE - t)
        links.arrive(s["fin_recv"].at[:, cols(source[1], 128)], fin_sent[t - 1], source)
    fin[...] = s["fin_recv"][...]
    for t in range(1, PLANE):
        links.arrive(emb_to.at[t], emb_sent[t - 1], place.plane(PLANE - t))
    links.drain()
    patch_store.wait()


def mega(w_qkv, w_out, w_up, w_down, w_embed, vectors, skipped, lengths, route, x, cot):
    dma = pltpu.SemaphoreType.DMA
    vmem = pl.BlockSpec(memory_space=pltpu.VMEM)
    smem = pl.BlockSpec(memory_space=pltpu.SMEM)
    hbm = pl.BlockSpec(memory_space=pl.ANY)
    return pl.pallas_call(
        kernel,
        out_shape=(
            jax.ShapeDtypeStruct((ROWS, D), F32),
            jax.ShapeDtypeStruct((32, 2048), BF),
            jax.ShapeDtypeStruct((STRIPS, WINDOW, SEG), BF),
            jax.ShapeDtypeStruct((1, D), F32),
        )
        + (jax.ShapeDtypeStruct((PLANE, SEG, DE), BF),) * 4,
        in_specs=[vmem] * 8 + [smem, vmem, hbm],
        out_specs=(hbm, vmem, vmem, vmem) + (hbm,) * 4,
        scratch_shapes=[pltpu.VMEM(shape, kind) for shape, kind in SCRATCH.values()]
        + [pltpu.VMEM(shape, BF) for shape in reduce_bufs()]
        + [dma((N_SEM,)), dma((N_SEM,)), dma((2,))]
        + [pltpu.SemaphoreType.REGULAR],
        compiler_params=pltpu.CompilerParams(
            collective_id=1, has_side_effects=True, vmem_limit_bytes=64 * 1024 * 1024
        ),
        name="layer",
    )(w_qkv, w_out, w_up, w_down, w_embed, vectors, skipped, lengths, route, x, cot)


VECTOR_AT = (0, 6, 12, 18, 24, 30, 36, 48, 42, 72, 76)
VECTOR_SIZE = (6, 6, 6, 6, 6, 6, 6, 24, 6, 4, 4)


def finish_kernel(route, patch, fin, perms, mask, emb, dec_out, patch_out, g_qkv, g_out, g_up,
                  g_down, g_embed, *rest):
    vectors, (dec, wide, strips, rows, sems) = rest[:11], rest[11:]
    loads = []
    for k in range(STRIPS):
        source = emb.at[route[0, k]]
        loads.append(pltpu.make_async_copy(source, strips.at[k], sems.at[2 + k]))
        loads[-1].start()
    patch_load = pltpu.make_async_copy(patch, rows, sems.at[0])
    patch_load.start()
    token = mask[0:1, 0:DE]
    blank = jnp.broadcast_to(token.astype(BF), (64, DE))

    def fill(i, _):
        dec[pl.ds(pl.multiple_of(i * 64, 64), 64), :] = blank
        return 0

    lax.fori_loop(0, OUT_ROWS // 64, fill, 0)
    dec[OUT_ROWS - 8 :, :] = blank[0:8]
    for k in range(STRIPS):
        perm = perms[k]
        base = STRIP_POS * k - (STRIP_POS * k) % 16
        filled = dot(perm, jnp.ones((SEG, 128), BF))[:, 0:1]
        loads[k].wait()
        placed = dot(perm, strips[k])
        dec[base : base + WINDOW] = jnp.where(filled > 0.5, placed, token).astype(BF)
    dec_store = pltpu.make_async_copy(dec, dec_out, sems.at[1])
    dec_store.start()
    patch_load.wait()
    patch_store = pltpu.make_async_copy(rows, patch_out, sems.at[0])
    patch_store.start()
    row, col = iota((8, 32), 0), iota((8, 32), 1)
    for k in range(5):
        pick = hot((col == row + 6 * k) & (row < 6))
        wide[:, 2048 * k : 2048 * k + 2048] = dot(pick, fin[...])
    g_qkv[...] = wide[0:6, L_QKV:L_OUT]
    g_out[...] = wide[0:6, L_OUT:L_UP]
    for q in range(4):
        g_down[6 * q : 6 * q + 6, :] = wide[0:6, L_DOWN + D * q : L_DOWN + D * q + D]
    g_embed[...] = wide[0:6, L_EMBED : L_EMBED + DE]
    col = iota((256, 384), 1)
    device = (col * 2731) >> 16
    inner = col - 24 * device
    part = (inner * 43) >> 8
    source = 6 * device + (inner - 6 * part)
    row = iota((256, 384), 0)
    for shift in range(4):
        pick = [hot((part == q) & (row == source + (96 * shift) % 128)) for q in range(4)]
        for m in (shift, shift + 4):
            start = L_UP + (96 * m) // 128 * 128
            total = jnp.zeros((8, 384), F32)
            for q in range(4):
                window = wide[:, start + D * q : start + D * q + 256].astype(BF)
                total = total + dot(window, pick[q])
            g_up[:, 384 * m : 384 * m + 384] = total[0:6]
    for ref, at, size in zip(vectors, VECTOR_AT, VECTOR_SIZE):
        ref[...] = wide[0, at : at + size]
    patch_store.wait()
    dec_store.wait()


def finish(route, patch, fin, perms, mask, emb):
    vmem = pl.BlockSpec(memory_space=pltpu.VMEM)
    hbm = pl.BlockSpec(memory_space=pl.ANY)
    shape = jax.ShapeDtypeStruct
    return pl.pallas_call(
        finish_kernel,
        out_shape=(shape((OUT_ROWS, DE), BF), shape((ROWS, D), F32))
        + tuple(shape(s, F32) for s in ((6, 3 * D), (6, D), (6, FF), (24, D), (6, DE)))
        + tuple(shape((n,), F32) for n in VECTOR_SIZE),
        in_specs=[pl.BlockSpec(memory_space=pltpu.SMEM), hbm, vmem, vmem, vmem, hbm],
        out_specs=(hbm, hbm) + (vmem,) * 16,
        scratch_shapes=[
            pltpu.VMEM((OUT_ROWS, DE), BF),
            pltpu.VMEM((8, 10240), F32),
            pltpu.VMEM((STRIPS, SEG, DE), BF),
            pltpu.VMEM((ROWS, D), F32),
            pltpu.SemaphoreType.DMA((2 + STRIPS,)),
        ],
        compiler_params=pltpu.CompilerParams(vmem_limit_bytes=64 * 1024 * 1024),
        name="finish",
    )(route, patch, fin, perms, mask, emb)


def on_device(patches, lengths, skipped, strip_order, decoder_grad, qkv_weight, out_weight,
              up_weight, down_weight, embed_weight, gain_one, shift_one, gain_two, shift_two,
              bias_query, bias_value, bias_out, bias_up, bias_down, bias_embed, mask_token):
    pieces = (gain_one, shift_one, gain_two, shift_two, bias_query, bias_value, bias_out,
              bias_down, bias_up, bias_embed, mask_token)
    vectors, at = None, 0
    for piece in pieces:
        size = piece.shape[0]
        padded = jnp.pad(piece, (at, 128 - at - size))
        vectors = padded if vectors is None else vectors + padded
        at += size
    strip = lax.broadcasted_iota(I32, (PLANE, STRIPS), 1)
    place = lax.broadcasted_iota(I32, (PLANE, STRIPS), 0)
    match = (strip_order[0, None, 0:STRIPS] == place).astype(I32)
    inverse = STRIPS + jnp.sum(match * (strip - STRIPS), 1)
    route = jnp.stack([strip_order[0], inverse])
    patch_grad, fin, perms, mask, _, _, _, emb = mega(
        qkv_weight, out_weight, up_weight, down_weight, embed_weight, vectors[None],
        skipped.reshape(4, 128), lengths, route, patches, decoder_grad,
    )
    return tuple(finish(route, patch_grad, fin, perms, mask, emb))


def solution(mesh):
    both = ("dp", "fsdp")
    rows, vector = P(both, None), P(both)
    return jax.shard_map(
        on_device,
        mesh=mesh,
        in_specs=(rows, rows, rows, P("dp", None), rows) + (rows,) * 5 + (vector,) * 11,
        out_specs=(rows,) * 7 + (vector,) * 11,
        check_vma=False,
    )
```

```python
import functools

import jax
import jax.numpy as jnp
from jax import lax
from jax.experimental import pallas as pl
from jax.experimental.pallas import tpu as pltpu
from jax.sharding import PartitionSpec as P

MESH = pl.DeviceIdType.MESH
BF, F32, I32 = jnp.bfloat16, jnp.float32, jnp.int32
ROWS, D, FF, DE, HEADS = 512, 768, 3072, 512, 12
PLANE, STRIPS, STRIP_POS, SEG = 16, 8, 529, 128
OUT_ROWS = STRIPS * STRIP_POS
WINDOW = 272
EPS = 1e-06
MASKED = -1e9
H_VEC, H_QKV, H_OUT, H_UP, H_DOWN, H_EMBED = 0, 1, 10, 13, 25, 37
GROUPS = ((0, 2), (2, 3))
SUM_GROUPS = ((0, 1), (1, 1), (2, 3))
ORDERS = ("xyz", "yzx", "zxy")
V_BE, V_MASK = 12, 13
L_QKV, L_OUT, L_UP, L_DOWN, L_EMBED = 256, 2560, 3328, 6400, 9472


def dot(a, b):
    return jnp.dot(a, b, preferred_element_type=F32)


def dot_t(a, b):
    return lax.dot_general(a, b, (((1,), (1,)), ((), ())), preferred_element_type=F32)


def tdot(a, b):
    return lax.dot_general(a, b, (((0,), (0,)), ((), ())), preferred_element_type=F32)


def iota(shape, dim):
    return lax.broadcasted_iota(I32, shape, dim)


def hot(mask):
    return jnp.where(mask, 1.0, 0.0).astype(BF)


def spread_hot(each, first):
    row, col = iota((D, 256), 0), iota((D, 256), 1) + first
    owner = (col * 10923) >> 16 if each == 6 else col >> 2
    return hot(row == 6 * owner)


class Place:
    def __init__(self):
        self.dp = lax.axis_index("dp")
        self.fs = lax.axis_index("fsdp")
        self.z, self.c = self.dp // 2, self.dp % 2
        self.y, self.x = self.fs // 4, self.fs % 4
        self.own = {"x": self.x, "y": self.y, "z": self.z}

    def near(self, axis, step):
        at = dict(self.own)
        at[axis] = (at[axis] + step) % 4
        return (at["z"] * 2 + self.c, at["y"] * 4 + at["x"])

    def sibling(self):
        return (self.z * 2 + 1 - self.c, self.fs)

    def plane(self, step):
        return (self.dp, (self.fs + step) % PLANE)


def announce(place):
    barrier = pltpu.get_barrier_semaphore()
    others = [place.near("z", s) for s in (1, 2, 3)] + [place.sibling()]
    others += [place.plane(t) for t in range(1, PLANE)]
    for other in others:
        pl.semaphore_signal(barrier, inc=1, device_id=other, device_id_type=MESH)
    return len(others)


class Links:
    def __init__(self, send_sem, recv_sem):
        self.send_sem, self.recv_sem = send_sem, recv_sem
        self.used = 0
        self.started = []

    def make(self, src, dst, index, device):
        return pltpu.make_async_remote_copy(
            src_ref=src,
            dst_ref=dst,
            send_sem=self.send_sem.at[index],
            recv_sem=self.recv_sem.at[index],
            device_id=device,
            device_id_type=MESH,
        )

    def send(self, src, dst, device):
        index = self.used
        self.used += 1
        copy = self.make(src, dst, index, device)
        copy.start()
        self.started.append(copy)
        return index

    def arrive(self, dst, index, device):
        self.make(dst, dst, index, device).wait_recv()

    def drain(self, count=None):
        count = len(self.started) if count is None else count
        for copy in self.started[:count]:
            copy.wait_send()
        self.started = self.started[count:]


def region(ks, coords, core, rows):
    ys = slice(None) if coords["y"] is None else coords["y"]
    zs = slice(None) if coords["z"] is None else coords["z"]
    xs = (
        slice(None)
        if coords["x"] is None
        else pl.ds(pl.multiple_of(coords["x"] * 128, 128), 128)
    )
    return (pl.ds(ks[0], ks[1]), ys, zs, core, rows, xs)


def rows_of(part, half=None):
    return pl.ds(32 * part, 32) if half is None else pl.ds(32 * part + 16 * half, 16)


def free(own, order, count):
    return {a: (None if a in order[:count] else own[a]) for a in "xyz"}


class Spread:
    def __init__(self, place, links, g, ks):
        self.p, self.l, self.g, self.ks = place, links, g, ks

    def at(self, coords, part, half=None, core=None):
        core = self.p.c if core is None else core
        return self.g.at[region(self.ks, coords, core, rows_of(part, half))]

    def send(self, coords, part, half, device):
        view = self.at(coords, part, half)
        return self.l.send(view, view, device)

    def direct(self, phase):
        sent = []
        for part, order in enumerate(ORDERS):
            coords = free(self.p.own, order, phase)
            axis = order[phase]
            for step in (1, 3, 2):
                index = self.send(coords, part, None, self.p.near(axis, step))
                sent.append((part, coords, axis, step, index))
        return sent

    def direct_arrive(self, sent):
        for part, coords, axis, step, index in sent:
            source = dict(coords, **{axis: (self.p.own[axis] + 4 - step) % 4})
            self.l.arrive(self.at(source, part), index, self.p.near(axis, 4 - step))

    def one(self):
        self.sent1 = self.direct(0)

    def two(self):
        self.direct_arrive(self.sent1)
        self.sent2 = self.direct(1)

    def three(self):
        self.direct_arrive(self.sent2)
        self.sib = []
        self.sent3 = []
        for part, order in enumerate(ORDERS):
            axis, base = order[2], free(self.p.own, order, 2)
            up = self.send(base, part, None, self.p.near(axis, 1))
            down = self.send(base, part, None, self.p.near(axis, 3))
            self.sent3.append((up, down))
        for part, order in enumerate(ORDERS):
            self.share(free(self.p.own, order, 2), part, None)

    def share(self, coords, part, half):
        index = self.send(coords, part, half, self.p.sibling())
        self.sib.append((coords, part, half, index))

    def four(self):
        self.sent4 = []
        for part, order in enumerate(ORDERS):
            axis, base = order[2], free(self.p.own, order, 2)
            up, down = self.sent3[part]
            own = self.p.own[axis]
            below = dict(base, **{axis: (own + 3) % 4})
            above = dict(base, **{axis: (own + 1) % 4})
            self.l.arrive(self.at(below, part), up, self.p.near(axis, 3))
            go_up = self.send(below, part, 0, self.p.near(axis, 1))
            self.l.arrive(self.at(above, part), down, self.p.near(axis, 1))
            go_down = self.send(above, part, 1, self.p.near(axis, 3))
            self.sent4.append((go_up, go_down))
            self.share(below, part, None)
            self.share(above, part, None)

    def five(self):
        for part, order in enumerate(ORDERS):
            axis, base = order[2], free(self.p.own, order, 2)
            go_up, go_down = self.sent4[part]
            far = dict(base, **{axis: (self.p.own[axis] + 2) % 4})
            self.l.arrive(self.at(far, part, 0), go_up, self.p.near(axis, 3))
            self.share(far, part, 0)
            self.l.arrive(self.at(far, part, 1), go_down, self.p.near(axis, 1))
            self.share(far, part, 1)

    def six(self):
        for coords, part, half, index in self.sib:
            self.l.arrive(
                self.at(coords, part, half, 1 - self.p.c), index, self.p.sibling()
            )


class Gather:
    def __init__(self, place, links, g, ks, bufs):
        self.p, self.l, self.g, self.ks = place, links, g, ks
        self.core_first = 0
        self.core_buf, self.half_bufs, self.full_bufs, self.two_bufs, self.one_bufs = bufs

    def at(self, coords, part, half=None):
        return self.g.at[region(self.ks, coords, self.p.c, rows_of(part, half))]

    def k(self):
        return pl.ds(self.ks[0], self.ks[1])

    def core_at(self):
        return self.core_buf.at[pl.ds(self.core_first, self.ks[1])]

    def add(self, coords, start, count, reads):
        xs = (
            slice(None)
            if coords["x"] is None
            else pl.ds(pl.multiple_of(coords["x"] * 128, 128), 128)
        )

        def body(k, _):
            for y in range(4) if coords["y"] is None else (coords["y"],):
                for z in range(4) if coords["z"] is None else (coords["z"],):
                    place = (k, y, z, self.p.c, pl.ds(start, count), xs)
                    if len(reads) == 1:
                        self.g[place] = self.g[place] + reads[0](k, y, z)
                        continue
                    total = self.g[place].astype(F32)
                    for read in reads:
                        total = total + read(k, y, z).astype(F32)
                    self.g[place] = total.astype(BF)
            return 0

        lax.fori_loop(self.ks[0], self.ks[0] + self.ks[1], body, 0)

    @staticmethod
    def reader(buf, coords, slot):
        def read(k, y, z):
            index = (slot, k)
            index += (y,) if coords["y"] is None else ()
            index += (z,) if coords["z"] is None else ()
            return buf[index]

        return read

    def core_reader(self, rows):
        shift = self.core_first - self.ks[0]
        return lambda k, y, z: self.core_buf[k + shift, y, z, rows]

    def one(self):
        src = self.g.at[self.k(), :, :, 1 - self.p.c]
        self.sent = self.l.send(src, self.core_at(), self.p.sibling())

    def two(self):
        self.l.arrive(self.core_at(), self.sent, self.p.sibling())
        whole = {"x": None, "y": None, "z": None}
        self.sent1 = []
        for part, order in enumerate(ORDERS):
            rows = rows_of(part)
            self.add(whole, 32 * part, 32, [self.core_reader(rows)])
            axis, base = order[2], free(self.p.own, order, 2)
            far = dict(base, **{axis: (self.p.own[axis] + 2) % 4})
            buf = self.half_bufs[part]
            up = self.l.send(self.at(far, part, 0), buf.at[0, self.k()], self.p.near(axis, 1))
            down = self.l.send(self.at(far, part, 1), buf.at[1, self.k()], self.p.near(axis, 3))
            self.sent1.append((up, down))

    def three(self):
        self.sent2 = []
        for part, order in enumerate(ORDERS):
            axis, base = order[2], free(self.p.own, order, 2)
            half, full = self.half_bufs[part], self.full_bufs[part]
            up, down = self.sent1[part]
            above = dict(base, **{axis: (self.p.own[axis] + 1) % 4})
            below = dict(base, **{axis: (self.p.own[axis] + 3) % 4})
            self.l.arrive(half.at[0, self.k()], up, self.p.near(axis, 3))
            self.add(above, 32 * part, 16, [self.reader(half, above, 0)])
            go_up = self.l.send(self.at(above, part), full.at[0, self.k()], self.p.near(axis, 1))
            self.l.arrive(half.at[1, self.k()], down, self.p.near(axis, 1))
            self.add(below, 32 * part + 16, 16, [self.reader(half, below, 1)])
            go_down = self.l.send(
                self.at(below, part), full.at[1, self.k()], self.p.near(axis, 3)
            )
            self.sent2.append((go_up, go_down))

    def direct(self, coords, part, axis, buf):
        sent = []
        for step in (1, 3, 2):
            target = dict(coords, **{axis: (self.p.own[axis] + step) % 4})
            device = self.p.near(axis, step)
            sent.append(
                (step, self.l.send(self.at(target, part), buf.at[step - 1, self.k()], device))
            )
        return sent

    def direct_arrive(self, sent, coords, part, axis, buf):
        for step, index in sent:
            self.l.arrive(buf.at[step - 1, self.k()], index, self.p.near(axis, 4 - step))
        self.add(coords, 32 * part, 32, [self.reader(buf, coords, s) for s in range(3)])

    def four(self):
        self.sent3 = []
        for part, order in enumerate(ORDERS):
            axis, base = order[2], free(self.p.own, order, 2)
            full = self.full_bufs[part]
            up, down = self.sent2[part]
            self.l.arrive(full.at[0, self.k()], up, self.p.near(axis, 3))
            self.l.arrive(full.at[1, self.k()], down, self.p.near(axis, 1))
            self.add(
                base, 32 * part, 32, [self.reader(full, base, 0), self.reader(full, base, 1)]
            )
            coords = free(self.p.own, order, 1)
            self.sent3.append(self.direct(coords, part, order[1], self.two_bufs[part]))

    def five(self):
        self.sent4 = []
        for part, order in enumerate(ORDERS):
            coords = free(self.p.own, order, 1)
            self.direct_arrive(self.sent3[part], coords, part, order[1], self.two_bufs[part])
            self.sent4.append(self.direct(self.p.own, part, order[0], self.one_bufs[part]))

    def six(self):
        for part, order in enumerate(ORDERS):
            self.direct_arrive(
                self.sent4[part], self.p.own, part, order[0], self.one_bufs[part]
            )


def reduce_bufs():
    half = [(2, 5, 4, 16, 512), (2, 5, 4, 4, 16, 128), (2, 5, 4, 16, 512)]
    full = [(2, 5, 4, 32, 512), (2, 5, 4, 4, 32, 128), (2, 5, 4, 32, 512)]
    two = [(3, 5, 32, 512), (3, 5, 4, 32, 128), (3, 5, 4, 32, 128)]
    one = [(3, 5, 32, 128)] * 3
    return [(3, 4, 4, 96, 512)] + half + full + two + one


def mean_rows(v):
    return jnp.mean(v, -1, keepdims=True)


def hat_of(v):
    center = v - mean_rows(v)
    factor = lax.rsqrt(mean_rows(center * center) + EPS)
    return center * factor, factor


def norm_back(dy, gain, hat, factor):
    scaled = dy * gain
    return factor * (scaled - mean_rows(scaled) - hat * mean_rows(scaled * hat))


def col_sum(v):
    return jnp.sum(v, 0, keepdims=True)


SCRATCH = {
    "g": ((5, 4, 4, 2, 96, 512), BF),
    "rb": ((PLANE, 32, 128), BF),
    "fin_send": ((PLANE, 32, 128), BF),
    "fin_recv": ((32, 2048), BF),
    "lanes": ((16, 10240), BF),
    "shard": ((32, 2048), BF),
    "up16": ((16, FF), BF),
    "meta": ((8, 128), I32),
    "strip": ((STRIPS + 1, SEG, DE), BF),
    "meta_all": ((PLANE, 8, 128), I32),
    "n1": ((ROWS, D), BF),
    "qkv": ((ROWS, 3 * D), BF),
    "prob": ((2 * HEADS, 256, 256), BF),
    "ctx": ((ROWS, D), BF),
    "h1": ((ROWS, D), F32),
    "n2": ((ROWS, D), BF),
    "act": ((ROWS, FF), BF),
    "slope": ((ROWS, FF), BF),
    "hb": ((ROWS, D), BF),
    "low": ((ROWS, D), BF),
    "emb": ((ROWS, DE), BF),
    "wide": ((ROWS, D), F32),
    "acc": ((ROWS, D), F32),
    "vec": ((16, D), F32),
    "vgrad": ((16, D), F32),
    "bqkv": ((8, 3 * D), F32),
    "bup": ((8, FF), F32),
    "dec": ((OUT_ROWS, DE), BF),
    "slots": ((PLANE, SEG, DE), BF),
}
FLIPPED = {"hb": 0, "ctx": D, "act": 2 * D, "n1": 2560, "n2": 2560 + D}
N_SEM = 260


def kernel(
    w_qkv, w_out, w_up, w_down, w_embed, vectors, skipped, lengths, route, x_ref, cot,
    patch_out, fin, perms, vec_out, cot_from, cot_to, emb_from, emb_to, *refs
):
    s = dict(zip(SCRATCH, refs))
    rest = refs[len(SCRATCH):]
    bufs, (send_sem, recv_sem, local_sem, core_free) = rest[:13], rest[13:]
    bufs = (bufs[0], bufs[1:4], bufs[4:7], bufs[7:10], bufs[10:13])
    g = s["g"]
    place = Place()
    links = Links(send_sem, recv_sem)

    def weight(h):
        tile = h // 2
        lanes = pl.ds(pl.multiple_of((h % 2) * 256, 256), 256)
        return g[tile // 4, tile % 4, :, :, :, lanes].reshape(D, 256)

    def put_grad(h, value):
        tile = h // 2
        lanes = pl.ds(pl.multiple_of((h % 2) * 256, 256), 256)
        g[tile // 4, tile % 4, :, :, :, lanes] = value.astype(BF).reshape(4, 2, 96, 256)

    def cols(i, width=256):
        return pl.ds(pl.multiple_of(i * width, width), width)

    cot_load = pltpu.make_async_copy(cot, s["dec"], local_sem.at[0])
    cot_load.start()
    callers = announce(place)
    meta = s["meta"]
    meta[...] = jnp.zeros_like(meta)
    meta[0:4, :] = skipped[...]
    for b in range(2):
        meta[4:5, 4 * b : 4 * b + 4] = lengths[b : b + 1, :]
    lanes = s["lanes"]
    lanes[...] = jnp.zeros_like(lanes)
    lanes[0:1, 0:128] = vectors[...]
    lanes[0:6, L_QKV:L_OUT] = w_qkv[...]
    lanes[0:6, L_OUT:L_UP] = w_out[...]
    for q in range(4):
        lanes[0:6, L_DOWN + D * q : L_DOWN + D * q + D] = w_down[6 * q : 6 * q + 6, :]
    lanes[0:6, L_EMBED : L_EMBED + DE] = w_embed[...]
    s["up16"][...] = jnp.zeros_like(s["up16"])
    s["up16"][0:6, :] = w_up[...]
    lane = iota((D, 128), 1)
    row = iota((D, 128), 0)
    for n in range(6):
        col = lane + 128 * n
        device = (col * 10923) >> 16
        start = min(24 * (128 * n // 6) // 128 * 128, FF - D)
        target = 24 * device + (col - 6 * device) - start
        for q in range(4):
            part = dot(s["up16"][:, start : start + D], hot(row == target + 6 * q))
            at = L_UP + D * q + 128 * n
            lanes[:, at : at + 128] = part.astype(BF)
    row, col = iota((32, 16), 0), iota((32, 16), 1)
    for i in range(4):
        packed = jnp.zeros((32, 512), F32)
        for k in range(5):
            first = 2048 * k + 512 * i
            pick = hot((row == col + 6 * k) & (col < 6))
            packed = packed + dot(pick, lanes[:, first : first + 512])
        s["shard"][:, 512 * i : 512 * i + 512] = packed.astype(BF)
    shard = s["shard"]
    rb, meta_all = s["rb"], s["meta_all"]
    pl.semaphore_wait(pltpu.get_barrier_semaphore(), callers)
    meta_sent = []
    for t in range(1, PLANE):
        meta_sent.append(links.send(meta, meta_all.at[t], place.plane(t)))
    sent = []
    for t in range(1, PLANE):
        to = place.plane(t)
        sent.append(links.send(shard.at[:, cols(to[1], 128)], rb.at[place.fs], to))
    rb[place.fs] = shard[:, cols(place.fs, 128)]
    meta_all[0] = meta[...]
    for t in range(1, PLANE):
        source = place.plane(PLANE - t)
        links.arrive(rb.at[source[1]], sent[t - 1], source)
    arrived = rb[...].reshape(PLANE * 32, 128)
    row, col = iota((96, PLANE * 32), 0), iota((96, PLANE * 32), 1)
    sender = (row * 43) >> 8
    target = sender * 32 + (row - sender * 6)
    own_lanes = pl.ds(pl.multiple_of(place.x * 128, 128), 128)
    for k in range(5):
        block = dot(hot(col == target + 6 * k), arrived).astype(BF)
        g[k, place.y, place.z, place.c, :, own_lanes] = block

    spreads = [Spread(place, links, g, ks) for ks in GROUPS]
    first, later = spreads
    first.one()
    later.one()
    first.two()
    later.two()
    first.three()
    later.three()

    for t in range(1, PLANE):
        links.arrive(meta_all.at[t], meta_sent[t - 1], place.plane(PLANE - t))
    cot_load.wait()

    def lens_of(m, blk):
        lens = [m[4:5, blk * 4 + j : blk * 4 + j + 1].astype(F32) for j in range(4)]
        starts = [jnp.zeros_like(lens[0])]
        for j in range(3):
            starts.append(starts[j] + lens[j])
        return lens, starts

    total = jnp.zeros((1, DE), F32)
    for k in range(STRIPS):
        m = meta_all[route[0, k]]
        blk, j = k // 4, k % 4
        lens, starts = lens_of(m, blk)
        skip = jnp.concatenate([m[2 * blk : 2 * blk + 1], m[2 * blk + 1 : 2 * blk + 2]], 1)
        skip = jnp.broadcast_to(skip.astype(F32), (8, 256)).astype(BF)
        r, t = iota((256, SEG), 0).astype(F32), iota((256, SEG), 1).astype(F32)
        local = dot(skip, hot(r - starts[j] == t))
        tri = hot(iota((SEG, SEG), 0) <= iota((SEG, SEG), 1))
        through = dot(local.astype(BF), tri)[0:1]
        off = (STRIP_POS * k) % 16
        base = STRIP_POS * k - off
        lane = iota((WINDOW, SEG), 1).astype(F32)
        spot = iota((WINDOW, SEG), 0).astype(F32)
        perm = hot((spot == lane + through + float(off)) & (lane < lens[j]))
        perms[k] = perm
        picked = tdot(perm, s["dec"][base : base + WINDOW])
        s["strip"][k] = picked.astype(BF)
        total = total - col_sum(picked)

    def sum_rows(i, acc):
        part = s["dec"][pl.ds(pl.multiple_of(i * 16, 16), 16), :].astype(F32)
        return acc + part

    summed = lax.fori_loop(0, OUT_ROWS // 16, sum_rows, jnp.zeros((16, DE), F32))
    total = total + col_sum(summed) + col_sum(s["dec"][OUT_ROWS - 8 :, :].astype(F32))
    s["vgrad"][...] = jnp.zeros_like(s["vgrad"])
    s["vgrad"][V_MASK : V_MASK + 1, 0:DE] = total

    s["strip"][STRIPS] = jnp.zeros((SEG, DE), BF)
    for t in range(PLANE):
        s["slots"][t] = s["strip"][route[1, (PLANE - t) % PLANE]]
    slot_store = pltpu.make_async_copy(s["slots"], cot_from, local_sem.at[0])
    slot_store.start()
    own_store = pltpu.make_async_copy(s["slots"].at[0], cot_to.at[0], local_sem.at[1])
    own_store.start()

    slot_store.wait()
    own_store.wait()
    cot_sent, cot_copies = [], []

    def send_cot(begin, end):
        for t in range(begin, end):
            slot = cot_to.at[PLANE - t]
            cot_sent.append(links.send(cot_from.at[t], slot, place.plane(t)))
            cot_copies.append(links.started.pop())

    first.four()
    later.four()
    first.five()
    later.five()
    first.six()
    later.six()
    links.drain()
    send_cot(1, PLANE)
    links.started = cot_copies

    chunk = g[0, 0, :, :, :, 0:128].reshape(D, 128)
    table = s["acc"]

    def spread_six(i, _):
        table[0:128, cols(i)] = tdot(chunk, spread_hot(6, 256 * i))
        return 0

    def spread_four(i, _):
        table[128:256, cols(i)] = tdot(chunk, spread_hot(4, 256 * i))
        return 0

    lax.fori_loop(0, 3, spread_six, 0)
    lax.fori_loop(0, 2, spread_four, 0)
    lane6 = iota((16, D), 1)
    lane6 = lane6 - 6 * ((lane6 * 10923) >> 16)
    row6 = iota((16, D), 0)
    for v in range(12):
        low = (6 * v) // 8 * 8
        window = table[low : low + 16, :]
        s["vec"][v : v + 1] = col_sum(jnp.where(row6 + (low - 6 * v) == lane6, window, 0.0))
    lane4, row4 = iota((8, DE), 1) & 3, iota((8, DE), 0)
    few = table[128 + 72 : 128 + 80, 0:DE]
    for i, v in enumerate((V_BE, V_MASK)):
        s["vec"][v : v + 1, 0:DE] = col_sum(jnp.where(row4 - 4 * i == lane4, few, 0.0))
    vec = s["vec"]
    s["bqkv"][...] = jnp.zeros_like(s["bqkv"])
    s["bqkv"][0:1, 0:D] = vec[4:5]
    s["bqkv"][0:1, 2 * D :] = vec[5:6]
    for q in range(4):
        s["bup"][0:1, q * D : (q + 1) * D] = vec[8 + q : 9 + q]

    def norm_one(i, _):
        rows = cols(i, 128)
        hat, _f = hat_of(x_ref[rows, :].astype(F32))
        s["n1"][rows, :] = (hat * vec[0:1] + vec[1:2]).astype(BF)
        return 0

    lax.fori_loop(0, 4, norm_one, 0, unroll=2)

    def qkv_tile(t, _):
        for i in range(2):
            rows = cols(i)
            out = dot(s["n1"][rows, :], weight(H_QKV + t)) + s["bqkv"][0:1, cols(t)]
            s["qkv"][rows, cols(t)] = out.astype(BF)
        return 0

    lax.fori_loop(0, 9, qkv_tile, 0, unroll=3)

    lens_own = [lens_of(meta[...], b) for b in range(2)]

    def doc_bias(starts):
        r, c = iota((256, 256), 0).astype(F32), iota((256, 256), 1).astype(F32)
        doc_r, doc_c = jnp.zeros_like(r), jnp.zeros_like(c)
        for j in range(1, 4):
            doc_r = doc_r + jnp.where(r >= starts[j], 1.0, 0.0)
            doc_c = doc_c + jnp.where(c >= starts[j], 1.0, 0.0)
        return doc_r == doc_c

    lane = iota((256, 128), 1)
    for blk in range(2):
        rows = slice(256 * blk, 256 * blk + 256)
        same = doc_bias(lens_own[blk][1])

        def heads(hp, _):
            q2 = s["qkv"][rows, cols(hp, 128)] * jnp.asarray(0.125, BF)
            k2 = s["qkv"][rows, cols(6 + hp, 128)]
            v2 = s["qkv"][rows, cols(12 + hp, 128)]
            outs = []
            for h in range(2):
                mine = (lane >= 64) if h else (lane < 64)
                scores = dot_t(jnp.where(mine, q2, jnp.zeros_like(q2)), k2)
                scores = jnp.where(same, scores, MASKED)
                e = jnp.exp(scores - jnp.max(scores, -1, keepdims=True))
                p = (e * (1.0 / jnp.sum(e, -1, keepdims=True))).astype(BF)
                s["prob"][12 * blk + 2 * hp + h] = p
                outs.append(dot(p, v2))
            s["ctx"][rows, cols(hp, 128)] = jnp.where(lane < 64, outs[0], outs[1]).astype(BF)
            return 0

        lax.fori_loop(0, 6, heads, 0, unroll=2)

    def out_tile(t, _):
        out = dot(s["ctx"][...], weight(H_OUT + t)) + vec[6:7, cols(t)]
        s["h1"][:, cols(t)] = x_ref[:, cols(t)].astype(F32) + out
        return 0

    lax.fori_loop(0, 3, out_tile, 0, unroll=3)

    def norm_two(i, _):
        rows = cols(i, 128)
        hat, _f = hat_of(s["h1"][rows, :])
        s["n2"][rows, :] = (hat * vec[2:3] + vec[3:4]).astype(BF)
        return 0

    lax.fori_loop(0, 4, norm_two, 0, unroll=2)

    def up_tile(t, _):
        for i in range(2):
            rows = cols(i)
            u = dot(s["n2"][rows, :], weight(H_UP + t)) + s["bup"][0:1, cols(t)]
            phi = 0.5 * (1.0 + lax.erf(u * 0.7071067811865476))
            density = jnp.exp(-0.5 * u * u) * 0.3989422804014327
            s["act"][rows, cols(t)] = (u * phi).astype(BF)
            s["slope"][rows, cols(t)] = (phi + u * density).astype(BF)
        return 0

    lax.fori_loop(0, 12, up_tile, 0, unroll=2)
    for t in range(3):
        for i in range(2):
            rows = cols(i)
            out = s["h1"][rows, cols(t)] + vec[7:8, cols(t)]
            for q in range(4):
                out = out + dot(s["act"][rows, cols(q, D)], weight(H_DOWN + 3 * q + t))
            s["hb"][rows, cols(t)] = out.astype(BF)
    for t in range(2):
        out = dot(s["hb"][...], weight(H_EMBED + t)) + vec[V_BE : V_BE + 1, cols(t)]
        s["emb"][:, cols(t)] = out.astype(BF)

    def strip_hot(blk):
        lens, starts = lens_own[blk]
        picks = []
        for j in range(4):
            r, t = iota((256, SEG), 0).astype(F32), iota((256, SEG), 1).astype(F32)
            picks.append(hot((r - starts[j] == t) & (t < lens[j])))
        return jnp.concatenate(picks, 1)

    for blk in range(2):
        moved = tdot(strip_hot(blk), s["emb"][256 * blk : 256 * blk + 256])
        for j in range(4):
            s["strip"][4 * blk + j] = moved[SEG * j : SEG * j + SEG].astype(BF)
    for t in range(PLANE):
        s["slots"][t] = s["strip"][route[1, t]]
    slot_store = pltpu.make_async_copy(s["slots"], emb_from, local_sem.at[0])
    slot_store.start()
    own_store = pltpu.make_async_copy(s["slots"].at[0], emb_to.at[0], local_sem.at[1])
    own_store.start()
    slot_store.wait()
    own_store.wait()
    emb_sent = []

    def send_emb(first, last):
        for t in range(first, last):
            emb_sent.append(links.send(emb_from.at[t], emb_to.at[t], place.plane(t)))

    send_emb(1, PLANE)

    def flipped(name):
        return s["dec"][FLIPPED[name] : FLIPPED[name] + D, :]

    for name in ("n1", "n2", "ctx", "hb"):

        def flip(i, _, name=name):
            at = pl.ds(pl.multiple_of(FLIPPED[name] + 128 * i, 128), 128)
            s["dec"][at, :] = s[name][:, cols(i, 128)].T
            return 0

        lax.fori_loop(0, 6, flip, 0)

    cot_back = [pltpu.make_async_copy(cot_to.at[0], s["slots"].at[0], local_sem.at[2])]
    cot_back[0].start()
    for t in range(1, PLANE):
        slot = PLANE - t
        links.arrive(cot_to.at[slot], cot_sent[t - 1], place.plane(PLANE - t))
        to = s["slots"].at[slot]
        cot_back.append(pltpu.make_async_copy(cot_to.at[slot], to, local_sem.at[2 + t]))
        cot_back[t].start()
    de = s["emb"]
    for copy in cot_back:
        copy.wait()
    for blk in range(2):
        got = [s["slots"][route[0, 4 * blk + j]] for j in range(4)]
        moved = dot(strip_hot(blk), jnp.concatenate(got, 0))
        de[256 * blk : 256 * blk + 256] = moved.astype(BF)
    vg = s["vgrad"]
    vg[V_BE : V_BE + 1, 0:DE] = col_sum(de[...].astype(F32))
    wide = s["wide"]

    def embed_back(i, acc):
        rows = cols(i)
        dh = dot_t(de[rows, 0:256], weight(H_EMBED)) + dot_t(de[rows, 256:], weight(H_EMBED + 1))
        wide[rows, :] = dh
        s["low"][rows, :] = dh.astype(BF)
        return acc + col_sum(dh)

    vg[7:8] = lax.fori_loop(0, 2, embed_back, jnp.zeros((1, D), F32), unroll=2)
    for t in range(2):
        put_grad(H_EMBED + t, dot(flipped("hb"), de[:, cols(t)]))

    def down_part(q, _):

        def rows_part(i, acc):
            rows = cols(i)
            da = dot_t(s["low"][rows, 0:256], weight(H_DOWN + 3 * q))
            for t in range(1, 3):
                da = da + dot_t(s["low"][rows, cols(t)], weight(H_DOWN + 3 * q + t))
            du = (da * s["slope"][rows, cols(q, D)].astype(F32)).astype(BF)
            s["slope"][rows, cols(q, D)] = du
            return acc + col_sum(du.astype(F32))

        vg[pl.ds(8 + q, 1), :] = lax.fori_loop(0, 2, rows_part, jnp.zeros((1, D), F32), unroll=2)
        for i in range(6):
            at = FLIPPED["act"] + 128 * i
            s["dec"][at : at + 128, :] = s["act"][:, cols(6 * q + i, 128)].T
        for t in range(3):
            put_grad(H_DOWN + 3 * q + t, dot(flipped("act"), s["low"][:, cols(t)]))
        return 0

    lax.fori_loop(0, 4, down_part, 0)
    acc = s["acc"]

    def up_part(q, _):
        def rows_part(i, _):
            rows = cols(i)
            total = dot_t(s["slope"][rows, cols(3 * q)], weight(H_UP + 3 * q))
            for t in range(1, 3):
                total = total + dot_t(s["slope"][rows, cols(3 * q + t)], weight(H_UP + 3 * q + t))
            acc[rows, :] = jnp.where(q == 0, total, acc[rows, :] + total)
            return 0

        lax.fori_loop(0, 2, rows_part, 0, unroll=2)
        for t in range(3):
            put_grad(H_UP + 3 * q + t, dot(flipped("n2"), s["slope"][:, cols(3 * q + t)]))
        return 0

    lax.fori_loop(0, 4, up_part, 0)

    g_first, g_mid, g_later = [Gather(place, links, g, ks, bufs) for ks in SUM_GROUPS]
    g_mid.core_first = 1
    g_later.one()

    def norm_two_back(i, sums):
        rows = cols(i, 128)
        hat, factor = hat_of(s["h1"][rows, :])
        dn = acc[rows, :]
        dh = wide[rows, :] + norm_back(dn, vec[2:3], hat, factor)
        wide[rows, :] = dh
        s["low"][rows, :] = dh.astype(BF)
        return (sums[0] + col_sum(dn * hat), sums[1] + col_sum(dn), sums[2] + col_sum(dh))

    zero = jnp.zeros((1, D), F32)
    vg[2:3], vg[3:4], vg[6:7] = lax.fori_loop(0, 4, norm_two_back, (zero, zero, zero), unroll=2)


    def out_back(i, _):
        rows = cols(i)
        total = dot_t(s["low"][rows, 0:256], weight(H_OUT))
        for t in range(1, 3):
            total = total + dot_t(s["low"][rows, cols(t)], weight(H_OUT + t))
        s["hb"][rows, :] = total.astype(BF)
        return 0

    lax.fori_loop(0, 2, out_back, 0, unroll=2)
    for t in range(3):
        put_grad(H_OUT + t, dot(flipped("ctx"), s["low"][:, cols(t)]))

    for blk in range(2):
        rows = slice(256 * blk, 256 * blk + 256)

        def put(chunk, value, blk=blk):
            at = pl.ds(pl.multiple_of(512 * (chunk // 4) + 256 * blk, 256), 256)
            s["dec"][at, cols(chunk % 4, 128)] = value.astype(BF)

        def heads_back(hp, _):
            q2 = s["qkv"][rows, cols(hp, 128)]
            k2 = s["qkv"][rows, cols(6 + hp, 128)]
            v2 = s["qkv"][rows, cols(12 + hp, 128)]
            do2 = s["hb"][rows, cols(hp, 128)]
            dq, dk, dv = [], [], []
            for h in range(2):
                mine = (lane >= 64) if h else (lane < 64)
                p = s["prob"][12 * blk + 2 * hp + h]
                dp = dot_t(jnp.where(mine, do2, jnp.zeros_like(do2)), v2)
                pf = p.astype(F32)
                inner = jnp.sum(pf * dp, -1, keepdims=True)
                ds = (pf * (dp - inner)).astype(BF)
                dq.append(dot(ds, k2))
                dk.append(tdot(ds, q2))
                dv.append(tdot(p, do2))
            lo = lane < 64
            put(hp, jnp.where(lo, dq[0], dq[1]) * 0.125)
            put(6 + hp, jnp.where(lo, dk[0], dk[1]) * 0.125)
            put(12 + hp, jnp.where(lo, dv[0], dv[1]))
            return 0

        lax.fori_loop(0, 6, heads_back, 0, unroll=2)
        if blk == 0:
            g_later.two()
            sibling = place.sibling()
            pl.semaphore_signal(core_free, inc=1, device_id=sibling, device_id_type=MESH)
        else:
            g_later.three()

    def dqkv(t, start=0, size=ROWS):
        rows = pl.ds(pl.multiple_of(512 * (t // 2) + start, 64), size)
        return s["dec"][rows, cols(t % 2)]

    def bias_sums(i, sums):
        q = [dqkv(t, 64 * i, 64).astype(F32) for t in (0, 1, 2)]
        v = [dqkv(t, 64 * i, 64).astype(F32) for t in (6, 7, 8)]
        q, v = [jnp.concatenate(part, 1) for part in (q, v)]
        return (sums[0] + col_sum(q), sums[1] + col_sum(v))

    vg[4:5], vg[5:6] = lax.fori_loop(0, 8, bias_sums, (zero, zero), unroll=2)

    def qkv_part(q, _):
        def rows_part(i, _):
            rows = cols(i)
            total = dot_t(dqkv(3 * q, 256 * i, 256), weight(H_QKV + 3 * q))
            for t in range(1, 3):
                total = total + dot_t(dqkv(3 * q + t, 256 * i, 256), weight(H_QKV + 3 * q + t))
            acc[rows, :] = jnp.where(q == 2, total, acc[rows, :] + total)
            return 0

        lax.fori_loop(0, 2, rows_part, 0, unroll=2)
        for t in range(3):
            put_grad(H_QKV + 3 * q + t, dot(flipped("n1"), dqkv(3 * q + t)))
        return 0

    qkv_part(2, 0)
    pl.semaphore_wait(core_free, 1)
    g_mid.one()
    lax.fori_loop(0, 2, qkv_part, 0)
    g_mid.two()

    def norm_one_back(i, sums):
        rows = cols(i, 128)
        hat, factor = hat_of(x_ref[rows, :].astype(F32))
        dn = acc[rows, :]
        wide[rows, :] = wide[rows, :] + norm_back(dn, vec[0:1], hat, factor)
        return (sums[0] + col_sum(dn * hat), sums[1] + col_sum(dn))

    vg[0:1], vg[1:2] = lax.fori_loop(0, 4, norm_one_back, (zero, zero), unroll=2)
    patch_store = pltpu.make_async_copy(wide, patch_out, local_sem.at[1])
    patch_store.start()

    table[0:256, :] = jnp.zeros((256, D), F32)
    lane6 = iota((8, D), 1)
    lane6 = lane6 - 6 * ((lane6 * 10923) >> 16)
    row6 = iota((8, D), 0)
    for a in range(9):
        rows = jnp.zeros((8, D), F32)
        for v in range(12):
            if 6 * v < 8 * a + 8 and 6 * v + 6 > 8 * a:
                rows = jnp.where(row6 + (8 * a - 6 * v) == lane6, vg[v : v + 1], rows)
        table[8 * a : 8 * a + 8, :] = rows
    rows = jnp.zeros((8, DE), F32)
    for i, v in enumerate((V_BE, V_MASK)):
        rows = jnp.where(row4 - 4 * i == lane4, vg[v : v + 1, 0:DE], rows)
    table[128 + 72 : 128 + 80, 0:DE] = rows

    def fold_six(i, total):
        return total + dot_t(spread_hot(6, 256 * i), table[0:128, cols(i)].astype(BF))

    def fold_four(i, total):
        return total + dot_t(spread_hot(4, 256 * i), table[128:256, cols(i)].astype(BF))

    chunk = lax.fori_loop(0, 3, fold_six, jnp.zeros((D, 128), F32))
    chunk = lax.fori_loop(0, 2, fold_four, chunk)
    g[0, 0, :, :, :, 0:128] = chunk.astype(BF).reshape(4, 2, 96, 128)

    g_first.one()
    vec_out[...] = vec[V_MASK : V_MASK + 1, :]
    g_later.four()
    g_first.two()
    g_mid.three()
    g_later.five()
    g_first.three()
    g_mid.four()
    g_later.six()
    g_first.four()
    g_mid.five()
    g_first.five()
    g_mid.six()
    g_first.six()
    row, col = iota((PLANE * 32, 96), 0), iota((PLANE * 32, 96), 1)
    inner_row = row & 31
    base_row = 6 * (row >> 5)
    slots = jnp.zeros((PLANE * 32, 128), F32)
    for k in range(5):
        j = inner_row - 6 * k
        pick = hot((col == base_row + j) & (j >= 0) & (j < 6))
        slots = slots + dot(pick, g[k, place.y, place.z, place.c, :, own_lanes])
    s["fin_send"][...] = slots.astype(BF).reshape(PLANE, 32, 128)
    fin_sent = []
    for t in range(1, PLANE):
        to = place.plane(t)
        slot = s["fin_recv"].at[:, cols(place.fs, 128)]
        fin_sent.append(links.send(s["fin_send"].at[to[1]], slot, to))
    s["fin_recv"][:, cols(place.fs, 128)] = s["fin_send"][place.fs]
    for t in range(1, PLANE):
        source = place.plane(PLANE - t)
        links.arrive(s["fin_recv"].at[:, cols(source[1], 128)], fin_sent[t - 1], source)
    fin[...] = s["fin_recv"][...]
    for t in range(1, PLANE):
        links.arrive(emb_to.at[t], emb_sent[t - 1], place.plane(PLANE - t))
    links.drain()
    patch_store.wait()


def mega(w_qkv, w_out, w_up, w_down, w_embed, vectors, skipped, lengths, route, x, cot):
    dma = pltpu.SemaphoreType.DMA
    vmem = pl.BlockSpec(memory_space=pltpu.VMEM)
    smem = pl.BlockSpec(memory_space=pltpu.SMEM)
    hbm = pl.BlockSpec(memory_space=pl.ANY)
    return pl.pallas_call(
        kernel,
        out_shape=(
            jax.ShapeDtypeStruct((ROWS, D), F32),
            jax.ShapeDtypeStruct((32, 2048), BF),
            jax.ShapeDtypeStruct((STRIPS, WINDOW, SEG), BF),
            jax.ShapeDtypeStruct((1, D), F32),
        )
        + (jax.ShapeDtypeStruct((PLANE, SEG, DE), BF),) * 4,
        in_specs=[vmem] * 8 + [smem, vmem, hbm],
        out_specs=(hbm, vmem, vmem, vmem) + (hbm,) * 4,
        scratch_shapes=[pltpu.VMEM(shape, kind) for shape, kind in SCRATCH.values()]
        + [pltpu.VMEM(shape, BF) for shape in reduce_bufs()]
        + [dma((N_SEM,)), dma((N_SEM,)), dma((2 + PLANE,))]
        + [pltpu.SemaphoreType.REGULAR],
        compiler_params=pltpu.CompilerParams(
            collective_id=1, has_side_effects=True, vmem_limit_bytes=64 * 1024 * 1024
        ),
        name="layer",
    )(w_qkv, w_out, w_up, w_down, w_embed, vectors, skipped, lengths, route, x, cot)


VECTOR_AT = (0, 6, 12, 18, 24, 30, 36, 48, 42, 72, 76)
VECTOR_SIZE = (6, 6, 6, 6, 6, 6, 6, 24, 6, 4, 4)


def finish_kernel(route, patch, fin, perms, mask, emb, dec_out, patch_out, g_qkv, g_out, g_up,
                  g_down, g_embed, *rest):
    vectors, (dec, wide, strips, rows, sems) = rest[:11], rest[11:]
    loads = []
    for k in range(STRIPS):
        source = emb.at[route[0, k]]
        loads.append(pltpu.make_async_copy(source, strips.at[k], sems.at[2 + k]))
        loads[-1].start()
    patch_load = pltpu.make_async_copy(patch, rows, sems.at[0])
    patch_load.start()
    token = mask[0:1, 0:DE]
    blank = jnp.broadcast_to(token.astype(BF), (64, DE))

    def fill(i, _):
        dec[pl.ds(pl.multiple_of(i * 64, 64), 64), :] = blank
        return 0

    lax.fori_loop(0, OUT_ROWS // 64, fill, 0)
    dec[OUT_ROWS - 8 :, :] = blank[0:8]
    for k in range(STRIPS):
        perm = perms[k]
        base = STRIP_POS * k - (STRIP_POS * k) % 16
        filled = dot(perm, jnp.ones((SEG, 128), BF))[:, 0:1]
        loads[k].wait()
        placed = dot(perm, strips[k])
        dec[base : base + WINDOW] = jnp.where(filled > 0.5, placed, token).astype(BF)
    dec_store = pltpu.make_async_copy(dec, dec_out, sems.at[1])
    dec_store.start()
    patch_load.wait()
    patch_store = pltpu.make_async_copy(rows, patch_out, sems.at[0])
    patch_store.start()
    row, col = iota((8, 32), 0), iota((8, 32), 1)
    for k in range(5):
        pick = hot((col == row + 6 * k) & (row < 6))
        wide[:, 2048 * k : 2048 * k + 2048] = dot(pick, fin[...])
    g_qkv[...] = wide[0:6, L_QKV:L_OUT]
    g_out[...] = wide[0:6, L_OUT:L_UP]
    for q in range(4):
        g_down[6 * q : 6 * q + 6, :] = wide[0:6, L_DOWN + D * q : L_DOWN + D * q + D]
    g_embed[...] = wide[0:6, L_EMBED : L_EMBED + DE]
    col = iota((256, 384), 1)
    device = (col * 2731) >> 16
    inner = col - 24 * device
    part = (inner * 43) >> 8
    source = 6 * device + (inner - 6 * part)
    row = iota((256, 384), 0)
    for shift in range(4):
        pick = [hot((part == q) & (row == source + (96 * shift) % 128)) for q in range(4)]
        for m in (shift, shift + 4):
            start = L_UP + (96 * m) // 128 * 128
            total = jnp.zeros((8, 384), F32)
            for q in range(4):
                window = wide[:, start + D * q : start + D * q + 256].astype(BF)
                total = total + dot(window, pick[q])
            g_up[:, 384 * m : 384 * m + 384] = total[0:6]
    for ref, at, size in zip(vectors, VECTOR_AT, VECTOR_SIZE):
        ref[...] = wide[0, at : at + size]
    patch_store.wait()
    dec_store.wait()


def finish(route, patch, fin, perms, mask, emb):
    vmem = pl.BlockSpec(memory_space=pltpu.VMEM)
    hbm = pl.BlockSpec(memory_space=pl.ANY)
    shape = jax.ShapeDtypeStruct
    return pl.pallas_call(
        finish_kernel,
        out_shape=(shape((OUT_ROWS, DE), BF), shape((ROWS, D), F32))
        + tuple(shape(s, F32) for s in ((6, 3 * D), (6, D), (6, FF), (24, D), (6, DE)))
        + tuple(shape((n,), F32) for n in VECTOR_SIZE),
        in_specs=[pl.BlockSpec(memory_space=pltpu.SMEM), hbm, vmem, vmem, vmem, hbm],
        out_specs=(hbm, hbm) + (vmem,) * 16,
        scratch_shapes=[
            pltpu.VMEM((OUT_ROWS, DE), BF),
            pltpu.VMEM((8, 10240), F32),
            pltpu.VMEM((STRIPS, SEG, DE), BF),
            pltpu.VMEM((ROWS, D), F32),
            pltpu.SemaphoreType.DMA((2 + STRIPS,)),
        ],
        compiler_params=pltpu.CompilerParams(vmem_limit_bytes=64 * 1024 * 1024),
        name="finish",
    )(route, patch, fin, perms, mask, emb)


def on_device(patches, lengths, skipped, strip_order, decoder_grad, qkv_weight, out_weight,
              up_weight, down_weight, embed_weight, gain_one, shift_one, gain_two, shift_two,
              bias_query, bias_value, bias_out, bias_up, bias_down, bias_embed, mask_token):
    pieces = (gain_one, shift_one, gain_two, shift_two, bias_query, bias_value, bias_out,
              bias_down, bias_up, bias_embed, mask_token)
    vectors, at = None, 0
    for piece in pieces:
        size = piece.shape[0]
        padded = jnp.pad(piece, (at, 128 - at - size))
        vectors = padded if vectors is None else vectors + padded
        at += size
    strip = lax.broadcasted_iota(I32, (PLANE, STRIPS), 1)
    place = lax.broadcasted_iota(I32, (PLANE, STRIPS), 0)
    match = (strip_order[0, None, 0:STRIPS] == place).astype(I32)
    inverse = STRIPS + jnp.sum(match * (strip - STRIPS), 1)
    route = jnp.stack([strip_order[0], inverse])
    patch_grad, fin, perms, mask, _, _, _, emb = mega(
        qkv_weight, out_weight, up_weight, down_weight, embed_weight, vectors[None],
        skipped.reshape(4, 128), lengths, route, patches, decoder_grad,
    )
    return tuple(finish(route, patch_grad, fin, perms, mask, emb))


def solution(mesh):
    both = ("dp", "fsdp")
    rows, vector = P(both, None), P(both)
    return jax.shard_map(
        on_device,
        mesh=mesh,
        in_specs=(rows, rows, rows, P("dp", None), rows) + (rows,) * 5 + (vector,) * 11,
        out_specs=(rows,) * 7 + (vector,) * 11,
        check_vma=False,
    )
```

```python
import functools

import jax
import jax.numpy as jnp
from jax import lax
from jax.experimental import pallas as pl
from jax.experimental.pallas import tpu as pltpu
from jax.sharding import PartitionSpec as P

MESH = pl.DeviceIdType.MESH
BF, F32, I32 = jnp.bfloat16, jnp.float32, jnp.int32
ROWS, D, FF, DE, HEADS = 512, 768, 3072, 512, 12
PLANE, STRIPS, STRIP_POS, SEG = 16, 8, 529, 128
OUT_ROWS = STRIPS * STRIP_POS
WINDOW = 272
EPS = 1e-06
MASKED = -1e9
H_VEC, H_QKV, H_OUT, H_UP, H_DOWN, H_EMBED = 0, 1, 10, 13, 25, 37
GROUPS = ((0, 2), (2, 3))
SUM_GROUPS = ((0, 1), (1, 1), (2, 3))
ORDERS = ("xyz", "yzx", "zxy")
V_BE, V_MASK = 12, 13
L_QKV, L_OUT, L_UP, L_DOWN, L_EMBED = 256, 2560, 3328, 6400, 9472


def dot(a, b):
    return jnp.dot(a, b, preferred_element_type=F32)


def dot_t(a, b):
    return lax.dot_general(a, b, (((1,), (1,)), ((), ())), preferred_element_type=F32)


def tdot(a, b):
    return lax.dot_general(a, b, (((0,), (0,)), ((), ())), preferred_element_type=F32)


def iota(shape, dim):
    return lax.broadcasted_iota(I32, shape, dim)


def hot(mask):
    return jnp.where(mask, 1.0, 0.0).astype(BF)


def spread_hot(each, first):
    row, col = iota((D, 256), 0), iota((D, 256), 1) + first
    owner = (col * 10923) >> 16 if each == 6 else col >> 2
    return hot(row == 6 * owner)


class Place:
    def __init__(self):
        self.dp = lax.axis_index("dp")
        self.fs = lax.axis_index("fsdp")
        self.z, self.c = self.dp // 2, self.dp % 2
        self.y, self.x = self.fs // 4, self.fs % 4
        self.own = {"x": self.x, "y": self.y, "z": self.z}

    def near(self, axis, step):
        at = dict(self.own)
        at[axis] = (at[axis] + step) % 4
        return (at["z"] * 2 + self.c, at["y"] * 4 + at["x"])

    def sibling(self):
        return (self.z * 2 + 1 - self.c, self.fs)

    def plane(self, step):
        return (self.dp, (self.fs + step) % PLANE)


def announce(place):
    barrier = pltpu.get_barrier_semaphore()
    others = [place.near("z", s) for s in (1, 2, 3)] + [place.sibling()]
    others += [place.plane(t) for t in range(1, PLANE)]
    for other in others:
        pl.semaphore_signal(barrier, inc=1, device_id=other, device_id_type=MESH)
    return len(others)


class Links:
    def __init__(self, send_sem, recv_sem):
        self.send_sem, self.recv_sem = send_sem, recv_sem
        self.used = 0
        self.started = []

    def make(self, src, dst, index, device):
        return pltpu.make_async_remote_copy(
            src_ref=src,
            dst_ref=dst,
            send_sem=self.send_sem.at[index],
            recv_sem=self.recv_sem.at[index],
            device_id=device,
            device_id_type=MESH,
        )

    def send(self, src, dst, device):
        index = self.used
        self.used += 1
        copy = self.make(src, dst, index, device)
        copy.start()
        self.started.append(copy)
        return index

    def arrive(self, dst, index, device):
        self.make(dst, dst, index, device).wait_recv()

    def drain(self, count=None):
        count = len(self.started) if count is None else count
        for copy in self.started[:count]:
            copy.wait_send()
        self.started = self.started[count:]


def region(ks, coords, core, rows):
    ys = slice(None) if coords["y"] is None else coords["y"]
    zs = slice(None) if coords["z"] is None else coords["z"]
    xs = (
        slice(None)
        if coords["x"] is None
        else pl.ds(pl.multiple_of(coords["x"] * 128, 128), 128)
    )
    return (pl.ds(ks[0], ks[1]), ys, zs, core, rows, xs)


def rows_of(part, half=None):
    return pl.ds(32 * part, 32) if half is None else pl.ds(32 * part + 16 * half, 16)


def free(own, order, count):
    return {a: (None if a in order[:count] else own[a]) for a in "xyz"}


class Spread:
    def __init__(self, place, links, g, ks):
        self.p, self.l, self.g, self.ks = place, links, g, ks

    def at(self, coords, part, half=None, core=None):
        core = self.p.c if core is None else core
        return self.g.at[region(self.ks, coords, core, rows_of(part, half))]

    def send(self, coords, part, half, device):
        view = self.at(coords, part, half)
        return self.l.send(view, view, device)

    def direct(self, phase):
        sent = []
        for part, order in enumerate(ORDERS):
            coords = free(self.p.own, order, phase)
            axis = order[phase]
            for step in (1, 3, 2):
                index = self.send(coords, part, None, self.p.near(axis, step))
                sent.append((part, coords, axis, step, index))
        return sent

    def direct_arrive(self, sent):
        for part, coords, axis, step, index in sent:
            source = dict(coords, **{axis: (self.p.own[axis] + 4 - step) % 4})
            self.l.arrive(self.at(source, part), index, self.p.near(axis, 4 - step))

    def one(self):
        self.sent1 = self.direct(0)

    def two(self):
        self.direct_arrive(self.sent1)
        self.sent2 = self.direct(1)

    def three(self):
        self.direct_arrive(self.sent2)
        self.sib = []
        self.sent3 = []
        for part, order in enumerate(ORDERS):
            axis, base = order[2], free(self.p.own, order, 2)
            up = self.send(base, part, None, self.p.near(axis, 1))
            down = self.send(base, part, None, self.p.near(axis, 3))
            self.sent3.append((up, down))
        for part, order in enumerate(ORDERS):
            self.share(free(self.p.own, order, 2), part, None)

    def share(self, coords, part, half):
        index = self.send(coords, part, half, self.p.sibling())
        self.sib.append((coords, part, half, index))

    def four(self):
        self.sent4 = []
        for part, order in enumerate(ORDERS):
            axis, base = order[2], free(self.p.own, order, 2)
            up, down = self.sent3[part]
            own = self.p.own[axis]
            below = dict(base, **{axis: (own + 3) % 4})
            above = dict(base, **{axis: (own + 1) % 4})
            self.l.arrive(self.at(below, part), up, self.p.near(axis, 3))
            go_up = self.send(below, part, 0, self.p.near(axis, 1))
            self.l.arrive(self.at(above, part), down, self.p.near(axis, 1))
            go_down = self.send(above, part, 1, self.p.near(axis, 3))
            self.sent4.append((go_up, go_down))
            self.share(below, part, None)
            self.share(above, part, None)

    def five(self):
        for part, order in enumerate(ORDERS):
            axis, base = order[2], free(self.p.own, order, 2)
            go_up, go_down = self.sent4[part]
            far = dict(base, **{axis: (self.p.own[axis] + 2) % 4})
            self.l.arrive(self.at(far, part, 0), go_up, self.p.near(axis, 3))
            self.share(far, part, 0)
            self.l.arrive(self.at(far, part, 1), go_down, self.p.near(axis, 1))
            self.share(far, part, 1)

    def six(self):
        for coords, part, half, index in self.sib:
            self.l.arrive(
                self.at(coords, part, half, 1 - self.p.c), index, self.p.sibling()
            )


class Gather:
    def __init__(self, place, links, g, ks, bufs):
        self.p, self.l, self.g, self.ks = place, links, g, ks
        self.core_first = 0
        self.core_buf, self.half_bufs, self.full_bufs, self.two_bufs, self.one_bufs = bufs

    def at(self, coords, part, half=None):
        return self.g.at[region(self.ks, coords, self.p.c, rows_of(part, half))]

    def k(self):
        return pl.ds(self.ks[0], self.ks[1])

    def core_at(self):
        return self.core_buf.at[pl.ds(self.core_first, self.ks[1])]

    def add(self, coords, start, count, reads):
        xs = (
            slice(None)
            if coords["x"] is None
            else pl.ds(pl.multiple_of(coords["x"] * 128, 128), 128)
        )

        def body(k, _):
            for y in range(4) if coords["y"] is None else (coords["y"],):
                for z in range(4) if coords["z"] is None else (coords["z"],):
                    place = (k, y, z, self.p.c, pl.ds(start, count), xs)
                    if len(reads) == 1:
                        self.g[place] = self.g[place] + reads[0](k, y, z)
                        continue
                    total = self.g[place].astype(F32)
                    for read in reads:
                        total = total + read(k, y, z).astype(F32)
                    self.g[place] = total.astype(BF)
            return 0

        lax.fori_loop(self.ks[0], self.ks[0] + self.ks[1], body, 0)

    @staticmethod
    def reader(buf, coords, slot):
        def read(k, y, z):
            index = (slot, k)
            index += (y,) if coords["y"] is None else ()
            index += (z,) if coords["z"] is None else ()
            return buf[index]

        return read

    def core_reader(self, rows):
        shift = self.core_first - self.ks[0]
        return lambda k, y, z: self.core_buf[k + shift, y, z, rows]

    def one(self):
        src = self.g.at[self.k(), :, :, 1 - self.p.c]
        self.sent = self.l.send(src, self.core_at(), self.p.sibling())

    def two(self):
        self.l.arrive(self.core_at(), self.sent, self.p.sibling())
        whole = {"x": None, "y": None, "z": None}
        self.sent1 = []
        for part, order in enumerate(ORDERS):
            rows = rows_of(part)
            self.add(whole, 32 * part, 32, [self.core_reader(rows)])
            axis, base = order[2], free(self.p.own, order, 2)
            far = dict(base, **{axis: (self.p.own[axis] + 2) % 4})
            buf = self.half_bufs[part]
            up = self.l.send(self.at(far, part, 0), buf.at[0, self.k()], self.p.near(axis, 1))
            down = self.l.send(self.at(far, part, 1), buf.at[1, self.k()], self.p.near(axis, 3))
            self.sent1.append((up, down))

    def three(self):
        self.sent2 = []
        for part, order in enumerate(ORDERS):
            axis, base = order[2], free(self.p.own, order, 2)
            half, full = self.half_bufs[part], self.full_bufs[part]
            up, down = self.sent1[part]
            above = dict(base, **{axis: (self.p.own[axis] + 1) % 4})
            below = dict(base, **{axis: (self.p.own[axis] + 3) % 4})
            self.l.arrive(half.at[0, self.k()], up, self.p.near(axis, 3))
            self.add(above, 32 * part, 16, [self.reader(half, above, 0)])
            go_up = self.l.send(self.at(above, part), full.at[0, self.k()], self.p.near(axis, 1))
            self.l.arrive(half.at[1, self.k()], down, self.p.near(axis, 1))
            self.add(below, 32 * part + 16, 16, [self.reader(half, below, 1)])
            go_down = self.l.send(
                self.at(below, part), full.at[1, self.k()], self.p.near(axis, 3)
            )
            self.sent2.append((go_up, go_down))

    def direct(self, coords, part, axis, buf):
        sent = []
        for step in (1, 3, 2):
            target = dict(coords, **{axis: (self.p.own[axis] + step) % 4})
            device = self.p.near(axis, step)
            sent.append(
                (step, self.l.send(self.at(target, part), buf.at[step - 1, self.k()], device))
            )
        return sent

    def direct_arrive(self, sent, coords, part, axis, buf):
        for step, index in sent:
            self.l.arrive(buf.at[step - 1, self.k()], index, self.p.near(axis, 4 - step))
        self.add(coords, 32 * part, 32, [self.reader(buf, coords, s) for s in range(3)])

    def four(self):
        self.sent3 = []
        for part, order in enumerate(ORDERS):
            axis, base = order[2], free(self.p.own, order, 2)
            full = self.full_bufs[part]
            up, down = self.sent2[part]
            self.l.arrive(full.at[0, self.k()], up, self.p.near(axis, 3))
            self.l.arrive(full.at[1, self.k()], down, self.p.near(axis, 1))
            self.add(
                base, 32 * part, 32, [self.reader(full, base, 0), self.reader(full, base, 1)]
            )
            coords = free(self.p.own, order, 1)
            self.sent3.append(self.direct(coords, part, order[1], self.two_bufs[part]))

    def five(self):
        self.sent4 = []
        for part, order in enumerate(ORDERS):
            coords = free(self.p.own, order, 1)
            self.direct_arrive(self.sent3[part], coords, part, order[1], self.two_bufs[part])
            self.sent4.append(self.direct(self.p.own, part, order[0], self.one_bufs[part]))

    def six(self):
        for part, order in enumerate(ORDERS):
            self.direct_arrive(
                self.sent4[part], self.p.own, part, order[0], self.one_bufs[part]
            )


def reduce_bufs():
    half = [(2, 5, 4, 16, 512), (2, 5, 4, 4, 16, 128), (2, 5, 4, 16, 512)]
    full = [(2, 5, 4, 32, 512), (2, 5, 4, 4, 32, 128), (2, 5, 4, 32, 512)]
    two = [(3, 5, 32, 512), (3, 5, 4, 32, 128), (3, 5, 4, 32, 128)]
    one = [(3, 5, 32, 128)] * 3
    return [(3, 4, 4, 96, 512)] + half + full + two + one


def mean_rows(v):
    return jnp.mean(v, -1, keepdims=True)


def hat_of(v):
    center = v - mean_rows(v)
    factor = lax.rsqrt(mean_rows(center * center) + EPS)
    return center * factor, factor


def norm_back(dy, gain, hat, factor):
    scaled = dy * gain
    return factor * (scaled - mean_rows(scaled) - hat * mean_rows(scaled * hat))


def col_sum(v):
    return jnp.sum(v, 0, keepdims=True)


SCRATCH = {
    "g": ((5, 4, 4, 2, 96, 512), BF),
    "rb": ((PLANE, 32, 128), BF),
    "fin_send": ((PLANE, 32, 128), BF),
    "fin_recv": ((32, 2048), BF),
    "lanes": ((16, 10240), BF),
    "shard": ((32, 2048), BF),
    "up16": ((16, FF), BF),
    "meta": ((8, 128), I32),
    "strip": ((STRIPS + 1, SEG, DE), BF),
    "meta_all": ((PLANE, 8, 128), I32),
    "n1": ((ROWS, D), BF),
    "qkv": ((ROWS, 3 * D), BF),
    "prob": ((2 * HEADS, 256, 256), BF),
    "ctx": ((ROWS, D), BF),
    "h1": ((ROWS, D), F32),
    "n2": ((ROWS, D), BF),
    "act": ((ROWS, FF), BF),
    "slope": ((ROWS, FF), BF),
    "hb": ((ROWS, D), BF),
    "low": ((ROWS, D), BF),
    "emb": ((ROWS, DE), BF),
    "wide": ((ROWS, D), F32),
    "acc": ((ROWS, D), F32),
    "vec": ((16, D), F32),
    "vgrad": ((16, D), F32),
    "bqkv": ((8, 3 * D), F32),
    "bup": ((8, FF), F32),
    "dec": ((OUT_ROWS, DE), BF),
    "slots": ((PLANE, SEG, DE), BF),
}
FLIPPED = {"hb": 0, "ctx": D, "act": 2 * D, "n1": 2560, "n2": 2560 + D}
N_SEM = 260


def kernel(
    w_qkv, w_out, w_up, w_down, w_embed, vectors, skipped, lengths, route, x_ref, cot,
    patch_out, fin, perms, vec_out, cot_from, cot_to, emb_from, emb_to, *refs
):
    s = dict(zip(SCRATCH, refs))
    rest = refs[len(SCRATCH):]
    bufs, (send_sem, recv_sem, local_sem, core_free) = rest[:13], rest[13:]
    bufs = (bufs[0], bufs[1:4], bufs[4:7], bufs[7:10], bufs[10:13])
    g = s["g"]
    place = Place()
    links = Links(send_sem, recv_sem)

    def weight(h):
        tile = h // 2
        lanes = pl.ds(pl.multiple_of((h % 2) * 256, 256), 256)
        return g[tile // 4, tile % 4, :, :, :, lanes].reshape(D, 256)

    def put_grad(h, value):
        tile = h // 2
        lanes = pl.ds(pl.multiple_of((h % 2) * 256, 256), 256)
        g[tile // 4, tile % 4, :, :, :, lanes] = value.astype(BF).reshape(4, 2, 96, 256)

    def cols(i, width=256):
        return pl.ds(pl.multiple_of(i * width, width), width)

    cot_load = pltpu.make_async_copy(cot, s["dec"], local_sem.at[0])
    cot_load.start()
    callers = announce(place)
    meta = s["meta"]
    meta[...] = jnp.zeros_like(meta)
    meta[0:4, :] = skipped[...]
    for b in range(2):
        meta[4:5, 4 * b : 4 * b + 4] = lengths[b : b + 1, :]
    lanes = s["lanes"]
    lanes[...] = jnp.zeros_like(lanes)
    lanes[0:1, 0:128] = vectors[...]
    lanes[0:6, L_QKV:L_OUT] = w_qkv[...]
    lanes[0:6, L_OUT:L_UP] = w_out[...]
    for q in range(4):
        lanes[0:6, L_DOWN + D * q : L_DOWN + D * q + D] = w_down[6 * q : 6 * q + 6, :]
    lanes[0:6, L_EMBED : L_EMBED + DE] = w_embed[...]
    s["up16"][...] = jnp.zeros_like(s["up16"])
    s["up16"][0:6, :] = w_up[...]
    lane = iota((D, 128), 1)
    row = iota((D, 128), 0)
    for n in range(6):
        col = lane + 128 * n
        device = (col * 10923) >> 16
        start = min(24 * (128 * n // 6) // 128 * 128, FF - D)
        target = 24 * device + (col - 6 * device) - start
        for q in range(4):
            part = dot(s["up16"][:, start : start + D], hot(row == target + 6 * q))
            at = L_UP + D * q + 128 * n
            lanes[:, at : at + 128] = part.astype(BF)
    row, col = iota((32, 16), 0), iota((32, 16), 1)
    for i in range(4):
        packed = jnp.zeros((32, 512), F32)
        for k in range(5):
            first = 2048 * k + 512 * i
            pick = hot((row == col + 6 * k) & (col < 6))
            packed = packed + dot(pick, lanes[:, first : first + 512])
        s["shard"][:, 512 * i : 512 * i + 512] = packed.astype(BF)
    shard = s["shard"]
    rb, meta_all = s["rb"], s["meta_all"]
    pl.semaphore_wait(pltpu.get_barrier_semaphore(), callers)
    meta_sent = []
    for t in range(1, PLANE):
        meta_sent.append(links.send(meta, meta_all.at[t], place.plane(t)))
    sent = []
    for t in range(1, PLANE):
        to = place.plane(t)
        sent.append(links.send(shard.at[:, cols(to[1], 128)], rb.at[place.fs], to))
    rb[place.fs] = shard[:, cols(place.fs, 128)]
    meta_all[0] = meta[...]
    for t in range(1, PLANE):
        source = place.plane(PLANE - t)
        links.arrive(rb.at[source[1]], sent[t - 1], source)
    arrived = rb[...].reshape(PLANE * 32, 128)
    row, col = iota((96, PLANE * 32), 0), iota((96, PLANE * 32), 1)
    sender = (row * 43) >> 8
    target = sender * 32 + (row - sender * 6)
    own_lanes = pl.ds(pl.multiple_of(place.x * 128, 128), 128)
    for k in range(5):
        block = dot(hot(col == target + 6 * k), arrived).astype(BF)
        g[k, place.y, place.z, place.c, :, own_lanes] = block

    spreads = [Spread(place, links, g, ks) for ks in GROUPS]
    first, later = spreads
    first.one()
    later.one()
    first.two()
    later.two()
    first.three()
    later.three()

    for t in range(1, PLANE):
        links.arrive(meta_all.at[t], meta_sent[t - 1], place.plane(PLANE - t))
    cot_load.wait()

    def lens_of(m, blk):
        lens = [m[4:5, blk * 4 + j : blk * 4 + j + 1].astype(F32) for j in range(4)]
        starts = [jnp.zeros_like(lens[0])]
        for j in range(3):
            starts.append(starts[j] + lens[j])
        return lens, starts

    total = jnp.zeros((1, DE), F32)
    for k in range(STRIPS):
        m = meta_all[route[0, k]]
        blk, j = k // 4, k % 4
        lens, starts = lens_of(m, blk)
        skip = jnp.concatenate([m[2 * blk : 2 * blk + 1], m[2 * blk + 1 : 2 * blk + 2]], 1)
        skip = jnp.broadcast_to(skip.astype(F32), (8, 256)).astype(BF)
        r, t = iota((256, SEG), 0).astype(F32), iota((256, SEG), 1).astype(F32)
        local = dot(skip, hot(r - starts[j] == t))
        tri = hot(iota((SEG, SEG), 0) <= iota((SEG, SEG), 1))
        through = dot(local.astype(BF), tri)[0:1]
        off = (STRIP_POS * k) % 16
        base = STRIP_POS * k - off
        lane = iota((WINDOW, SEG), 1).astype(F32)
        spot = iota((WINDOW, SEG), 0).astype(F32)
        perm = hot((spot == lane + through + float(off)) & (lane < lens[j]))
        perms[k] = perm
        picked = tdot(perm, s["dec"][base : base + WINDOW])
        s["strip"][k] = picked.astype(BF)
        total = total - col_sum(picked)

    def sum_rows(i, acc):
        part = s["dec"][pl.ds(pl.multiple_of(i * 16, 16), 16), :].astype(F32)
        return acc + part

    summed = lax.fori_loop(0, OUT_ROWS // 16, sum_rows, jnp.zeros((16, DE), F32))
    total = total + col_sum(summed) + col_sum(s["dec"][OUT_ROWS - 8 :, :].astype(F32))
    s["vgrad"][...] = jnp.zeros_like(s["vgrad"])
    s["vgrad"][V_MASK : V_MASK + 1, 0:DE] = total

    s["strip"][STRIPS] = jnp.zeros((SEG, DE), BF)
    for t in range(PLANE):
        s["slots"][t] = s["strip"][route[1, (PLANE - t) % PLANE]]
    slot_store = pltpu.make_async_copy(s["slots"], cot_from, local_sem.at[0])
    slot_store.start()
    own_store = pltpu.make_async_copy(s["slots"].at[0], cot_to.at[0], local_sem.at[1])
    own_store.start()

    slot_store.wait()
    own_store.wait()
    cot_sent, cot_copies = [], []

    def send_cot(begin, end):
        for t in range(begin, end):
            slot = cot_to.at[PLANE - t]
            cot_sent.append(links.send(cot_from.at[t], slot, place.plane(t)))
            cot_copies.append(links.started.pop())

    first.four()
    later.four()
    first.five()
    later.five()
    first.six()
    later.six()
    links.drain()
    send_cot(1, PLANE)
    links.started = cot_copies

    chunk = g[0, 0, :, :, :, 0:128].reshape(D, 128)
    table = s["acc"]

    def spread_six(i, _):
        table[0:128, cols(i)] = tdot(chunk, spread_hot(6, 256 * i))
        return 0

    def spread_four(i, _):
        table[128:256, cols(i)] = tdot(chunk, spread_hot(4, 256 * i))
        return 0

    lax.fori_loop(0, 3, spread_six, 0)
    lax.fori_loop(0, 2, spread_four, 0)
    lane6 = iota((16, D), 1)
    lane6 = lane6 - 6 * ((lane6 * 10923) >> 16)
    row6 = iota((16, D), 0)
    for v in range(12):
        low = (6 * v) // 8 * 8
        window = table[low : low + 16, :]
        s["vec"][v : v + 1] = col_sum(jnp.where(row6 + (low - 6 * v) == lane6, window, 0.0))
    lane4, row4 = iota((8, DE), 1) & 3, iota((8, DE), 0)
    few = table[128 + 72 : 128 + 80, 0:DE]
    for i, v in enumerate((V_BE, V_MASK)):
        s["vec"][v : v + 1, 0:DE] = col_sum(jnp.where(row4 - 4 * i == lane4, few, 0.0))
    vec = s["vec"]
    s["bqkv"][...] = jnp.zeros_like(s["bqkv"])
    s["bqkv"][0:1, 0:D] = vec[4:5]
    s["bqkv"][0:1, 2 * D :] = vec[5:6]
    for q in range(4):
        s["bup"][0:1, q * D : (q + 1) * D] = vec[8 + q : 9 + q]

    def norm_one(i, _):
        rows = cols(i, 128)
        hat, _f = hat_of(x_ref[rows, :].astype(F32))
        s["n1"][rows, :] = (hat * vec[0:1] + vec[1:2]).astype(BF)
        return 0

    lax.fori_loop(0, 4, norm_one, 0, unroll=2)

    def qkv_tile(t, _):
        for i in range(2):
            rows = cols(i)
            out = dot(s["n1"][rows, :], weight(H_QKV + t)) + s["bqkv"][0:1, cols(t)]
            s["qkv"][rows, cols(t)] = out.astype(BF)
        return 0

    lax.fori_loop(0, 9, qkv_tile, 0, unroll=3)

    lens_own = [lens_of(meta[...], b) for b in range(2)]

    def doc_bias(starts):
        r, c = iota((256, 256), 0).astype(F32), iota((256, 256), 1).astype(F32)
        doc_r, doc_c = jnp.zeros_like(r), jnp.zeros_like(c)
        for j in range(1, 4):
            doc_r = doc_r + jnp.where(r >= starts[j], 1.0, 0.0)
            doc_c = doc_c + jnp.where(c >= starts[j], 1.0, 0.0)
        return doc_r == doc_c

    lane = iota((256, 128), 1)
    for blk in range(2):
        rows = slice(256 * blk, 256 * blk + 256)
        same = doc_bias(lens_own[blk][1])

        def heads(hp, _):
            q2 = s["qkv"][rows, cols(hp, 128)] * jnp.asarray(0.125, BF)
            k2 = s["qkv"][rows, cols(6 + hp, 128)]
            v2 = s["qkv"][rows, cols(12 + hp, 128)]
            outs = []
            for h in range(2):
                mine = (lane >= 64) if h else (lane < 64)
                scores = dot_t(jnp.where(mine, q2, jnp.zeros_like(q2)), k2)
                scores = jnp.where(same, scores, MASKED)
                e = jnp.exp(scores - jnp.max(scores, -1, keepdims=True))
                p = (e * (1.0 / jnp.sum(e, -1, keepdims=True))).astype(BF)
                s["prob"][12 * blk + 2 * hp + h] = p
                outs.append(dot(p, v2))
            s["ctx"][rows, cols(hp, 128)] = jnp.where(lane < 64, outs[0], outs[1]).astype(BF)
            return 0

        lax.fori_loop(0, 6, heads, 0, unroll=2)

    def out_tile(t, _):
        out = dot(s["ctx"][...], weight(H_OUT + t)) + vec[6:7, cols(t)]
        s["h1"][:, cols(t)] = x_ref[:, cols(t)].astype(F32) + out
        return 0

    lax.fori_loop(0, 3, out_tile, 0, unroll=3)

    def norm_two(i, _):
        rows = cols(i, 128)
        hat, _f = hat_of(s["h1"][rows, :])
        s["n2"][rows, :] = (hat * vec[2:3] + vec[3:4]).astype(BF)
        return 0

    lax.fori_loop(0, 4, norm_two, 0, unroll=2)

    def up_tile(t, _):
        for i in range(2):
            rows = cols(i)
            u = dot(s["n2"][rows, :], weight(H_UP + t)) + s["bup"][0:1, cols(t)]
            phi = 0.5 * (1.0 + lax.erf(u * 0.7071067811865476))
            density = jnp.exp(-0.5 * u * u) * 0.3989422804014327
            s["act"][rows, cols(t)] = (u * phi).astype(BF)
            s["slope"][rows, cols(t)] = (phi + u * density).astype(BF)
        return 0

    lax.fori_loop(0, 12, up_tile, 0, unroll=2)
    for t in range(3):
        for i in range(2):
            rows = cols(i)
            out = s["h1"][rows, cols(t)] + vec[7:8, cols(t)]
            for q in range(4):
                out = out + dot(s["act"][rows, cols(q, D)], weight(H_DOWN + 3 * q + t))
            s["hb"][rows, cols(t)] = out.astype(BF)
    for t in range(2):
        out = dot(s["hb"][...], weight(H_EMBED + t)) + vec[V_BE : V_BE + 1, cols(t)]
        s["emb"][:, cols(t)] = out.astype(BF)

    def strip_hot(blk):
        lens, starts = lens_own[blk]
        picks = []
        for j in range(4):
            r, t = iota((256, SEG), 0).astype(F32), iota((256, SEG), 1).astype(F32)
            picks.append(hot((r - starts[j] == t) & (t < lens[j])))
        return jnp.concatenate(picks, 1)

    for blk in range(2):
        moved = tdot(strip_hot(blk), s["emb"][256 * blk : 256 * blk + 256])
        for j in range(4):
            s["strip"][4 * blk + j] = moved[SEG * j : SEG * j + SEG].astype(BF)
    for t in range(PLANE):
        s["slots"][t] = s["strip"][route[1, t]]
    slot_store = pltpu.make_async_copy(s["slots"], emb_from, local_sem.at[0])
    slot_store.start()
    own_store = pltpu.make_async_copy(s["slots"].at[0], emb_to.at[0], local_sem.at[1])
    own_store.start()
    slot_store.wait()
    own_store.wait()
    emb_sent = []

    def send_emb(first, last):
        for t in range(first, last):
            emb_sent.append(links.send(emb_from.at[t], emb_to.at[t], place.plane(t)))

    send_emb(1, PLANE)

    def flipped(name):
        return s["dec"][FLIPPED[name] : FLIPPED[name] + D, :]

    for name in ("n1", "n2", "ctx", "hb"):

        def flip(i, _, name=name):
            at = pl.ds(pl.multiple_of(FLIPPED[name] + 128 * i, 128), 128)
            s["dec"][at, :] = s[name][:, cols(i, 128)].T
            return 0

        lax.fori_loop(0, 6, flip, 0)

    for t in range(1, PLANE):
        links.arrive(cot_to.at[PLANE - t], cot_sent[t - 1], place.plane(PLANE - t))
    de = s["emb"]
    cot_back = pltpu.make_async_copy(cot_to, s["slots"], local_sem.at[0])
    cot_back.start()
    cot_back.wait()
    for blk in range(2):
        got = [s["slots"][route[0, 4 * blk + j]] for j in range(4)]
        moved = dot(strip_hot(blk), jnp.concatenate(got, 0))
        de[256 * blk : 256 * blk + 256] = moved.astype(BF)
    vg = s["vgrad"]
    vg[V_BE : V_BE + 1, 0:DE] = col_sum(de[...].astype(F32))
    wide = s["wide"]

    def embed_back(i, acc):
        rows = cols(i)
        dh = dot_t(de[rows, 0:256], weight(H_EMBED)) + dot_t(de[rows, 256:], weight(H_EMBED + 1))
        wide[rows, :] = dh
        s["low"][rows, :] = dh.astype(BF)
        return acc + col_sum(dh)

    vg[7:8] = lax.fori_loop(0, 2, embed_back, jnp.zeros((1, D), F32), unroll=2)
    for t in range(2):
        put_grad(H_EMBED + t, dot(flipped("hb"), de[:, cols(t)]))

    def down_part(q, _):

        def rows_part(i, acc):
            rows = cols(i)
            da = dot_t(s["low"][rows, 0:256], weight(H_DOWN + 3 * q))
            for t in range(1, 3):
                da = da + dot_t(s["low"][rows, cols(t)], weight(H_DOWN + 3 * q + t))
            du = (da * s["slope"][rows, cols(q, D)].astype(F32)).astype(BF)
            s["slope"][rows, cols(q, D)] = du
            return acc + col_sum(du.astype(F32))

        vg[pl.ds(8 + q, 1), :] = lax.fori_loop(0, 2, rows_part, jnp.zeros((1, D), F32), unroll=2)
        for i in range(6):
            at = FLIPPED["act"] + 128 * i
            s["dec"][at : at + 128, :] = s["act"][:, cols(6 * q + i, 128)].T
        for t in range(3):
            put_grad(H_DOWN + 3 * q + t, dot(flipped("act"), s["low"][:, cols(t)]))
        return 0

    lax.fori_loop(0, 4, down_part, 0)
    acc = s["acc"]

    def up_part(q, _):
        def rows_part(i, _):
            rows = cols(i)
            total = dot_t(s["slope"][rows, cols(3 * q)], weight(H_UP + 3 * q))
            for t in range(1, 3):
                total = total + dot_t(s["slope"][rows, cols(3 * q + t)], weight(H_UP + 3 * q + t))
            acc[rows, :] = jnp.where(q == 0, total, acc[rows, :] + total)
            return 0

        lax.fori_loop(0, 2, rows_part, 0, unroll=2)
        for t in range(3):
            put_grad(H_UP + 3 * q + t, dot(flipped("n2"), s["slope"][:, cols(3 * q + t)]))
        return 0

    lax.fori_loop(0, 4, up_part, 0)

    def norm_two_back(i, sums):
        rows = cols(i, 128)
        hat, factor = hat_of(s["h1"][rows, :])
        dn = acc[rows, :]
        dh = wide[rows, :] + norm_back(dn, vec[2:3], hat, factor)
        wide[rows, :] = dh
        s["low"][rows, :] = dh.astype(BF)
        return (sums[0] + col_sum(dn * hat), sums[1] + col_sum(dn), sums[2] + col_sum(dh))

    zero = jnp.zeros((1, D), F32)
    vg[2:3], vg[3:4], vg[6:7] = lax.fori_loop(0, 4, norm_two_back, (zero, zero, zero), unroll=2)

    g_first, g_mid, g_later = [Gather(place, links, g, ks, bufs) for ks in SUM_GROUPS]
    g_mid.core_first = 1
    g_later.one()

    def out_back(i, _):
        rows = cols(i)
        total = dot_t(s["low"][rows, 0:256], weight(H_OUT))
        for t in range(1, 3):
            total = total + dot_t(s["low"][rows, cols(t)], weight(H_OUT + t))
        s["hb"][rows, :] = total.astype(BF)
        return 0

    lax.fori_loop(0, 2, out_back, 0, unroll=2)
    for t in range(3):
        put_grad(H_OUT + t, dot(flipped("ctx"), s["low"][:, cols(t)]))

    for blk in range(2):
        rows = slice(256 * blk, 256 * blk + 256)

        def put(chunk, value, blk=blk):
            at = pl.ds(pl.multiple_of(512 * (chunk // 4) + 256 * blk, 256), 256)
            s["dec"][at, cols(chunk % 4, 128)] = value.astype(BF)

        def heads_back(hp, _):
            q2 = s["qkv"][rows, cols(hp, 128)]
            k2 = s["qkv"][rows, cols(6 + hp, 128)]
            v2 = s["qkv"][rows, cols(12 + hp, 128)]
            do2 = s["hb"][rows, cols(hp, 128)]
            dq, dk, dv = [], [], []
            for h in range(2):
                mine = (lane >= 64) if h else (lane < 64)
                p = s["prob"][12 * blk + 2 * hp + h]
                dp = dot_t(jnp.where(mine, do2, jnp.zeros_like(do2)), v2)
                pf = p.astype(F32)
                inner = jnp.sum(pf * dp, -1, keepdims=True)
                ds = (pf * (dp - inner)).astype(BF)
                dq.append(dot(ds, k2))
                dk.append(tdot(ds, q2))
                dv.append(tdot(p, do2))
            lo = lane < 64
            put(hp, jnp.where(lo, dq[0], dq[1]) * 0.125)
            put(6 + hp, jnp.where(lo, dk[0], dk[1]) * 0.125)
            put(12 + hp, jnp.where(lo, dv[0], dv[1]))
            return 0

        lax.fori_loop(0, 6, heads_back, 0, unroll=2)
        if blk == 0:
            g_later.two()
            sibling = place.sibling()
            pl.semaphore_signal(core_free, inc=1, device_id=sibling, device_id_type=MESH)
        else:
            g_later.three()

    def dqkv(t, start=0, size=ROWS):
        rows = pl.ds(pl.multiple_of(512 * (t // 2) + start, 64), size)
        return s["dec"][rows, cols(t % 2)]

    def bias_sums(i, sums):
        q = [dqkv(t, 64 * i, 64).astype(F32) for t in (0, 1, 2)]
        v = [dqkv(t, 64 * i, 64).astype(F32) for t in (6, 7, 8)]
        q, v = [jnp.concatenate(part, 1) for part in (q, v)]
        return (sums[0] + col_sum(q), sums[1] + col_sum(v))

    vg[4:5], vg[5:6] = lax.fori_loop(0, 8, bias_sums, (zero, zero), unroll=2)

    def qkv_part(q, _):
        def rows_part(i, _):
            rows = cols(i)
            total = dot_t(dqkv(3 * q, 256 * i, 256), weight(H_QKV + 3 * q))
            for t in range(1, 3):
                total = total + dot_t(dqkv(3 * q + t, 256 * i, 256), weight(H_QKV + 3 * q + t))
            acc[rows, :] = jnp.where(q == 2, total, acc[rows, :] + total)
            return 0

        lax.fori_loop(0, 2, rows_part, 0, unroll=2)
        for t in range(3):
            put_grad(H_QKV + 3 * q + t, dot(flipped("n1"), dqkv(3 * q + t)))
        return 0

    qkv_part(2, 0)
    pl.semaphore_wait(core_free, 1)
    g_mid.one()
    lax.fori_loop(0, 2, qkv_part, 0)
    g_mid.two()

    def norm_one_back(i, sums):
        rows = cols(i, 128)
        hat, factor = hat_of(x_ref[rows, :].astype(F32))
        dn = acc[rows, :]
        wide[rows, :] = wide[rows, :] + norm_back(dn, vec[0:1], hat, factor)
        return (sums[0] + col_sum(dn * hat), sums[1] + col_sum(dn))

    vg[0:1], vg[1:2] = lax.fori_loop(0, 4, norm_one_back, (zero, zero), unroll=2)
    patch_store = pltpu.make_async_copy(wide, patch_out, local_sem.at[1])
    patch_store.start()

    table[0:256, :] = jnp.zeros((256, D), F32)
    lane6 = iota((8, D), 1)
    lane6 = lane6 - 6 * ((lane6 * 10923) >> 16)
    row6 = iota((8, D), 0)
    for a in range(9):
        rows = jnp.zeros((8, D), F32)
        for v in range(12):
            if 6 * v < 8 * a + 8 and 6 * v + 6 > 8 * a:
                rows = jnp.where(row6 + (8 * a - 6 * v) == lane6, vg[v : v + 1], rows)
        table[8 * a : 8 * a + 8, :] = rows
    rows = jnp.zeros((8, DE), F32)
    for i, v in enumerate((V_BE, V_MASK)):
        rows = jnp.where(row4 - 4 * i == lane4, vg[v : v + 1, 0:DE], rows)
    table[128 + 72 : 128 + 80, 0:DE] = rows

    def fold_six(i, total):
        return total + dot_t(spread_hot(6, 256 * i), table[0:128, cols(i)].astype(BF))

    def fold_four(i, total):
        return total + dot_t(spread_hot(4, 256 * i), table[128:256, cols(i)].astype(BF))

    chunk = lax.fori_loop(0, 3, fold_six, jnp.zeros((D, 128), F32))
    chunk = lax.fori_loop(0, 2, fold_four, chunk)
    g[0, 0, :, :, :, 0:128] = chunk.astype(BF).reshape(4, 2, 96, 128)

    g_first.one()
    vec_out[...] = vec[V_MASK : V_MASK + 1, :]
    g_later.four()
    g_first.two()
    g_mid.three()
    g_later.five()
    g_first.three()
    g_mid.four()
    g_later.six()
    g_first.four()
    g_mid.five()
    g_first.five()
    g_mid.six()
    g_first.six()
    row, col = iota((PLANE * 32, 96), 0), iota((PLANE * 32, 96), 1)
    inner_row = row & 31
    base_row = 6 * (row >> 5)
    slots = jnp.zeros((PLANE * 32, 128), F32)
    for k in range(5):
        j = inner_row - 6 * k
        pick = hot((col == base_row + j) & (j >= 0) & (j < 6))
        slots = slots + dot(pick, g[k, place.y, place.z, place.c, :, own_lanes])
    s["fin_send"][...] = slots.astype(BF).reshape(PLANE, 32, 128)
    fin_sent = []
    for t in range(1, PLANE):
        to = place.plane(t)
        slot = s["fin_recv"].at[:, cols(place.fs, 128)]
        fin_sent.append(links.send(s["fin_send"].at[to[1]], slot, to))
    s["fin_recv"][:, cols(place.fs, 128)] = s["fin_send"][place.fs]
    for t in range(1, PLANE):
        source = place.plane(PLANE - t)
        links.arrive(s["fin_recv"].at[:, cols(source[1], 128)], fin_sent[t - 1], source)
    fin[...] = s["fin_recv"][...]
    for t in range(1, PLANE):
        links.arrive(emb_to.at[t], emb_sent[t - 1], place.plane(PLANE - t))
    links.drain()
    patch_store.wait()


def mega(w_qkv, w_out, w_up, w_down, w_embed, vectors, skipped, lengths, route, x, cot):
    dma = pltpu.SemaphoreType.DMA
    vmem = pl.BlockSpec(memory_space=pltpu.VMEM)
    smem = pl.BlockSpec(memory_space=pltpu.SMEM)
    hbm = pl.BlockSpec(memory_space=pl.ANY)
    return pl.pallas_call(
        kernel,
        out_shape=(
            jax.ShapeDtypeStruct((ROWS, D), F32),
            jax.ShapeDtypeStruct((32, 2048), BF),
            jax.ShapeDtypeStruct((STRIPS, WINDOW, SEG), BF),
            jax.ShapeDtypeStruct((1, D), F32),
        )
        + (jax.ShapeDtypeStruct((PLANE, SEG, DE), BF),) * 4,
        in_specs=[vmem] * 8 + [smem, vmem, hbm],
        out_specs=(hbm, vmem, vmem, vmem) + (hbm,) * 4,
        scratch_shapes=[pltpu.VMEM(shape, kind) for shape, kind in SCRATCH.values()]
        + [pltpu.VMEM(shape, BF) for shape in reduce_bufs()]
        + [dma((N_SEM,)), dma((N_SEM,)), dma((2,))]
        + [pltpu.SemaphoreType.REGULAR],
        compiler_params=pltpu.CompilerParams(
            collective_id=1, has_side_effects=True, vmem_limit_bytes=64 * 1024 * 1024
        ),
        name="layer",
    )(w_qkv, w_out, w_up, w_down, w_embed, vectors, skipped, lengths, route, x, cot)


VECTOR_AT = (0, 6, 12, 18, 24, 30, 36, 48, 42, 72, 76)
VECTOR_SIZE = (6, 6, 6, 6, 6, 6, 6, 24, 6, 4, 4)


def finish_kernel(route, patch, fin, perms, mask, emb, dec_out, patch_out, g_qkv, g_out, g_up,
                  g_down, g_embed, *rest):
    vectors, (dec, wide, strips, rows, sems) = rest[:11], rest[11:]
    loads = []
    for k in range(STRIPS):
        source = emb.at[route[0, k]]
        loads.append(pltpu.make_async_copy(source, strips.at[k], sems.at[2 + k]))
        loads[-1].start()
    patch_load = pltpu.make_async_copy(patch, rows, sems.at[0])
    patch_load.start()
    token = mask[0:1, 0:DE]
    blank = jnp.broadcast_to(token.astype(BF), (64, DE))

    def fill(i, _):
        dec[pl.ds(pl.multiple_of(i * 64, 64), 64), :] = blank
        return 0

    lax.fori_loop(0, OUT_ROWS // 64, fill, 0, unroll=6)
    dec[OUT_ROWS - 8 :, :] = blank[0:8]
    for k in range(STRIPS):
        perm = perms[k]
        base = STRIP_POS * k - (STRIP_POS * k) % 16
        loads[k].wait()
        both = dot(perm, jnp.concatenate([strips[k], jnp.ones((SEG, 128), BF)], 1))
        placed, filled = both[:, 0:DE], both[:, DE : DE + 1]
        dec[base : base + WINDOW] = jnp.where(filled > 0.5, placed, token).astype(BF)
    dec_store = pltpu.make_async_copy(dec, dec_out, sems.at[1])
    dec_store.start()
    patch_load.wait()
    patch_store = pltpu.make_async_copy(rows, patch_out, sems.at[0])
    patch_store.start()
    row, col = iota((8, 32), 0), iota((8, 32), 1)
    for k in range(5):
        pick = hot((col == row + 6 * k) & (row < 6))
        wide[:, 2048 * k : 2048 * k + 2048] = dot(pick, fin[...])
    g_qkv[...] = wide[0:6, L_QKV:L_OUT]
    g_out[...] = wide[0:6, L_OUT:L_UP]
    for q in range(4):
        g_down[6 * q : 6 * q + 6, :] = wide[0:6, L_DOWN + D * q : L_DOWN + D * q + D]
    g_embed[...] = wide[0:6, L_EMBED : L_EMBED + DE]
    col = iota((256, 384), 1)
    device = (col * 2731) >> 16
    inner = col - 24 * device
    part = (inner * 43) >> 8
    source = 6 * device + (inner - 6 * part)
    row = iota((256, 384), 0)
    for shift in range(4):
        pick = [hot((part == q) & (row == source + (96 * shift) % 128)) for q in range(4)]
        for m in (shift, shift + 4):
            start = L_UP + (96 * m) // 128 * 128
            total = jnp.zeros((8, 384), F32)
            for q in range(4):
                window = wide[:, start + D * q : start + D * q + 256].astype(BF)
                total = total + dot(window, pick[q])
            g_up[:, 384 * m : 384 * m + 384] = total[0:6]
    for ref, at, size in zip(vectors, VECTOR_AT, VECTOR_SIZE):
        ref[...] = wide[0, at : at + size]
    patch_store.wait()
    dec_store.wait()


def finish(route, patch, fin, perms, mask, emb):
    vmem = pl.BlockSpec(memory_space=pltpu.VMEM)
    hbm = pl.BlockSpec(memory_space=pl.ANY)
    shape = jax.ShapeDtypeStruct
    return pl.pallas_call(
        finish_kernel,
        out_shape=(shape((OUT_ROWS, DE), BF), shape((ROWS, D), F32))
        + tuple(shape(s, F32) for s in ((6, 3 * D), (6, D), (6, FF), (24, D), (6, DE)))
        + tuple(shape((n,), F32) for n in VECTOR_SIZE),
        in_specs=[pl.BlockSpec(memory_space=pltpu.SMEM), hbm, vmem, vmem, vmem, hbm],
        out_specs=(hbm, hbm) + (vmem,) * 16,
        scratch_shapes=[
            pltpu.VMEM((OUT_ROWS, DE), BF),
            pltpu.VMEM((8, 10240), F32),
            pltpu.VMEM((STRIPS, SEG, DE), BF),
            pltpu.VMEM((ROWS, D), F32),
            pltpu.SemaphoreType.DMA((2 + STRIPS,)),
        ],
        compiler_params=pltpu.CompilerParams(vmem_limit_bytes=64 * 1024 * 1024),
        name="finish",
    )(route, patch, fin, perms, mask, emb)


def on_device(patches, lengths, skipped, strip_order, decoder_grad, qkv_weight, out_weight,
              up_weight, down_weight, embed_weight, gain_one, shift_one, gain_two, shift_two,
              bias_query, bias_value, bias_out, bias_up, bias_down, bias_embed, mask_token):
    pieces = (gain_one, shift_one, gain_two, shift_two, bias_query, bias_value, bias_out,
              bias_down, bias_up, bias_embed, mask_token)
    vectors, at = None, 0
    for piece in pieces:
        size = piece.shape[0]
        padded = jnp.pad(piece, (at, 128 - at - size))
        vectors = padded if vectors is None else vectors + padded
        at += size
    strip = lax.broadcasted_iota(I32, (PLANE, STRIPS), 1)
    place = lax.broadcasted_iota(I32, (PLANE, STRIPS), 0)
    match = (strip_order[0, None, 0:STRIPS] == place).astype(I32)
    inverse = STRIPS + jnp.sum(match * (strip - STRIPS), 1)
    route = jnp.stack([strip_order[0], inverse])
    patch_grad, fin, perms, mask, _, _, _, emb = mega(
        qkv_weight, out_weight, up_weight, down_weight, embed_weight, vectors[None],
        skipped.reshape(4, 128), lengths, route, patches, decoder_grad,
    )
    return tuple(finish(route, patch_grad, fin, perms, mask, emb))


def solution(mesh):
    both = ("dp", "fsdp")
    rows, vector = P(both, None), P(both)
    return jax.shard_map(
        on_device,
        mesh=mesh,
        in_specs=(rows, rows, rows, P("dp", None), rows) + (rows,) * 5 + (vector,) * 11,
        out_specs=(rows,) * 7 + (vector,) * 11,
        check_vma=False,
    )
```
